32 devices in a mesh: groups: 2 (over x), ctx: 8 (over z, y), head: 2 (over core).
Axes of the slice: x: 2, y: 2, z: 4, core: 2. Of those that a mesh axis runs over, the one named last changes fastest.
Arguments:
- queries: bfloat16 [2048, 12288], P(('groups', 'ctx'), 'head'), parts along dimension 0, may hold values from -32 to 32
- span_latents: bfloat16 [2048, 576], P(('groups', 'ctx')), parts along dimension 0, may hold values from -600 to 600
- cache_latents: bfloat16 [256, 576], P(('groups', 'ctx')), parts along dimension 0, may hold values from -32 to 32
- latent_gain: float32 [512], replicated, may hold values from 0.1 to 1.9
- key_weight: bfloat16 [512, 8192], P(None, 'head'), may hold values from -0.25 to 0.25
- value_weight: bfloat16 [512, 8192], P(None, 'head'), may hold values from -0.25 to 0.25
- prefix_length: int32 [2], P('groups'), parts along dimension 0, may hold values from 64 to 128
- block_order: int32 [16], P('groups'), parts along dimension 0, may hold values from 0 to 7, each once
Outputs:
- attended: bfloat16 [2048, 8192], P(('groups', 'ctx'), 'head'), parts along dimension 0
The draws below stay inside these ranges and needn't reach their ends.
There are 2 independent parts, one for each index of `groups`. The reference program is written for one: setup_inputs(seed, part) draws one part's arguments, and reference() takes and returns one part's arrays. A program takes and returns all parts, laid end to end along the dimension named above; an argument that names none is the same for every part. Nothing has to cross between parts.
Inputs may be any that keep to these rules, and one draw needn't show every extreme that they name: Cache slots 0 to prefix_length[0] - 1 hold the prefix. A permutation; shard c of ctx holds span positions block_order[c] * 128 to block_order[c] * 128 + 127.
All inputs are finite; a program needn't handle non-finite values.
Results may differ from the reference program's by a relative error of at most 0.0076.
Values may be sent and summed in bfloat16 or wider, within the bound.
No kernel may reach another device: no remote copies, remote signals or barrier semaphores. Data moves between devices by JAX's collectives and lax.ppermute only.
A program may use at most 64 MiB of HBM per device.

```python
import math
import jax
import jax.numpy as jnp
from jax import lax

HEADS = 64
LATENT = 512
ROPE = 64
NOPE = 128
VDIM = 128
TOK_DEV = 128
TOKENS = 1024
CACHE = 128
N_CTX = 8


def draw_queries(key, part):
    key = jax.random.fold_in(key, 3)
    entries = jnp.clip(jax.random.normal(key, (TOKENS, HEADS, NOPE + ROPE), jnp.float32) * 2.5, -12.0, 12.0)
    return entries.reshape(TOKENS, HEADS * (NOPE + ROPE)).astype(jnp.bfloat16)


def draw_cache_latents(key, part):
    key = jax.random.fold_in(key, 5)
    entries = jnp.clip(jax.random.normal(key, (CACHE, LATENT + ROPE), jnp.float32), -6.0, 6.0)
    return entries.astype(jnp.bfloat16)


def draw_span_latents(key, part):
    key = jax.random.fold_in(key, 7)
    subkeys = jax.random.split(key, 3)
    row_scale = jnp.exp(jax.random.uniform(subkeys[0], (TOKENS, 1), jnp.float32, 0.0, math.log(10.0)))
    column_scale = jnp.exp(jax.random.uniform(subkeys[1], (1, LATENT), jnp.float32, 0.0, math.log(10.0)))
    entries = jnp.clip(jax.random.normal(subkeys[2], (TOKENS, LATENT + ROPE), jnp.float32), -6.0, 6.0)
    latent = entries[:, :LATENT] * row_scale * column_scale
    return jnp.concatenate([latent, entries[:, LATENT:]], axis=1).astype(jnp.bfloat16)


def block_scale(rng, dims, cuts, low, largest):
    level = 1.0
    for position, shards_of in cuts:
        draws = jax.random.uniform(jax.random.fold_in(jax.random.fold_in(rng, 6), position), (shards_of,), jnp.float32, low / len(cuts), largest / len(cuts))
        level = level * jnp.repeat(jnp.exp(draws), dims[position] // shards_of).reshape((-1,) + (1,) * (len(dims) - 1 - position))
    return level


def scatter_about(key, dims, spread, most, cuts=(), kind=jnp.bfloat16):
    gain = block_scale(key, dims, cuts, -0.22, 0.18) if cuts else 1.0
    drawn = jax.random.normal(key, dims, jnp.float32) * spread * gain
    return jnp.minimum(jnp.maximum(drawn, -most), most).astype(kind)


def setup_inputs(seed: int = 0, part: int = 0) -> dict:
    splits = jax.random.split(jax.random.key(seed), 9)
    own_keys = jax.random.split(jax.random.fold_in(splits[8], part), 9)
    return {
        "queries": draw_queries(jax.random.fold_in(jax.random.fold_in(splits[8], part), 71), part),
        "span_latents": draw_span_latents(jax.random.fold_in(jax.random.fold_in(splits[8], part), 71), part),
        "cache_latents": draw_cache_latents(jax.random.fold_in(jax.random.fold_in(splits[8], part), 71), part),
        "latent_gain": jnp.clip(1.0 + 0.18 * jax.random.normal(splits[3], (LATENT,), jnp.float32), 0.1, 1.9),
        "key_weight": scatter_about(splits[4], (LATENT, HEADS * NOPE), LATENT ** -0.5, 0.25, ((1, 2),)),
        "value_weight": scatter_about(splits[5], (LATENT, HEADS * VDIM), LATENT ** -0.5, 0.25, ((1, 2),)),
        "prefix_length": jax.random.randint(own_keys[6], (1,), CACHE // 2, CACHE + 1).astype(jnp.int32),
        "block_order": jax.random.permutation(own_keys[7], N_CTX).astype(jnp.int32),
    }


def span_rows(span_latents, latent_gain):
    raw_rows = span_latents.astype(jnp.float32)
    latent = raw_rows[:, :LATENT]
    mean_square = lax.optimization_barrier(jnp.mean(latent * latent, axis=1, keepdims=True))
    normed = latent * lax.rsqrt(mean_square + 1e-06) * latent_gain.astype(jnp.float32)[None, :]
    return jnp.concatenate([normed, raw_rows[:, LATENT:]], axis=1).astype(jnp.bfloat16)

def reference(queries, span_latents, cache_latents, latent_gain, key_weight, value_weight, prefix_length, block_order):
    key_rows = jnp.concatenate([cache_latents, span_rows(span_latents, latent_gain)], axis=0)
    token_index = jnp.arange(TOKENS, dtype=jnp.int32)
    query_pos = (block_order[token_index // TOK_DEV] * TOK_DEV + token_index % TOK_DEV).astype(jnp.int32)
    slot_index = jnp.arange(CACHE, dtype=jnp.int32)
    cache_pos = jnp.where(slot_index < prefix_length[0], -1, TOKENS).astype(jnp.int32)
    key_pos = jnp.concatenate([cache_pos, query_pos])
    visible = key_pos[None, :] <= query_pos[:, None]
    latent = key_rows[:, :LATENT]
    rotary = key_rows[:, LATENT:]
    qk_width = NOPE + ROPE
    score_scale = 1.0 / math.sqrt(qk_width)

    def one_head(head_number):
        w_key = lax.dynamic_slice_in_dim(key_weight, head_number * NOPE, NOPE, 1)
        w_value = lax.dynamic_slice_in_dim(value_weight, head_number * VDIM, VDIM, 1)
        key_nope = jnp.dot(latent, w_key, preferred_element_type=jnp.float32).astype(jnp.bfloat16)
        values = jnp.dot(latent, w_value, preferred_element_type=jnp.float32).astype(jnp.bfloat16)
        key_full = jnp.concatenate([key_nope, rotary], axis=1)
        query_head = lax.dynamic_slice_in_dim(queries, head_number * qk_width, qk_width, 1)
        scores = lax.dot_general(query_head, key_full, (((1,), (1,)), ((), ())), preferred_element_type=jnp.float32) * score_scale
        scores = jnp.where(visible, scores, -1e+30)
        row_max = lax.optimization_barrier(jnp.max(scores, axis=1, keepdims=True))
        exponent = jnp.exp(scores - row_max)
        weight_sum = lax.optimization_barrier(jnp.sum(exponent, axis=1, keepdims=True))
        weights = exponent.astype(jnp.bfloat16)
        head_mixed = jnp.dot(weights, values, preferred_element_type=jnp.float32) / weight_sum
        return head_mixed.astype(jnp.bfloat16)
    per_head = lax.map(one_head, jnp.arange(HEADS, dtype=jnp.int32))
    return jnp.transpose(per_head, (1, 0, 2)).reshape(TOKENS, HEADS * VDIM)
```

```python
import functools
import math

import jax
import jax.numpy as jnp
from jax import lax
from jax.experimental import pallas as pl
from jax.experimental.pallas import tpu as pltpu
from jax.sharding import PartitionSpec as P

LATENT = 512
ROPE = 64
NOPE = 128
VDIM = 128
PACKED = 640
QK = 256
NEG = -1e30
AXES = ("ctx", "head")
BF = jnp.bfloat16
F32 = jnp.float32


def vmem_spec():
    return pl.BlockSpec(memory_space=pltpu.VMEM)


def smem_spec():
    return pl.BlockSpec(memory_space=pltpu.SMEM)


def any_spec():
    return pl.BlockSpec(memory_space=pl.ANY)


def pack_kernel(shard_count, order_ref, prefix_ref, span_ref, cache_ref, gain_ref, out_ref):
    tok_rows = span_ref.shape[0]
    cache_rows = cache_ref.shape[0]
    me = lax.axis_index("ctx")
    latent = span_ref[:, :LATENT].astype(F32)
    mean_square = jnp.mean(latent * latent, axis=1, keepdims=True)
    normed = latent * lax.rsqrt(mean_square + 1e-06) * gain_ref[...]
    out_ref[:tok_rows, :LATENT] = normed.astype(BF)
    out_ref[tok_rows:, :LATENT] = cache_ref[:, :LATENT]
    lanes = lax.broadcasted_iota(jnp.int32, (tok_rows, 128), 1)
    out_ref[:tok_rows, LATENT:] = jnp.where(lanes == ROPE + order_ref[me], 1.0, 0.0).astype(BF)
    out_ref[:tok_rows, LATENT : LATENT + ROPE] = span_ref[:, LATENT:]
    lanes = lax.broadcasted_iota(jnp.int32, (cache_rows, 128), 1)
    slots = me * cache_rows + lax.broadcasted_iota(jnp.int32, (cache_rows, 128), 0)
    hidden = jnp.logical_and(lanes == ROPE + shard_count, slots >= prefix_ref[0])
    out_ref[tok_rows:, LATENT:] = jnp.where(hidden, 1.0, 0.0).astype(BF)
    out_ref[tok_rows:, LATENT : LATENT + ROPE] = cache_ref[:, LATENT:]


def pack(span_latents, cache_latents, gain, prefix_length, block_order):
    rows = span_latents.shape[0] + cache_latents.shape[0]
    return pl.pallas_call(
        functools.partial(pack_kernel, block_order.shape[0]),
        out_shape=jax.ShapeDtypeStruct((rows, PACKED), BF),
        in_specs=[smem_spec(), smem_spec(), vmem_spec(), vmem_spec(), vmem_spec()],
        out_specs=vmem_spec(),
        name="pack_rows",
    )(block_order, prefix_length, span_latents, cache_latents, gain.reshape(1, LATENT))


def query_kernel(order_ref, q_ref, out_ref):
    me = lax.axis_index("ctx")
    rows = q_ref.shape[0]
    lanes = lax.broadcasted_iota(jnp.int32, (rows, 128), 1)
    low = lanes < ROPE
    hide = jnp.where(lanes - ROPE > order_ref[me], NEG, 0.0)
    for pair in range(q_ref.shape[1] // 384):
        base = pair * 384
        second = q_ref[:, base + 128 : base + 256].astype(F32)
        third = q_ref[:, base + 256 : base + 384].astype(F32)
        second_turned = pltpu.roll(second, 64, 1)
        third_turned = pltpu.roll(third, 64, 1)
        to = pair * 2 * QK
        out_ref[:, to : to + 128] = q_ref[:, base : base + 128]
        out_ref[:, to + 128 : to + 256] = jnp.where(low, second, hide).astype(BF)
        out_ref[:, to + 256 : to + 384] = jnp.where(low, second_turned, third_turned).astype(BF)
        out_ref[:, to + 384 : to + 512] = jnp.where(low, third_turned, hide).astype(BF)


def arrange_queries(queries, block_order):
    rows, width = queries.shape
    heads = width // (NOPE + ROPE)
    return pl.pallas_call(
        query_kernel,
        out_shape=jax.ShapeDtypeStruct((rows, heads * QK), BF),
        grid=(4,),
        in_specs=[smem_spec(), pl.BlockSpec((rows, width // 4), lambda i: (0, i))],
        out_specs=pl.BlockSpec((rows, heads * QK // 4), lambda i: (0, i)),
        cost_estimate=pl.CostEstimate(flops=rows * width * 4, bytes_accessed=rows * width * 4, transcendentals=0),
        name="arrange_queries",
    )(block_order, queries)


def attend_kernel(pairs, own_rows, tok_rows, heads, q_ref, wk_ref, wv_ref, *rest):
    sources = rest[: 1 + sum(len(p) for p in pairs)]
    out_ref, rows_ref, keys_ref, sems = rest[1 + sum(len(p) for p in pairs) :]
    core = lax.axis_index("head")

    def target(slot):
        return rows_ref.at[pl.ds(slot * own_rows, own_rows), :]

    @pl.when(pl.program_id(0) == 0)
    def _():
        at = 0
        slot = 0
        for group in [(0,)] + list(pairs):
            if len(group) == 1:
                pltpu.make_async_copy(sources[at], target(slot), sems.at[slot]).start()
            else:
                for which in range(2):

                    @pl.when(core == which)
                    def _():
                        pltpu.make_async_copy(sources[at + which], target(slot), sems.at[slot]).start()

            at += len(group)
            slot += 1
        for index in range(slot):
            pltpu.make_async_copy(sources[0], target(index), sems.at[index]).wait()
        for head in range(heads):
            keys_ref[head, :, NOPE:] = rows_ref[:, LATENT:]

    scale = math.log2(math.e) / math.sqrt(NOPE + ROPE)
    latent = rows_ref[:, :LATENT]
    row_ids = lax.broadcasted_iota(jnp.int32, (tok_rows, tok_rows), 0)
    col_ids = lax.broadcasted_iota(jnp.int32, (tok_rows, tok_rows), 1)
    causal = jnp.where(col_ids <= row_ids, 0.0, NEG)
    for pair in range(heads // 2):
        keys = jnp.dot(latent, wk_ref[:, pair * 256 : pair * 256 + 256], preferred_element_type=F32).astype(BF)
        keys_ref[2 * pair, :, :NOPE] = keys[:, :NOPE]
        keys_ref[2 * pair + 1, :, :NOPE] = keys[:, NOPE:]
    for head in range(heads):
        scores = lax.dot_general(
            q_ref[:, head * QK : head * QK + QK],
            keys_ref[head],
            (((1,), (1,)), ((), ())),
            preferred_element_type=F32,
        )
        scores = jnp.concatenate([scores[:, :tok_rows] + causal, scores[:, tok_rows:]], axis=1)
        row_max = jnp.max(scores, axis=1, keepdims=True)
        exponent = jnp.exp2((scores - row_max) * scale)
        weight_sum = jnp.sum(exponent, axis=1, keepdims=True)
        mixed = jnp.dot(exponent.astype(BF), latent, preferred_element_type=F32).astype(BF)
        wv = wv_ref[:, head * VDIM : head * VDIM + VDIM]
        out = jnp.dot(mixed, wv, preferred_element_type=F32) / weight_sum
        out_ref[:, head * VDIM : head * VDIM + VDIM] = out.astype(BF)


def attend(arranged, key_weight, value_weight, own, pairs):
    tok_rows = arranged.shape[0]
    own_rows = own.shape[0]
    all_heads = key_weight.shape[1] // NOPE
    slots = 1 + len(pairs)
    heads = 4 if slots * own_rows <= 2048 else 2
    flat = [own] + [entry for group in pairs for entry in group]
    keys = slots * own_rows
    return pl.pallas_call(
        functools.partial(attend_kernel, pairs, own_rows, tok_rows, heads),
        out_shape=jax.ShapeDtypeStruct((tok_rows, all_heads * VDIM), BF),
        grid=(all_heads // heads,),
        in_specs=[
            pl.BlockSpec((tok_rows, heads * QK), lambda i: (0, i)),
            pl.BlockSpec((LATENT, heads * NOPE), lambda i: (0, i)),
            pl.BlockSpec((LATENT, heads * VDIM), lambda i: (0, i)),
        ]
        + [any_spec()] * len(flat),
        out_specs=pl.BlockSpec((tok_rows, heads * VDIM), lambda i: (0, i)),
        scratch_shapes=[
            pltpu.VMEM((keys, PACKED), BF),
            pltpu.VMEM((heads, keys, QK), BF),
            pltpu.SemaphoreType.DMA((slots,)),
        ],
        compiler_params=pltpu.CompilerParams(vmem_limit_bytes=56 * 1024 * 1024),
        cost_estimate=pl.CostEstimate(
            flops=2 * keys * all_heads * (LATENT * NOPE + tok_rows * (QK + LATENT)),
            bytes_accessed=LATENT * all_heads * 512,
            transcendentals=keys * tok_rows * all_heads,
        ),
        name="attend",
    )(arranged, key_weight, value_weight, *flat)


def exchange(own, shard_count):
    line = shard_count // 2

    def dev(place, side, core):
        return ((place % line) * 2 + side) * 2 + core

    def move(value, route):
        return lax.ppermute(
            value, AXES, [route(place, side) for place in range(line) for side in range(2)]
        )

    both = [
        (dev(place, side, core), dev(place, 1 - side, core))
        for place in range(line)
        for side in range(2)
        for core in range(2)
    ]
    steps = range(1, line)
    along = [move(own, lambda p, s, k=k: (dev(p, s, 0), dev(p + k, s, 0))) for k in steps]
    across = lax.ppermute(own, AXES, both)
    crossed = [move(a, lambda p, s: (dev(p, s, 0), dev(p, 1 - s, 1))) for a in along]
    shared = [move(a, lambda p, s: (dev(p, s, 0), dev(p, s, 1))) for a in along]
    back = [move(c, lambda p, s: (dev(p, s, 1), dev(p, s, 0))) for c in crossed]
    pairs = [(across,)]
    pairs += [(a, w) for a, w in zip(along, shared)]
    pairs += [(b, c) for b, c in zip(back, crossed)]
    return pairs


def per_device(
    queries,
    span_latents,
    cache_latents,
    latent_gain,
    key_weight,
    value_weight,
    prefix_length,
    block_order,
):
    shard_count = lax.axis_size("ctx")
    own = pack(span_latents, cache_latents, latent_gain, prefix_length, block_order)
    pairs = exchange(own, shard_count)
    arranged = arrange_queries(queries, block_order)
    return attend(arranged, key_weight, value_weight, own, pairs)


def solution(mesh):
    return jax.shard_map(
        per_device,
        mesh=mesh,
        in_specs=(
            P(("groups", "ctx"), "head"),
            P(("groups", "ctx"), None),
            P(("groups", "ctx"), None),
            P(),
            P(None, "head"),
            P(None, "head"),
            P("groups"),
            P("groups"),
        ),
        out_specs=P(("groups", "ctx"), "head"),
        check_vma=False,
    )
```

```python
import functools
import math

import jax
import jax.numpy as jnp
from jax import lax
from jax.experimental import pallas as pl
from jax.experimental.pallas import tpu as pltpu
from jax.sharding import PartitionSpec as P

LATENT = 512
ROPE = 64
NOPE = 128
VDIM = 128
PACKED = 640
QK = 256
NEG = -1e30
AXES = ("ctx", "head")
BF = jnp.bfloat16
F32 = jnp.float32


def vmem_spec():
    return pl.BlockSpec(memory_space=pltpu.VMEM)


def smem_spec():
    return pl.BlockSpec(memory_space=pltpu.SMEM)


def any_spec():
    return pl.BlockSpec(memory_space=pl.ANY)


def pack_kernel(shard_count, order_ref, prefix_ref, span_ref, cache_ref, gain_ref, out_ref):
    tok_rows = span_ref.shape[1]
    cache_rows = cache_ref.shape[0]
    me = lax.axis_index("ctx")
    latent = span_ref[:LATENT, :].astype(F32)
    mean_square = jnp.mean(latent * latent, axis=0, keepdims=True)
    normed = (latent * lax.rsqrt(mean_square + 1e-06)).T * gain_ref[...]
    out_ref[:tok_rows, :LATENT] = normed.astype(BF)
    rest = lax.broadcasted_iota(jnp.int32, (ROPE, tok_rows), 0)
    rest = jnp.where(rest == order_ref[me], 1.0, 0.0)
    tail = jnp.concatenate([span_ref[LATENT:, :].astype(F32), rest], axis=0)
    out_ref[:tok_rows, LATENT:] = tail.T.astype(BF)
    out_ref[tok_rows:, :LATENT] = cache_ref[:, :LATENT]
    lanes = lax.broadcasted_iota(jnp.int32, (cache_rows, 128), 1)
    slots = me * cache_rows + lax.broadcasted_iota(jnp.int32, (cache_rows, 128), 0)
    hidden = jnp.logical_and(lanes == ROPE + shard_count, slots >= prefix_ref[0])
    out_ref[tok_rows:, LATENT:] = jnp.where(hidden, 1.0, 0.0).astype(BF)
    out_ref[tok_rows:, LATENT : LATENT + ROPE] = cache_ref[:, LATENT:]


def pack(span_latents, cache_latents, gain, prefix_length, block_order):
    rows = span_latents.shape[0] + cache_latents.shape[0]
    return pl.pallas_call(
        functools.partial(pack_kernel, block_order.shape[0]),
        out_shape=jax.ShapeDtypeStruct((rows, PACKED), BF),
        in_specs=[smem_spec(), smem_spec(), vmem_spec(), vmem_spec(), vmem_spec()],
        out_specs=vmem_spec(),
        name="pack_rows",
    )(block_order, prefix_length, span_latents.T, cache_latents, gain.reshape(1, LATENT))


def prepare_kernel(order_ref, q_ref, wv_ref, qt_ref, wvt_ref):
    me = lax.axis_index("ctx")
    rows = q_ref.shape[0]
    places = lax.broadcasted_iota(jnp.int32, (ROPE, rows), 0)
    hide = jnp.where(places > order_ref[me], NEG, 0.0).astype(BF)
    for pair in range(q_ref.shape[1] // 384):
        base = pair * 384
        to = pair * 2 * QK
        turned = q_ref[:, base : base + 384].T
        qt_ref[to : to + 192, :] = turned[:192]
        qt_ref[to + 192 : to + 256, :] = hide
        qt_ref[to + 256 : to + 448, :] = turned[192:]
        qt_ref[to + 448 : to + 512, :] = hide
    wvt_ref[...] = wv_ref[...].T


def prepare(queries, value_weight, block_order):
    rows, width = queries.shape
    heads = width // (NOPE + ROPE)
    steps = 8
    return pl.pallas_call(
        prepare_kernel,
        out_shape=(
            jax.ShapeDtypeStruct((heads * QK, rows), BF),
            jax.ShapeDtypeStruct((heads * VDIM, LATENT), BF),
        ),
        grid=(steps,),
        in_specs=[
            smem_spec(),
            pl.BlockSpec((rows, width // steps), lambda i: (0, i)),
            pl.BlockSpec((LATENT, heads * VDIM // steps), lambda i: (0, i)),
        ],
        out_specs=(
            pl.BlockSpec((heads * QK // steps, rows), lambda i: (i, 0)),
            pl.BlockSpec((heads * VDIM // steps, LATENT), lambda i: (i, 0)),
        ),
        cost_estimate=pl.CostEstimate(
            flops=rows * width * 4, bytes_accessed=LATENT * heads * VDIM * 6, transcendentals=0
        ),
        name="prepare",
    )(block_order, queries, value_weight)


def attend_kernel(blocks, tok_rows, heads, qt_ref, wk_ref, wvt_ref, *rest):
    sources = rest[:blocks]
    out_ref, rows_ref, turned_ref = rest[blocks:]
    own_rows = sources[0].shape[0]

    @pl.when(pl.program_id(0) == 0)
    def _():
        for slot in range(blocks):
            rows_ref[slot * own_rows : (slot + 1) * own_rows, :] = sources[slot][...]
        turned_ref[...] = rows_ref[:, :LATENT].T

    scale = math.log2(math.e) / math.sqrt(NOPE + ROPE)
    latent = rows_ref[:, :LATENT]
    tail = rows_ref[:, LATENT:]
    key_ids = lax.broadcasted_iota(jnp.int32, (tok_rows, tok_rows), 0)
    query_ids = lax.broadcasted_iota(jnp.int32, (tok_rows, tok_rows), 1)
    causal = jnp.where(key_ids <= query_ids, 0.0, NEG)
    for pair in range(heads // 2):
        keys = jnp.dot(latent, wk_ref[:, pair * 256 : pair * 256 + 256], preferred_element_type=F32).astype(BF)
        weights = []
        sums = []
        for side in range(2):
            head = pair * 2 + side
            full = jnp.concatenate([keys[:, side * NOPE : side * NOPE + NOPE], tail], axis=1)
            scores = jnp.dot(full, qt_ref[head * QK : head * QK + QK, :], preferred_element_type=F32)
            scores = jnp.concatenate([scores[:tok_rows] + causal, scores[tok_rows:]], axis=0)
            col_max = jnp.max(scores, axis=0, keepdims=True)
            exponent = jnp.exp2((scores - col_max) * scale)
            sums.append(jnp.sum(exponent, axis=0, keepdims=True))
            weights.append(exponent.astype(BF))
        mixed = jnp.dot(turned_ref[...], jnp.concatenate(weights, axis=1), preferred_element_type=F32).astype(BF)
        for side in range(2):
            head = pair * 2 + side
            out = jnp.dot(
                wvt_ref[head * VDIM : head * VDIM + VDIM, :],
                mixed[:, side * tok_rows : (side + 1) * tok_rows],
                preferred_element_type=F32,
            )
            out_ref[:, head * VDIM : head * VDIM + VDIM] = (out / sums[side]).T.astype(BF)


def attend(queries_turned, key_weight, values_turned, blocks):
    tok_rows = queries_turned.shape[1]
    all_heads = key_weight.shape[1] // NOPE
    keys = len(blocks) * blocks[0].shape[0]
    heads = 4 if keys <= 2048 else 2
    return pl.pallas_call(
        functools.partial(attend_kernel, len(blocks), tok_rows, heads),
        out_shape=jax.ShapeDtypeStruct((tok_rows, all_heads * VDIM), BF),
        grid=(all_heads // heads,),
        in_specs=[
            pl.BlockSpec((heads * QK, tok_rows), lambda i: (i, 0)),
            pl.BlockSpec((LATENT, heads * NOPE), lambda i: (0, i)),
            pl.BlockSpec((heads * VDIM, LATENT), lambda i: (i, 0)),
        ]
        + [vmem_spec()] * len(blocks),
        out_specs=pl.BlockSpec((tok_rows, heads * VDIM), lambda i: (0, i)),
        scratch_shapes=[pltpu.VMEM((keys, PACKED), BF), pltpu.VMEM((LATENT, keys), BF)],
        compiler_params=pltpu.CompilerParams(vmem_limit_bytes=48 * 1024 * 1024),
        cost_estimate=pl.CostEstimate(
            flops=2 * keys * all_heads * (LATENT * NOPE + tok_rows * (QK + LATENT)),
            bytes_accessed=LATENT * all_heads * 512,
            transcendentals=keys * tok_rows * all_heads,
        ),
        name="attend",
    )(queries_turned, key_weight, values_turned, *blocks)


def exchange(own, shard_count):
    line = shard_count // 2

    def move(value, route):
        pairs = []
        for place in range(line):
            for side in range(2):
                for core in range(2):
                    to_place, to_side, to_core = route(place, side, core)
                    source = (place * 2 + side) * 2 + core
                    target = ((to_place % line) * 2 + to_side) * 2 + to_core
                    pairs.append((source, target))
        return lax.ppermute(value, AXES, pairs)

    steps = range(1, line)
    along = [move(own, lambda p, s, c, k=k: (p + k, s ^ c, c)) for k in steps]
    across = move(own, lambda p, s, c: (p, 1 - s, c))
    swapped = [move(a, lambda p, s, c: (p, s, 1 - c)) for a in along]
    return [across] + along + swapped


def per_device(
    queries,
    span_latents,
    cache_latents,
    latent_gain,
    key_weight,
    value_weight,
    prefix_length,
    block_order,
):
    shard_count = lax.axis_size("ctx")
    own = pack(span_latents, cache_latents, latent_gain, prefix_length, block_order)
    others = exchange(own, shard_count)
    queries_turned, values_turned = prepare(queries, value_weight, block_order)
    return attend(queries_turned, key_weight, values_turned, [own] + others)


def solution(mesh):
    return jax.shard_map(
        per_device,
        mesh=mesh,
        in_specs=(
            P(("groups", "ctx"), "head"),
            P(("groups", "ctx"), None),
            P(("groups", "ctx"), None),
            P(),
            P(None, "head"),
            P(None, "head"),
            P("groups"),
            P("groups"),
        ),
        out_specs=P(("groups", "ctx"), "head"),
        check_vma=False,
    )
```

```python
import functools
import math

import jax
import jax.numpy as jnp
from jax import lax
from jax.experimental import pallas as pl
from jax.experimental.pallas import tpu as pltpu
from jax.sharding import PartitionSpec as P

LATENT = 512
ROPE = 64
NOPE = 128
VDIM = 128
PACKED = 640
QK = 256
NEG = -1e30
AXES = ("ctx", "head")
BF = jnp.bfloat16
F32 = jnp.float32


def vmem_spec():
    return pl.BlockSpec(memory_space=pltpu.VMEM)


def smem_spec():
    return pl.BlockSpec(memory_space=pltpu.SMEM)


def any_spec():
    return pl.BlockSpec(memory_space=pl.ANY)


def pack_kernel(shard_count, order_ref, prefix_ref, span_ref, cache_ref, gain_ref, out_ref):
    tok_rows = span_ref.shape[1]
    cache_rows = cache_ref.shape[0]
    me = lax.axis_index("ctx")
    latent = span_ref[:LATENT, :].astype(F32)
    mean_square = jnp.mean(latent * latent, axis=0, keepdims=True)
    normed = (latent * lax.rsqrt(mean_square + 1e-06)).T * gain_ref[...]
    out_ref[:tok_rows, :LATENT] = normed.astype(BF)
    rest = lax.broadcasted_iota(jnp.int32, (ROPE, tok_rows), 0)
    rest = jnp.where(rest == order_ref[me], 1.0, 0.0)
    tail = jnp.concatenate([span_ref[LATENT:, :].astype(F32), rest], axis=0)
    out_ref[:tok_rows, LATENT:] = tail.T.astype(BF)
    out_ref[tok_rows:, :LATENT] = cache_ref[:, :LATENT]
    lanes = lax.broadcasted_iota(jnp.int32, (cache_rows, 128), 1)
    slots = me * cache_rows + lax.broadcasted_iota(jnp.int32, (cache_rows, 128), 0)
    hidden = jnp.logical_and(lanes == ROPE + shard_count, slots >= prefix_ref[0])
    out_ref[tok_rows:, LATENT:] = jnp.where(hidden, 1.0, 0.0).astype(BF)
    out_ref[tok_rows:, LATENT : LATENT + ROPE] = cache_ref[:, LATENT:]


def pack(span_latents, cache_latents, gain, prefix_length, block_order):
    rows = span_latents.shape[0] + cache_latents.shape[0]
    return pl.pallas_call(
        functools.partial(pack_kernel, block_order.shape[0]),
        out_shape=jax.ShapeDtypeStruct((rows, PACKED), BF),
        in_specs=[smem_spec(), smem_spec(), vmem_spec(), vmem_spec(), vmem_spec()],
        out_specs=vmem_spec(),
        name="pack_rows",
    )(block_order, prefix_length, span_latents.T, cache_latents, gain.reshape(1, LATENT))


def prepare_kernel(order_ref, q_ref, wk_ref, q_out_ref, wkt_ref):
    me = lax.axis_index("ctx")
    rows = q_ref.shape[0]
    lanes = lax.broadcasted_iota(jnp.int32, (rows, 128), 1)
    low = lanes < ROPE
    hide = jnp.where(lanes - ROPE > order_ref[me], NEG, 0.0)
    for pair in range(q_ref.shape[1] // 384):
        base = pair * 384
        second = q_ref[:, base + 128 : base + 256].astype(F32)
        third = q_ref[:, base + 256 : base + 384].astype(F32)
        second_turned = pltpu.roll(second, 64, 1)
        third_turned = pltpu.roll(third, 64, 1)
        to = pair * 2 * QK
        q_out_ref[:, to : to + 128] = q_ref[:, base : base + 128]
        q_out_ref[:, to + 128 : to + 256] = jnp.where(low, second, hide).astype(BF)
        q_out_ref[:, to + 256 : to + 384] = jnp.where(low, second_turned, third_turned).astype(BF)
        q_out_ref[:, to + 384 : to + 512] = jnp.where(low, third_turned, hide).astype(BF)
    wkt_ref[...] = wk_ref[...].T


def prepare(queries, key_weight, block_order):
    rows, width = queries.shape
    heads = width // (NOPE + ROPE)
    steps = 8
    return pl.pallas_call(
        prepare_kernel,
        out_shape=(
            jax.ShapeDtypeStruct((rows, heads * QK), BF),
            jax.ShapeDtypeStruct((heads * NOPE, LATENT), BF),
        ),
        grid=(steps,),
        in_specs=[
            smem_spec(),
            pl.BlockSpec((rows, width // steps), lambda i: (0, i)),
            pl.BlockSpec((LATENT, heads * NOPE // steps), lambda i: (0, i)),
        ],
        out_specs=(
            pl.BlockSpec((rows, heads * QK // steps), lambda i: (0, i)),
            pl.BlockSpec((heads * NOPE // steps, LATENT), lambda i: (i, 0)),
        ),
        cost_estimate=pl.CostEstimate(
            flops=rows * width * 4, bytes_accessed=LATENT * heads * NOPE * 6, transcendentals=0
        ),
        name="prepare",
    )(block_order, queries, key_weight)


def attend_kernel(blocks, tok_rows, heads, q_ref, wkt_ref, wv_ref, *rest):
    sources = rest[:blocks]
    out_ref, rows_ref, turned_ref = rest[blocks:]
    own_rows = sources[0].shape[0]

    @pl.when(pl.program_id(0) == 0)
    def _():
        for slot in range(blocks):
            rows_ref[slot * own_rows : (slot + 1) * own_rows, :] = sources[slot][...]
        turned_ref[...] = rows_ref[...].T

    scale = math.log2(math.e) / math.sqrt(NOPE + ROPE)
    row_ids = lax.broadcasted_iota(jnp.int32, (tok_rows, tok_rows), 0)
    col_ids = lax.broadcasted_iota(jnp.int32, (tok_rows, tok_rows), 1)
    causal = jnp.where(col_ids <= row_ids, 0.0, NEG)
    keys = jnp.dot(wkt_ref[...], turned_ref[:LATENT, :], preferred_element_type=F32).astype(BF)
    tail = turned_ref[LATENT:, :]
    weights = []
    sums = []
    for head in range(heads):
        full = jnp.concatenate([keys[head * NOPE : head * NOPE + NOPE], tail], axis=0)
        scores = jnp.dot(q_ref[:, head * QK : head * QK + QK], full, preferred_element_type=F32)
        scores = jnp.concatenate([scores[:, :tok_rows] + causal, scores[:, tok_rows:]], axis=1)
        row_max = jnp.max(scores, axis=1, keepdims=True)
        exponent = jnp.exp2((scores - row_max) * scale)
        sums.append(jnp.sum(exponent, axis=1, keepdims=True))
        weights.append(exponent.astype(BF))
    mixed = jnp.dot(jnp.concatenate(weights, axis=0), rows_ref[:, :LATENT], preferred_element_type=F32).astype(BF)
    for head in range(heads):
        wv = wv_ref[:, head * VDIM : head * VDIM + VDIM]
        out = jnp.dot(mixed[head * tok_rows : (head + 1) * tok_rows], wv, preferred_element_type=F32)
        out_ref[:, head * VDIM : head * VDIM + VDIM] = (out / sums[head]).astype(BF)


def attend(arranged, keys_turned, value_weight, blocks):
    tok_rows = arranged.shape[0]
    all_heads = value_weight.shape[1] // VDIM
    keys = len(blocks) * blocks[0].shape[0]
    heads = 4 if keys <= 2048 else 2
    return pl.pallas_call(
        functools.partial(attend_kernel, len(blocks), tok_rows, heads),
        out_shape=jax.ShapeDtypeStruct((tok_rows, all_heads * VDIM), BF),
        grid=(all_heads // heads,),
        in_specs=[
            pl.BlockSpec((tok_rows, heads * QK), lambda i: (0, i)),
            pl.BlockSpec((heads * NOPE, LATENT), lambda i: (i, 0)),
            pl.BlockSpec((LATENT, heads * VDIM), lambda i: (0, i)),
        ]
        + [vmem_spec()] * len(blocks),
        out_specs=pl.BlockSpec((tok_rows, heads * VDIM), lambda i: (0, i)),
        scratch_shapes=[pltpu.VMEM((keys, PACKED), BF), pltpu.VMEM((PACKED, keys), BF)],
        compiler_params=pltpu.CompilerParams(vmem_limit_bytes=(24 if keys <= 2048 else 56) * 1024 * 1024),
        cost_estimate=pl.CostEstimate(
            flops=2 * keys * all_heads * (LATENT * NOPE + tok_rows * (QK + LATENT)),
            bytes_accessed=LATENT * all_heads * 512,
            transcendentals=keys * tok_rows * all_heads,
        ),
        name="attend",
    )(arranged, keys_turned, value_weight, *blocks)


def exchange(own, shard_count, beside):
    line = shard_count // 2

    def move(value, route):
        pairs = []
        for place in range(line):
            for side in range(2):
                for core in range(2):
                    to_place, to_side, to_core = route(place, side, core)
                    source = (place * 2 + side) * 2 + core
                    target = ((to_place % line) * 2 + to_side) * 2 + to_core
                    pairs.append((source, target))
        return lax.ppermute(value, AXES, pairs)

    steps = range(1, line)
    along = [move(own, lambda p, s, c, k=k: (p + k, s ^ c, c)) for k in steps]
    across = move(own, lambda p, s, c: (p, 1 - s, c))
    along, beside = lax.optimization_barrier((along, beside))
    swapped = [move(a, lambda p, s, c: (p, s, 1 - c)) for a in along]
    return [across] + along + swapped, *beside


def per_device(
    queries,
    span_latents,
    cache_latents,
    latent_gain,
    key_weight,
    value_weight,
    prefix_length,
    block_order,
):
    shard_count = lax.axis_size("ctx")
    own = pack(span_latents, cache_latents, latent_gain, prefix_length, block_order)
    arranged, keys_turned = prepare(queries, key_weight, block_order)
    others, arranged, keys_turned = exchange(own, shard_count, (arranged, keys_turned))
    return attend(arranged, keys_turned, value_weight, [own] + others)


def solution(mesh):
    return jax.shard_map(
        per_device,
        mesh=mesh,
        in_specs=(
            P(("groups", "ctx"), "head"),
            P(("groups", "ctx"), None),
            P(("groups", "ctx"), None),
            P(),
            P(None, "head"),
            P(None, "head"),
            P("groups"),
            P("groups"),
        ),
        out_specs=P(("groups", "ctx"), "head"),
        check_vma=False,
    )
```

```python
import functools
import math

import jax
import jax.numpy as jnp
from jax import lax
from jax.experimental import pallas as pl
from jax.experimental.pallas import tpu as pltpu
from jax.sharding import PartitionSpec as P

LATENT = 512
ROPE = 64
NOPE = 128
VDIM = 128
PACKED = 640
QK = 256
NEG = -1e30
AXES = ("ctx", "head")
BF = jnp.bfloat16
F32 = jnp.float32


def vmem_spec():
    return pl.BlockSpec(memory_space=pltpu.VMEM)


def smem_spec():
    return pl.BlockSpec(memory_space=pltpu.SMEM)


def any_spec():
    return pl.BlockSpec(memory_space=pl.ANY)


def pack_kernel(shard_count, order_ref, prefix_ref, span_ref, cache_ref, gain_ref, out_ref, half_ref):
    tok_rows = span_ref.shape[1]
    cache_rows = cache_ref.shape[0]
    half_rows = tok_rows // 2
    me = lax.axis_index("ctx")
    core = lax.axis_index("head")
    latent = span_ref[:LATENT, :].astype(F32)
    mean_square = jnp.mean(latent * latent, axis=0, keepdims=True)
    normed = (latent * lax.rsqrt(mean_square + 1e-06)).T * gain_ref[...]
    rest = lax.broadcasted_iota(jnp.int32, (ROPE, tok_rows), 0)
    rest = jnp.where(rest == order_ref[me], 1.0, 0.0)
    tail = jnp.concatenate([span_ref[LATENT:, :].astype(F32), rest], axis=0)
    span = jnp.concatenate([normed, tail.T], axis=1)
    out_ref[:tok_rows, :] = span.astype(BF)
    half_ref[:half_rows, :] = jnp.where(core == 0, span[:half_rows], span[half_rows:]).astype(BF)
    lanes = lax.broadcasted_iota(jnp.int32, (cache_rows, 128), 1)
    slots = me * cache_rows + lax.broadcasted_iota(jnp.int32, (cache_rows, 128), 0)
    hidden = jnp.logical_and(lanes == ROPE + shard_count, slots >= prefix_ref[0])
    for ref, at in ((out_ref, tok_rows), (half_ref, half_rows)):
        ref[at:, :LATENT] = cache_ref[:, :LATENT]
        ref[at:, LATENT:] = jnp.where(hidden, 1.0, 0.0).astype(BF)
        ref[at:, LATENT : LATENT + ROPE] = cache_ref[:, LATENT:]


def pack(span_latents, cache_latents, gain, prefix_length, block_order):
    tok_rows = span_latents.shape[0]
    cache_rows = cache_latents.shape[0]
    return pl.pallas_call(
        functools.partial(pack_kernel, block_order.shape[0]),
        out_shape=(
            jax.ShapeDtypeStruct((tok_rows + cache_rows, PACKED), BF),
            jax.ShapeDtypeStruct((tok_rows // 2 + cache_rows, PACKED), BF),
        ),
        in_specs=[smem_spec(), smem_spec(), vmem_spec(), vmem_spec(), vmem_spec()],
        out_specs=(vmem_spec(), vmem_spec()),
        name="pack_rows",
    )(block_order, prefix_length, span_latents.T, cache_latents, gain.reshape(1, LATENT))


def turn_kernel(wk_ref, wkt_ref):
    wkt_ref[...] = wk_ref[...].T


def turn(key_weight):
    depth, width = key_weight.shape
    steps = 8
    return pl.pallas_call(
        turn_kernel,
        out_shape=jax.ShapeDtypeStruct((width, depth), BF),
        grid=(steps,),
        in_specs=[pl.BlockSpec((depth, width // steps), lambda i: (0, i))],
        out_specs=pl.BlockSpec((width // steps, depth), lambda i: (i, 0)),
        cost_estimate=pl.CostEstimate(flops=0, bytes_accessed=depth * width * 4, transcendentals=0),
        name="turn_key_weight",
    )(key_weight)


def attend_kernel(blocks, heads, order_ref, q_ref, wkt_ref, wv_ref, own_ref, *rest):
    halves = rest[: 2 * (blocks - 1)]
    out_ref, rows_ref, turned_ref, bias_ref = rest[2 * (blocks - 1) :]
    tok_rows = q_ref.shape[0]
    own_rows = own_ref.shape[0]
    half = tok_rows // 2
    keys_count = blocks * own_rows

    @pl.when(pl.program_id(0) == 0)
    def _():
        rows_ref[:own_rows, :] = own_ref[...]
        for slot in range(1, blocks):
            at = slot * own_rows
            mine, theirs = halves[2 * slot - 2 : 2 * slot]
            rows_ref[at : at + half, :] = mine[:half, :]
            rows_ref[at + half : at + tok_rows, :] = theirs[:half, :]
            rows_ref[at + tok_rows : at + own_rows, :] = mine[half:, :]
        turned_ref[...] = rows_ref[...].T
        marks = turned_ref[LATENT + ROPE :, :].astype(F32)
        places = lax.broadcasted_iota(jnp.int32, marks.shape, 0)
        hide = jnp.where(places > order_ref[lax.axis_index("ctx")], marks, 0.0)
        bias_ref[...] = jnp.sum(hide, axis=0, keepdims=True) * NEG

    scale = math.log2(math.e) / math.sqrt(NOPE + ROPE)
    row_ids = lax.broadcasted_iota(jnp.int32, (tok_rows, tok_rows), 0)
    col_ids = lax.broadcasted_iota(jnp.int32, (tok_rows, tok_rows), 1)
    causal = jnp.where(col_ids <= row_ids, 0.0, NEG)
    bias = bias_ref[...]
    keys = jnp.dot(wkt_ref[...], turned_ref[:LATENT, :], preferred_element_type=F32).astype(BF)
    rotary = turned_ref[LATENT : LATENT + ROPE, :]
    nothing = jnp.zeros((QK - NOPE - ROPE, keys_count), BF)
    weights = []
    sums = []
    for head in range(heads):
        nope = keys[head * NOPE : head * NOPE + NOPE]
        if head % 2 == 0:
            at = (head // 2) * 384
            full = jnp.concatenate([nope, rotary, nothing], axis=0)
        else:
            at = (head // 2) * 384 + 128
            full = jnp.concatenate([nothing, nope, rotary], axis=0)
        scores = jnp.dot(q_ref[:, at : at + QK], full, preferred_element_type=F32)
        scores = jnp.concatenate([scores[:, :tok_rows] + causal, scores[:, tok_rows:] + bias[:, tok_rows:]], axis=1)
        row_max = jnp.max(scores, axis=1, keepdims=True)
        exponent = jnp.exp2((scores - row_max) * scale)
        sums.append(jnp.sum(exponent, axis=1, keepdims=True))
        weights.append(exponent.astype(BF))
    mixed = jnp.dot(jnp.concatenate(weights, axis=0), rows_ref[:, :LATENT], preferred_element_type=F32).astype(BF)
    for head in range(heads):
        wv = wv_ref[:, head * VDIM : head * VDIM + VDIM]
        out = jnp.dot(mixed[head * tok_rows : (head + 1) * tok_rows], wv, preferred_element_type=F32)
        out_ref[:, head * VDIM : head * VDIM + VDIM] = (out / sums[head]).astype(BF)


def attend(queries, keys_turned, value_weight, block_order, own, halves):
    tok_rows = queries.shape[0]
    all_heads = value_weight.shape[1] // VDIM
    blocks = 1 + len(halves) // 2
    keys = blocks * own.shape[0]
    heads = 4 if keys <= 2048 else 2
    return pl.pallas_call(
        functools.partial(attend_kernel, blocks, heads),
        out_shape=jax.ShapeDtypeStruct((tok_rows, all_heads * VDIM), BF),
        grid=(all_heads // heads,),
        in_specs=[
            smem_spec(),
            pl.BlockSpec((tok_rows, heads * (NOPE + ROPE)), lambda i: (0, i)),
            pl.BlockSpec((heads * NOPE, LATENT), lambda i: (i, 0)),
            pl.BlockSpec((LATENT, heads * VDIM), lambda i: (0, i)),
        ]
        + [vmem_spec()] * (1 + len(halves)),
        out_specs=pl.BlockSpec((tok_rows, heads * VDIM), lambda i: (0, i)),
        scratch_shapes=[
            pltpu.VMEM((keys, PACKED), BF),
            pltpu.VMEM((PACKED, keys), BF),
            pltpu.VMEM((1, keys), F32),
        ],
        compiler_params=pltpu.CompilerParams(vmem_limit_bytes=54 * 1024 * 1024),
        cost_estimate=pl.CostEstimate(
            flops=2 * keys * all_heads * (LATENT * NOPE + tok_rows * (QK + LATENT)),
            bytes_accessed=LATENT * all_heads * 512,
            transcendentals=keys * tok_rows * all_heads,
        ),
        name="attend",
    )(block_order, queries, keys_turned, value_weight, own, *halves)


def exchange(half, shard_count, beside):
    line = shard_count // 2

    def move(value, route):
        pairs = []
        for place in range(line):
            for side in range(2):
                for core in range(2):
                    to_place, to_side, to_core = route(place, side, core)
                    source = (place * 2 + side) * 2 + core
                    target = ((to_place % line) * 2 + to_side) * 2 + to_core
                    pairs.append((source, target))
        return lax.ppermute(value, AXES, pairs)

    def cross(value):
        return move(value, lambda p, s, c: (p, 1 - s, c))

    def swap(value):
        return move(value, lambda p, s, c: (p, s, 1 - c))

    along = [move(half, lambda p, s, c, k=k: (p + k, s, c)) for k in range(1, line)]
    across = cross(half)
    along, across, beside = lax.optimization_barrier((along, across, beside))
    crossed = [cross(a) for a in along]
    mine = [across] + along + crossed
    halves = []
    for value in mine:
        halves += [value, swap(value)]
    return halves, beside


def per_device(
    queries,
    span_latents,
    cache_latents,
    latent_gain,
    key_weight,
    value_weight,
    prefix_length,
    block_order,
):
    shard_count = lax.axis_size("ctx")
    own, half = pack(span_latents, cache_latents, latent_gain, prefix_length, block_order)
    halves, keys_turned = exchange(half, shard_count, turn(key_weight))
    return attend(queries, keys_turned, value_weight, block_order, own, halves)


def solution(mesh):
    return jax.shard_map(
        per_device,
        mesh=mesh,
        in_specs=(
            P(("groups", "ctx"), "head"),
            P(("groups", "ctx"), None),
            P(("groups", "ctx"), None),
            P(),
            P(None, "head"),
            P(None, "head"),
            P("groups"),
            P("groups"),
        ),
        out_specs=P(("groups", "ctx"), "head"),
        check_vma=False,
    )
```

```python
import functools
import math

import jax
import jax.numpy as jnp
from jax import lax
from jax.experimental import pallas as pl
from jax.experimental.pallas import tpu as pltpu
from jax.sharding import PartitionSpec as P

LATENT = 512
ROPE = 64
NOPE = 128
VDIM = 128
PACKED = 640
QK = 256
NEG = -1e30
AXES = ("ctx", "head")
BF = jnp.bfloat16
F32 = jnp.float32


def vmem_spec():
    return pl.BlockSpec(memory_space=pltpu.VMEM)


def smem_spec():
    return pl.BlockSpec(memory_space=pltpu.SMEM)


def pack_kernel(span_ref, cache_ref, gain_ref, out_ref):
    tok_rows = span_ref.shape[1]
    cache_rows = cache_ref.shape[0]
    latent = span_ref[:LATENT, :].astype(F32)
    mean_square = jnp.mean(latent * latent, axis=0, keepdims=True)
    normed = ((latent * lax.rsqrt(mean_square + 1e-06)).T * gain_ref[...]).astype(BF)
    tiles = LATENT // 128
    for tile in range(tiles):
        out_ref[tile * tok_rows : (tile + 1) * tok_rows, :] = normed[:, tile * 128 : (tile + 1) * 128]
    at = tiles * tok_rows
    out_ref[at : at + ROPE, :] = span_ref[LATENT:, :]
    at += ROPE
    for tile in range(tiles):
        out_ref[at : at + cache_rows, :] = cache_ref[:, tile * 128 : (tile + 1) * 128]
        at += cache_rows
    out_ref[at:, :] = jnp.zeros((cache_rows, 128), BF)
    out_ref[at:, :ROPE] = cache_ref[:, LATENT:]


def pack(span_latents, cache_latents, gain):
    tok_rows = span_latents.shape[0]
    cache_rows = cache_latents.shape[0]
    rows = (LATENT // 128) * (tok_rows + cache_rows) + ROPE + cache_rows
    return pl.pallas_call(
        pack_kernel,
        out_shape=jax.ShapeDtypeStruct((rows, 128), BF),
        in_specs=[vmem_spec(), vmem_spec(), vmem_spec()],
        out_specs=vmem_spec(),
        name="pack_rows",
    )(span_latents.T, cache_latents, gain.reshape(1, LATENT))


def origin(route, place, side, core, line):
    kind, step = route
    if kind == "own":
        return place * 2 + side
    if kind == "across":
        return place * 2 + 1 - side
    came = lax.rem(place + line - step, line)
    lane_side = lax.rem(side + core, 2) if kind == "along" else lax.rem(side + 1 - core, 2)
    return came * 2 + lane_side


def chunk_kernel(cfg, order_ref, prefix_ref, q_ref, wk_ref, wv_ref, *rest):
    first, last, routes, cached, heads, line, cache_rows = cfg
    held = 0 if first else 2
    prev = rest[:held]
    blocks = rest[held : held + len(routes)]
    tails = rest[held + len(routes) : held + len(routes) + len(cached)]
    rest = rest[held + len(routes) + len(cached) :]
    outs = 1 if last else (3 if first else 2)
    out_refs = rest[:outs]
    rows_ref, turned_ref, bias_ref = rest[outs:]
    tok_rows = q_ref.shape[0]
    tiles = LATENT // 128
    scale = math.log2(math.e) / math.sqrt(NOPE + ROPE)

    @pl.when(pl.program_id(0) == 0)
    def _():
        me = lax.axis_index("ctx")
        core = lax.axis_index("head")
        place = lax.div(me, 2)
        side = lax.rem(me, 2)
        for slot, route in enumerate(routes):
            to = slice(slot * tok_rows, (slot + 1) * tok_rows)
            for tile in range(tiles):
                part = blocks[slot][tile * tok_rows : (tile + 1) * tok_rows, :]
                rows_ref[to, tile * 128 : (tile + 1) * 128] = part
                turned_ref[tile * 128 : (tile + 1) * 128, to] = part.T
            turned_ref[LATENT:, to] = blocks[slot][tiles * tok_rows : tiles * tok_rows + ROPE, :]
            hidden = order_ref[origin(route, place, side, core, line)] > order_ref[me]
            bias_ref[:, to] = jnp.full((1, tok_rows), jnp.where(hidden, NEG, 0.0), F32)
        at = len(routes) * tok_rows
        lanes = lax.broadcasted_iota(jnp.int32, (1, max(1, len(cached)) * cache_rows), 1)
        slots = jnp.zeros_like(lanes)
        base = tiles * tok_rows + ROPE
        if cached:
            rotary = []
            for index, route in enumerate(cached):
                to = slice(at + index * cache_rows, at + (index + 1) * cache_rows)
                for tile in range(tiles):
                    begin = base + tile * cache_rows
                    rows_ref[to, tile * 128 : (tile + 1) * 128] = tails[index][begin : begin + cache_rows, :]
                rotary.append(tails[index][base + tiles * cache_rows :, :])
                inside = lanes - index * cache_rows
                source = origin(route, place, side, core, line) * cache_rows
                slots = jnp.where(jnp.logical_and(inside >= 0, inside < cache_rows), source + inside, slots)
            turned_ref[:LATENT, at:] = rows_ref[at:, :].T
            turned_ref[LATENT:, at:] = jnp.concatenate(rotary, axis=0).T[:ROPE, :]
            bias_ref[:, at:] = jnp.where(slots >= prefix_ref[0], NEG, 0.0)

    wk = wk_ref[...]
    if first:
        wk = wk.T
        out_refs[2][...] = wk
    keys = jnp.dot(wk, turned_ref[:LATENT, :], preferred_element_type=F32).astype(BF)
    rotary = turned_ref[LATENT:, :]
    nothing = jnp.zeros((QK - NOPE - ROPE, rotary.shape[1]), BF)
    bias = bias_ref[...]
    if first:
        row_ids = lax.broadcasted_iota(jnp.int32, (tok_rows, tok_rows), 0)
        col_ids = lax.broadcasted_iota(jnp.int32, (tok_rows, tok_rows), 1)
        causal = jnp.where(col_ids <= row_ids, 0.0, NEG)
    weights = []
    peaks = []
    sums = []
    for head in range(heads):
        nope = keys[head * NOPE : head * NOPE + NOPE]
        if head % 2 == 0:
            at = (head // 2) * 384
            full = jnp.concatenate([nope, rotary, nothing], axis=0)
        else:
            at = (head // 2) * 384 + 128
            full = jnp.concatenate([nothing, nope, rotary], axis=0)
        scores = jnp.dot(q_ref[:, at : at + QK], full, preferred_element_type=F32)
        if first:
            own = scores[:, :tok_rows] + causal
            scores = jnp.concatenate([own, scores[:, tok_rows:] + bias[:, tok_rows:]], axis=1)
        else:
            scores = scores + bias
        peak = jnp.max(scores, axis=1, keepdims=True)
        exponent = jnp.exp2((scores - peak) * scale)
        peaks.append(peak)
        sums.append(jnp.sum(exponent, axis=1, keepdims=True))
        weights.append(exponent.astype(BF))
    mixed = jnp.dot(jnp.concatenate(weights, axis=0), rows_ref[...], preferred_element_type=F32).astype(BF)
    lanes = lax.broadcasted_iota(jnp.int32, (tok_rows, 128), 1)
    state = jnp.zeros((tok_rows, 128), F32)
    for head in range(heads):
        here = slice(head * VDIM, (head + 1) * VDIM)
        out = jnp.dot(mixed[head * tok_rows : (head + 1) * tok_rows], wv_ref[:, here], preferred_element_type=F32)
        peak, total = peaks[head], sums[head]
        if not first:
            old_peak = prev[1][:, head : head + 1]
            old_total = prev[1][:, heads + head : heads + head + 1]
            top = jnp.maximum(old_peak, peak)
            keep = jnp.exp2((old_peak - top) * scale)
            add = jnp.exp2((peak - top) * scale)
            out = prev[0][:, here] * keep + out * add
            total = old_total * keep + total * add
            peak = top
        if last:
            out_refs[0][:, here] = (out / total).astype(BF)
        else:
            out_refs[0][:, here] = out
            state = jnp.where(lanes == head, peak, jnp.where(lanes == heads + head, total, state))
    if not last:
        out_refs[1][...] = state


def attend_chunk(first, last, scalars, queries, wk, wv, held, blocks, tails, line, cache_rows):
    tok_rows = queries.shape[0]
    all_heads = wv.shape[1] // VDIM
    routes = tuple(route for route, _ in blocks)
    cached = tuple(route for route, _ in tails)
    keys = len(routes) * tok_rows + len(cached) * cache_rows
    heads = 4
    if keys > 2048:
        heads = 2
    steps = all_heads // heads
    acc_spec = pl.BlockSpec((tok_rows, heads * VDIM), lambda i: (0, i))
    ml_spec = pl.BlockSpec((tok_rows, 128), lambda i: (0, i))
    across_spec = pl.BlockSpec((LATENT, heads * NOPE), lambda i: (0, i))
    down_spec = pl.BlockSpec((heads * NOPE, LATENT), lambda i: (i, 0))
    if last:
        out_shape = [jax.ShapeDtypeStruct((tok_rows, all_heads * VDIM), BF)]
        out_specs = [acc_spec]
    else:
        out_shape = [
            jax.ShapeDtypeStruct((tok_rows, all_heads * VDIM), F32),
            jax.ShapeDtypeStruct((tok_rows, steps * 128), F32),
        ]
        out_specs = [acc_spec, ml_spec]
        if first:
            out_shape.append(jax.ShapeDtypeStruct((all_heads * NOPE, LATENT), BF))
            out_specs.append(down_spec)
    return pl.pallas_call(
        functools.partial(chunk_kernel, (first, last, routes, cached, heads, line, cache_rows)),
        out_shape=out_shape,
        grid=(steps,),
        in_specs=[
            smem_spec(),
            smem_spec(),
            pl.BlockSpec((tok_rows, heads * (NOPE + ROPE)), lambda i: (0, i)),
            across_spec if first else down_spec,
            across_spec,
        ]
        + [acc_spec, ml_spec][: len(held)]
        + [vmem_spec()] * (len(blocks) + len(tails)),
        out_specs=out_specs,
        scratch_shapes=[
            pltpu.VMEM((keys, LATENT), BF),
            pltpu.VMEM((LATENT + ROPE, keys), BF),
            pltpu.VMEM((1, keys), F32),
        ],
        compiler_params=pltpu.CompilerParams(vmem_limit_bytes=54 * 1024 * 1024),
        cost_estimate=pl.CostEstimate(
            flops=2 * keys * all_heads * (LATENT * NOPE + tok_rows * (QK + LATENT)),
            bytes_accessed=LATENT * all_heads * 512,
            transcendentals=keys * tok_rows * all_heads,
        ),
        name="attend_first" if first else "attend_last" if last else "attend_next",
    )(*scalars, queries, wk, wv, *held, *[x for _, x in blocks], *[x for _, x in tails])


def mover(line):
    def move(value, route):
        pairs = []
        for place in range(line):
            for side in range(2):
                for core in range(2):
                    to_place, to_side, to_core = route(place, side, core)
                    source = (place * 2 + side) * 2 + core
                    target = ((to_place % line) * 2 + to_side) * 2 + to_core
                    pairs.append((source, target))
        return lax.ppermute(value, AXES, pairs)

    return move


def per_device(
    queries,
    span_latents,
    cache_latents,
    latent_gain,
    key_weight,
    value_weight,
    prefix_length,
    block_order,
):
    line = lax.axis_size("ctx") // 2
    cache_rows = cache_latents.shape[0]
    move = mover(line)
    own = pack(span_latents, cache_latents, latent_gain)
    across = move(own, lambda p, s, c: (p, 1 - s, c))
    along = [move(own, lambda p, s, c, k=k: (p + k, s ^ c, c)) for k in range(1, line)]
    near = [(("own", 0), own), (("across", 0), across)]
    chunk = functools.partial(attend_chunk, line=line, cache_rows=cache_rows)
    scalars = (block_order, prefix_length)
    acc, state, turned = chunk(True, False, scalars, queries, key_weight, value_weight, (), near, [])
    along, acc, state, turned = lax.optimization_barrier((along, acc, state, turned))
    swapped = [move(a, lambda p, s, c: (p, s, 1 - c)) for a in along]
    far = [(("along", k + 1), a) for k, a in enumerate(along)]
    far += [(("swapped", k + 1), w) for k, w in enumerate(swapped)]
    return chunk(False, True, scalars, queries, turned, value_weight, (acc, state), far, near + far)[0]


def solution(mesh):
    return jax.shard_map(
        per_device,
        mesh=mesh,
        in_specs=(
            P(("groups", "ctx"), "head"),
            P(("groups", "ctx"), None),
            P(("groups", "ctx"), None),
            P(),
            P(None, "head"),
            P(None, "head"),
            P("groups"),
            P("groups"),
        ),
        out_specs=P(("groups", "ctx"), "head"),
        check_vma=False,
    )
```

```python
import functools
import math

import jax
import jax.numpy as jnp
from jax import lax
from jax.experimental import pallas as pl
from jax.experimental.pallas import tpu as pltpu
from jax.sharding import PartitionSpec as P

LATENT = 512
ROPE = 64
NOPE = 128
VDIM = 128
PACKED = 640
QK = 256
NEG = -1e30
AXES = ("ctx", "head")
BF = jnp.bfloat16
F32 = jnp.float32


def vmem_spec():
    return pl.BlockSpec(memory_space=pltpu.VMEM)


def smem_spec():
    return pl.BlockSpec(memory_space=pltpu.SMEM)


def any_spec():
    return pl.BlockSpec(memory_space=pl.ANY)


def pack_kernel(span_ref, cache_ref, gain_ref, out_ref):
    tok_rows = span_ref.shape[1]
    cache_rows = cache_ref.shape[0]
    latent = span_ref[:LATENT, :].astype(F32)
    mean_square = jnp.mean(latent * latent, axis=0, keepdims=True)
    normed = ((latent * lax.rsqrt(mean_square + 1e-06)).T * gain_ref[...]).astype(BF)
    tiles = LATENT // 128
    for tile in range(tiles):
        out_ref[tile * tok_rows : (tile + 1) * tok_rows, :] = normed[:, tile * 128 : (tile + 1) * 128]
    at = tiles * tok_rows
    out_ref[at : at + ROPE, :] = span_ref[LATENT:, :]
    at += ROPE
    for tile in range(tiles):
        out_ref[at : at + cache_rows, :] = cache_ref[:, tile * 128 : (tile + 1) * 128]
        at += cache_rows
    out_ref[at:, :] = jnp.zeros((cache_rows, 128), BF)
    out_ref[at:, :ROPE] = cache_ref[:, LATENT:]


def pack(span_latents, cache_latents, gain):
    tok_rows = span_latents.shape[0]
    cache_rows = cache_latents.shape[0]
    rows = (LATENT // 128) * (tok_rows + cache_rows) + ROPE + cache_rows
    return pl.pallas_call(
        pack_kernel,
        out_shape=jax.ShapeDtypeStruct((rows, 128), BF),
        in_specs=[vmem_spec(), vmem_spec(), vmem_spec()],
        out_specs=vmem_spec(),
        name="pack_rows",
    )(span_latents.T, cache_latents, gain.reshape(1, LATENT))


def origin(route, place, side, core, line):
    kind, step = route
    if kind == "own":
        return place * 2 + side
    if kind == "across":
        return place * 2 + 1 - side
    came = lax.rem(place + line - step, line)
    lane_side = lax.rem(side + core, 2) if kind == "along" else lax.rem(side + 1 - core, 2)
    return came * 2 + lane_side


def turn_kernel(wk_ref, *rest):
    rest[-1][...] = wk_ref[...].T


def turn(key_weight, part, before):
    depth, width = key_weight.shape
    steps = 4
    block = width // (2 * steps)
    return pl.pallas_call(
        turn_kernel,
        out_shape=jax.ShapeDtypeStruct((width, depth), BF),
        grid=(steps,),
        in_specs=[pl.BlockSpec((depth, block), lambda i: (0, i + part * steps))] + [any_spec()] * len(before),
        out_specs=pl.BlockSpec((block, depth), lambda i: (i + part * steps, 0)),
        input_output_aliases={1: 0} if before else {},
        cost_estimate=pl.CostEstimate(flops=0, bytes_accessed=1024, transcendentals=0),
        name="turn_key_weight",
    )(key_weight, *before)


def gather_rows(cfg, order_ref, prefix_ref, blocks, tails, rows_ref, turned_ref, bias_ref):
    routes, cached, line, cache_rows, tok_rows = cfg
    tiles = LATENT // 128
    me = lax.axis_index("ctx")
    core = lax.axis_index("head")
    place = lax.div(me, 2)
    side = lax.rem(me, 2)
    for slot, route in enumerate(routes):
        to = slice(slot * tok_rows, (slot + 1) * tok_rows)
        for tile in range(tiles):
            part = blocks[slot][tile * tok_rows : (tile + 1) * tok_rows, :]
            rows_ref[to, tile * 128 : (tile + 1) * 128] = part
            turned_ref[tile * 128 : (tile + 1) * 128, to] = part.T
        turned_ref[LATENT:, to] = blocks[slot][tiles * tok_rows : tiles * tok_rows + ROPE, :]
        hidden = order_ref[origin(route, place, side, core, line)] > order_ref[me]
        bias_ref[:, to] = jnp.full((1, tok_rows), jnp.where(hidden, NEG, 0.0), F32)
    if not cached:
        return
    at = len(routes) * tok_rows
    lanes = lax.broadcasted_iota(jnp.int32, (1, len(cached) * cache_rows), 1)
    slots = jnp.zeros_like(lanes)
    base = tiles * tok_rows + ROPE
    rotary = []
    for index, route in enumerate(cached):
        to = slice(at + index * cache_rows, at + (index + 1) * cache_rows)
        for tile in range(tiles):
            begin = base + tile * cache_rows
            rows_ref[to, tile * 128 : (tile + 1) * 128] = tails[index][begin : begin + cache_rows, :]
        rotary.append(tails[index][base + tiles * cache_rows :, :])
        inside = lanes - index * cache_rows
        source = origin(route, place, side, core, line) * cache_rows
        slots = jnp.where(jnp.logical_and(inside >= 0, inside < cache_rows), source + inside, slots)
    turned_ref[:LATENT, at:] = rows_ref[at:, :].T
    turned_ref[LATENT:, at:] = jnp.concatenate(rotary, axis=0).T[:ROPE, :]
    bias_ref[:, at:] = jnp.where(slots >= prefix_ref[0], NEG, 0.0)


def chunk_kernel(cfg, last, steps, order_ref, prefix_ref, q_old_ref, q_new_ref, wk_ref, wv_ref, *rest):
    routes, cached = cfg[:2]
    tok_rows = cfg[4]
    if last:
        acc_ref, state_old_ref, state_new_ref = rest[:3]
        rest = rest[3:]
    blocks = rest[: len(routes)]
    tails = rest[len(routes) : len(routes) + len(cached)]
    rest = rest[len(routes) + len(cached) :]
    outs = 1 if last else 2
    out_refs = rest[:outs]
    rows_ref, turned_ref, bias_ref = rest[outs : outs + 3]
    key_refs = rest[outs + 3 : outs + 5]
    weight_refs = rest[outs + 5 : outs + 7]
    stat_refs = rest[outs + 7 : outs + 9]
    scale = math.log2(math.e) / math.sqrt(NOPE + ROPE)
    step = pl.program_id(0)

    def make_keys(buffer):
        wk = wk_ref[buffer * 256 : buffer * 256 + 256, :]
        key_refs[buffer][...] = jnp.dot(wk, turned_ref[:LATENT, :], preferred_element_type=F32).astype(BF)

    def make_scores(buffer, q_ref):
        rotary = turned_ref[LATENT:, :]
        nothing = jnp.zeros((QK - NOPE - ROPE, rotary.shape[1]), BF)
        result = []
        for head in range(2):
            nope = key_refs[buffer][head * NOPE : head * NOPE + NOPE, :]
            parts = [nope, rotary, nothing] if head == 0 else [nothing, nope, rotary]
            full = jnp.concatenate(parts, axis=0)
            query = q_ref[:, head * 128 : head * 128 + QK]
            result.append(jnp.dot(query, full, preferred_element_type=F32))
        return result

    def make_weights(buffer, both, state_ref):
        bias = bias_ref[...]
        for head in range(2):
            scores = both[head]
            if last:
                scores = scores + bias
            else:
                row_ids = lax.broadcasted_iota(jnp.int32, (tok_rows, tok_rows), 0)
                col_ids = lax.broadcasted_iota(jnp.int32, (tok_rows, tok_rows), 1)
                causal = jnp.where(col_ids <= row_ids, 0.0, NEG)
                own = scores[:, :tok_rows] + causal
                scores = jnp.concatenate([own, scores[:, tok_rows:] + bias[:, tok_rows:]], axis=1)
            peak = jnp.max(scores, axis=1, keepdims=True)
            if last:
                old_peak = state_ref[:, 2 * head : 2 * head + 1]
                peak = jnp.maximum(peak, old_peak)
                keep = jnp.exp2((old_peak - peak) * scale)
            exponent = jnp.exp2((scores - peak) * scale)
            total = jnp.sum(exponent, axis=1, keepdims=True)
            if last:
                total = total + state_ref[:, 2 * head + 1 : 2 * head + 2] * keep
                stat_refs[buffer][:, 2 * head : 2 * head + 1] = keep
            else:
                stat_refs[buffer][:, 2 * head : 2 * head + 1] = peak
            stat_refs[buffer][:, 2 * head + 1 : 2 * head + 2] = total
            weight_refs[buffer][head * tok_rows : (head + 1) * tok_rows, :] = exponent.astype(BF)

    def make_outputs(buffer):
        mixed = jnp.dot(weight_refs[buffer][...], rows_ref[...], preferred_element_type=F32).astype(BF)
        for head in range(2):
            here = slice((buffer * 2 + head) * VDIM, (buffer * 2 + head + 1) * VDIM)
            out = jnp.dot(mixed[head * tok_rows : (head + 1) * tok_rows], wv_ref[:, here], preferred_element_type=F32)
            if last:
                out = out + acc_ref[:, here] * stat_refs[buffer][:, 2 * head : 2 * head + 1]
                total = stat_refs[buffer][:, 2 * head + 1 : 2 * head + 2]
                out_refs[0][:, here] = (out / total).astype(BF)
            else:
                out_refs[0][:, here] = out
        if not last:
            out_refs[1][:, buffer * 128 : buffer * 128 + 128] = stat_refs[buffer][...]

    states = (state_old_ref, state_new_ref) if last else (None, None)

    @pl.when(step == 0)
    def _():
        gather_rows(cfg, order_ref, prefix_ref, blocks, tails, rows_ref, turned_ref, bias_ref)
        for ref in stat_refs:
            ref[...] = jnp.zeros_like(ref)
        make_keys(0)
        scores = make_scores(0, q_new_ref)
        make_keys(1)
        make_weights(0, scores, states[1])

    @pl.when(jnp.logical_and(step > 0, step < steps))
    def _():
        scores = make_scores(1, q_old_ref)
        make_keys(0)
        make_outputs(0)
        make_weights(1, scores, states[0])
        scores = make_scores(0, q_new_ref)
        make_keys(1)
        make_outputs(1)
        make_weights(0, scores, states[1])

    @pl.when(step == steps)
    def _():
        scores = make_scores(1, q_old_ref)
        make_outputs(0)
        make_weights(1, scores, states[0])
        make_outputs(1)


def attend_chunk(last, scalars, queries, wkt, wv, held, blocks, tails, line, cache_rows):
    tok_rows = queries.shape[0]
    all_heads = wv.shape[1] // VDIM
    routes = tuple(route for route, _ in blocks)
    cached = tuple(route for route, _ in tails)
    keys = len(routes) * tok_rows + len(cached) * cache_rows
    steps = all_heads // 4
    pairs = all_heads // 2
    pair_width = 2 * (NOPE + ROPE)

    def behind(i):
        return jnp.maximum(i - 1, 0)

    def ahead(i):
        return jnp.minimum(i, steps - 1)

    def old_pair(i):
        return jnp.maximum(2 * i - 1, 0)

    def new_pair(i):
        return jnp.minimum(2 * i, pairs - 1)

    out_spec = pl.BlockSpec((tok_rows, 4 * VDIM), lambda i: (0, behind(i)))
    in_specs = [
        smem_spec(),
        smem_spec(),
        pl.BlockSpec((tok_rows, pair_width), lambda i: (0, old_pair(i))),
        pl.BlockSpec((tok_rows, pair_width), lambda i: (0, new_pair(i))),
        pl.BlockSpec((4 * NOPE, LATENT), lambda i: (ahead(i), 0)),
        pl.BlockSpec((LATENT, 4 * VDIM), lambda i: (0, behind(i))),
    ]
    if last:
        out_shape = [jax.ShapeDtypeStruct((tok_rows, all_heads * VDIM), BF)]
        out_specs = [out_spec]
        in_specs += [
            out_spec,
            pl.BlockSpec((tok_rows, 128), lambda i: (0, old_pair(i))),
            pl.BlockSpec((tok_rows, 128), lambda i: (0, new_pair(i))),
        ]
        held = (held[0], held[1], held[1])
    else:
        out_shape = [
            jax.ShapeDtypeStruct((tok_rows, all_heads * VDIM), F32),
            jax.ShapeDtypeStruct((tok_rows, pairs * 128), F32),
        ]
        out_specs = [out_spec, pl.BlockSpec((tok_rows, 256), lambda i: (0, behind(i)))]
    cfg = (routes, cached, line, cache_rows, tok_rows)
    return pl.pallas_call(
        functools.partial(chunk_kernel, cfg, last, steps),
        out_shape=out_shape,
        grid=(steps + 1,),
        in_specs=in_specs + [vmem_spec()] * (len(blocks) + len(tails)),
        out_specs=out_specs,
        scratch_shapes=[
            pltpu.VMEM((keys, LATENT), BF),
            pltpu.VMEM((LATENT + ROPE, keys), BF),
            pltpu.VMEM((1, keys), F32),
            pltpu.VMEM((2 * NOPE, keys), BF),
            pltpu.VMEM((2 * NOPE, keys), BF),
            pltpu.VMEM((2 * tok_rows, keys), BF),
            pltpu.VMEM((2 * tok_rows, keys), BF),
            pltpu.VMEM((tok_rows, 128), F32),
            pltpu.VMEM((tok_rows, 128), F32),
        ],
        compiler_params=pltpu.CompilerParams(vmem_limit_bytes=54 * 1024 * 1024),
        cost_estimate=pl.CostEstimate(flops=0, bytes_accessed=1024, transcendentals=0),
        name="attend_last" if last else "attend_first",
    )(*scalars, queries, queries, wkt, wv, *held, *[x for _, x in blocks], *[x for _, x in tails])


def mover(line):
    def move(value, route):
        pairs = []
        for place in range(line):
            for side in range(2):
                for core in range(2):
                    to_place, to_side, to_core = route(place, side, core)
                    source = (place * 2 + side) * 2 + core
                    target = ((to_place % line) * 2 + to_side) * 2 + to_core
                    pairs.append((source, target))
        return lax.ppermute(value, AXES, pairs)

    return move


def per_device(
    queries,
    span_latents,
    cache_latents,
    latent_gain,
    key_weight,
    value_weight,
    prefix_length,
    block_order,
):
    line = lax.axis_size("ctx") // 2
    cache_rows = cache_latents.shape[0]
    move = mover(line)
    own = pack(span_latents, cache_latents, latent_gain)

    def swap(value):
        return move(value, lambda p, s, c: (p, s, 1 - c))

    across = move(own, lambda p, s, c: (p, 1 - s, c))
    along = {k: move(own, lambda p, s, c, k=k: (p + k, s ^ c, c)) for k in range(1, line)}
    soon = line - 1
    early = along.pop(soon)
    chunk = functools.partial(attend_chunk, line=line, cache_rows=cache_rows)
    scalars = (block_order, prefix_length)
    turned, early = lax.optimization_barrier((turn(key_weight, 0, ()), early))
    turned = turn(key_weight, 1, (turned,))
    near = [(("own", 0), own), (("across", 0), across)]
    near += [(("along", soon), early), (("swapped", soon), swap(early))]
    held = chunk(False, scalars, queries, turned, value_weight, (), near, [])
    along, held = lax.optimization_barrier((along, held))
    far = [(("along", k), a) for k, a in along.items()]
    far += [(("swapped", k), swap(a)) for k, a in along.items()]
    return chunk(True, scalars, queries, turned, value_weight, held, far, near + far)[0]


def solution(mesh):
    return jax.shard_map(
        per_device,
        mesh=mesh,
        in_specs=(
            P(("groups", "ctx"), "head"),
            P(("groups", "ctx"), None),
            P(("groups", "ctx"), None),
            P(),
            P(None, "head"),
            P(None, "head"),
            P("groups"),
            P("groups"),
        ),
        out_specs=P(("groups", "ctx"), "head"),
        check_vma=False,
    )
```

```python
import functools
import math

import jax
import jax.numpy as jnp
from jax import lax
from jax.experimental import pallas as pl
from jax.experimental.pallas import tpu as pltpu
from jax.sharding import PartitionSpec as P

LATENT = 512
ROPE = 64
NOPE = 128
VDIM = 128
PACKED = 640
QK = 256
NEG = -1e30
VMEM_BYTES = 50 * 1024 * 1024
AXES = ("ctx", "head")
BF = jnp.bfloat16
F32 = jnp.float32


def vmem_spec():
    return pl.BlockSpec(memory_space=pltpu.VMEM)


def smem_spec():
    return pl.BlockSpec(memory_space=pltpu.SMEM)


def pack_kernel(span_ref, cache_ref, gain_ref, out_ref):
    tok_rows = span_ref.shape[1]
    cache_rows = cache_ref.shape[0]
    latent = span_ref[:LATENT, :].astype(F32)
    mean_square = jnp.mean(latent * latent, axis=0, keepdims=True)
    normed = ((latent * lax.rsqrt(mean_square + 1e-06)).T * gain_ref[...]).astype(BF)
    tiles = LATENT // 128
    for tile in range(tiles):
        out_ref[tile * tok_rows : (tile + 1) * tok_rows, :] = normed[:, tile * 128 : (tile + 1) * 128]
    at = tiles * tok_rows
    out_ref[at : at + ROPE, :] = span_ref[LATENT:, :]
    at += ROPE
    for tile in range(tiles):
        out_ref[at : at + cache_rows, :] = cache_ref[:, tile * 128 : (tile + 1) * 128]
        at += cache_rows
    out_ref[at:, :] = jnp.zeros((cache_rows, 128), BF)
    out_ref[at:, :ROPE] = cache_ref[:, LATENT:]


def pack(span_latents, cache_latents, gain):
    tok_rows = span_latents.shape[0]
    cache_rows = cache_latents.shape[0]
    rows = (LATENT // 128) * (tok_rows + cache_rows) + ROPE + cache_rows
    return pl.pallas_call(
        pack_kernel,
        out_shape=jax.ShapeDtypeStruct((rows, 128), BF),
        in_specs=[vmem_spec(), vmem_spec(), vmem_spec()],
        out_specs=vmem_spec(),
        name="pack_rows",
    )(span_latents.T, cache_latents, gain.reshape(1, LATENT))


def origin(route, place, side, core, line):
    kind, step = route
    if kind == "own":
        return place * 2 + side
    if kind == "across":
        return place * 2 + 1 - side
    came = lax.rem(place + line - step, line)
    lane_side = lax.rem(side + core, 2) if kind == "along" else lax.rem(side + 1 - core, 2)
    return came * 2 + lane_side


def start_kernel(wk_ref, *rest):
    blocks = rest[:-3]
    wkt_ref, keys_ref, turned_ref = rest[-3:]
    tok_rows = turned_ref.shape[1] // len(blocks)

    @pl.when(pl.program_id(0) == 0)
    def _():
        for slot, block in enumerate(blocks):
            for tile in range(LATENT // 128):
                part = block[tile * tok_rows : (tile + 1) * tok_rows, :]
                turned_ref[tile * 128 : (tile + 1) * 128, slot * tok_rows : (slot + 1) * tok_rows] = part.T

    wkt = wk_ref[...].T
    wkt_ref[...] = wkt
    keys_ref[...] = jnp.dot(wkt, turned_ref[...], preferred_element_type=F32).astype(BF)


def start(key_weight, blocks, tok_rows):
    depth, width = key_weight.shape
    steps = 8
    block = width // steps
    keys = len(blocks) * tok_rows
    return pl.pallas_call(
        start_kernel,
        out_shape=(jax.ShapeDtypeStruct((width, depth), BF), jax.ShapeDtypeStruct((width, keys), BF)),
        grid=(steps,),
        in_specs=[pl.BlockSpec((depth, block), lambda i: (0, i))] + [vmem_spec()] * len(blocks),
        out_specs=(
            pl.BlockSpec((block, depth), lambda i: (i, 0)),
            pl.BlockSpec((block, keys), lambda i: (i, 0)),
        ),
        scratch_shapes=[pltpu.VMEM((depth, keys), BF)],
        compiler_params=pltpu.CompilerParams(vmem_limit_bytes=VMEM_BYTES),
        cost_estimate=pl.CostEstimate(
            flops=2 * keys * depth * width, bytes_accessed=depth * width * 4, transcendentals=0
        ),
        name="start_keys",
    )(key_weight, *blocks)


def gather_rows(cfg, early, order_ref, prefix_ref, blocks, tails, rows_ref, turned_ref, bias_ref):
    routes, cached, line, cache_rows, tok_rows = cfg
    tiles = LATENT // 128
    me = lax.axis_index("ctx")
    core = lax.axis_index("head")
    place = lax.div(me, 2)
    side = lax.rem(me, 2)
    for slot, route in enumerate(routes):
        to = slice(slot * tok_rows, (slot + 1) * tok_rows)
        for tile in range(tiles):
            part = blocks[slot][tile * tok_rows : (tile + 1) * tok_rows, :]
            rows_ref[to, tile * 128 : (tile + 1) * 128] = part
            if slot >= early:
                turned_ref[tile * 128 : (tile + 1) * 128, to] = part.T
        turned_ref[LATENT:, to] = blocks[slot][tiles * tok_rows : tiles * tok_rows + ROPE, :]
        hidden = order_ref[origin(route, place, side, core, line)] > order_ref[me]
        bias_ref[:, to] = jnp.full((1, tok_rows), jnp.where(hidden, NEG, 0.0), F32)
    if not cached:
        return
    at = len(routes) * tok_rows
    lanes = lax.broadcasted_iota(jnp.int32, (1, len(cached) * cache_rows), 1)
    slots = jnp.zeros_like(lanes)
    base = tiles * tok_rows + ROPE
    rotary = []
    for index, route in enumerate(cached):
        to = slice(at + index * cache_rows, at + (index + 1) * cache_rows)
        for tile in range(tiles):
            begin = base + tile * cache_rows
            rows_ref[to, tile * 128 : (tile + 1) * 128] = tails[index][begin : begin + cache_rows, :]
        rotary.append(tails[index][base + tiles * cache_rows :, :])
        inside = lanes - index * cache_rows
        source = origin(route, place, side, core, line) * cache_rows
        slots = jnp.where(jnp.logical_and(inside >= 0, inside < cache_rows), source + inside, slots)
    turned_ref[:LATENT, at:] = rows_ref[at:, :].T
    turned_ref[LATENT:, at:] = jnp.concatenate(rotary, axis=0).T[:ROPE, :]
    bias_ref[:, at:] = jnp.where(slots >= prefix_ref[0], NEG, 0.0)


def attend_kernel(cfg, early, heads, order_ref, prefix_ref, q_ref, wkt_ref, keys_ref, wv_ref, *rest):
    routes, cached = cfg[:2]
    tok_rows = cfg[4]
    blocks = rest[: len(routes)]
    out_ref, rows_ref, turned_ref, bias_ref = rest[len(routes) :]
    scale = math.log2(math.e) / math.sqrt(NOPE + ROPE)

    @pl.when(pl.program_id(0) == 0)
    def _():
        gather_rows(cfg, early, order_ref, prefix_ref, blocks, blocks, rows_ref, turned_ref, bias_ref)

    here = early * tok_rows
    late = jnp.dot(wkt_ref[...], turned_ref[:LATENT, here:], preferred_element_type=F32).astype(BF)
    keys = jnp.concatenate([keys_ref[...], late], axis=1)
    rotary = turned_ref[LATENT:, :]
    nothing = jnp.zeros((QK - NOPE - ROPE, rotary.shape[1]), BF)
    bias = bias_ref[:, tok_rows:]
    row_ids = lax.broadcasted_iota(jnp.int32, (tok_rows, tok_rows), 0)
    col_ids = lax.broadcasted_iota(jnp.int32, (tok_rows, tok_rows), 1)
    causal = jnp.where(col_ids <= row_ids, 0.0, NEG)
    weights = []
    sums = []
    for head in range(heads):
        nope = keys[head * NOPE : head * NOPE + NOPE]
        if head % 2 == 0:
            at = (head // 2) * 384
            full = jnp.concatenate([nope, rotary, nothing], axis=0)
        else:
            at = (head // 2) * 384 + 128
            full = jnp.concatenate([nothing, nope, rotary], axis=0)
        scores = jnp.dot(q_ref[:, at : at + QK], full, preferred_element_type=F32)
        scores = jnp.concatenate([scores[:, :tok_rows] + causal, scores[:, tok_rows:] + bias], axis=1)
        peak = jnp.max(scores, axis=1, keepdims=True)
        exponent = jnp.exp2((scores - peak) * scale)
        sums.append(jnp.sum(exponent, axis=1, keepdims=True))
        weights.append(exponent.astype(BF))
    mixed = jnp.dot(jnp.concatenate(weights, axis=0), rows_ref[...], preferred_element_type=F32).astype(BF)
    for pair in range(heads // 2):
        lanes = slice(pair * 2 * VDIM, (pair + 1) * 2 * VDIM)
        rows = mixed[pair * 2 * tok_rows : (pair + 1) * 2 * tok_rows]
        both = jnp.dot(rows, wv_ref[:, lanes], preferred_element_type=F32)
        for side in range(2):
            head = pair * 2 + side
            out = both[side * tok_rows : (side + 1) * tok_rows, side * VDIM : (side + 1) * VDIM]
            out_ref[:, head * VDIM : (head + 1) * VDIM] = (out / sums[head]).astype(BF)


def attend(scalars, queries, wkt, early_keys, wv, blocks, early, line, cache_rows):
    tok_rows = queries.shape[0]
    all_heads = wv.shape[1] // VDIM
    routes = tuple(route for route, _ in blocks)
    keys = len(routes) * (tok_rows + cache_rows)
    heads = 4 if keys <= 2048 else 2
    cfg = (routes, routes, line, cache_rows, tok_rows)
    return pl.pallas_call(
        functools.partial(attend_kernel, cfg, early, heads),
        out_shape=jax.ShapeDtypeStruct((tok_rows, all_heads * VDIM), BF),
        grid=(all_heads // heads,),
        in_specs=[
            smem_spec(),
            smem_spec(),
            pl.BlockSpec((tok_rows, heads * (NOPE + ROPE)), lambda i: (0, i)),
            pl.BlockSpec((heads * NOPE, LATENT), lambda i: (i, 0)),
            pl.BlockSpec((heads * NOPE, early * tok_rows), lambda i: (i, 0)),
            pl.BlockSpec((LATENT, heads * VDIM), lambda i: (0, i)),
        ]
        + [vmem_spec()] * len(blocks),
        out_specs=pl.BlockSpec((tok_rows, heads * VDIM), lambda i: (0, i)),
        scratch_shapes=[
            pltpu.VMEM((keys, LATENT), BF),
            pltpu.VMEM((LATENT + ROPE, keys), BF),
            pltpu.VMEM((1, keys), F32),
        ],
        compiler_params=pltpu.CompilerParams(vmem_limit_bytes=VMEM_BYTES),
        cost_estimate=pl.CostEstimate(
            flops=2 * keys * all_heads * (LATENT * NOPE + tok_rows * (QK + LATENT)),
            bytes_accessed=LATENT * all_heads * 512,
            transcendentals=keys * tok_rows * all_heads,
        ),
        name="attend",
    )(*scalars, queries, wkt, early_keys, wv, *[x for _, x in blocks])


def mover(line):
    def move(value, route):
        pairs = []
        for place in range(line):
            for side in range(2):
                for core in range(2):
                    to_place, to_side, to_core = route(place, side, core)
                    source = (place * 2 + side) * 2 + core
                    target = ((to_place % line) * 2 + to_side) * 2 + to_core
                    pairs.append((source, target))
        return lax.ppermute(value, AXES, pairs)

    return move


def per_device(
    queries,
    span_latents,
    cache_latents,
    latent_gain,
    key_weight,
    value_weight,
    prefix_length,
    block_order,
):
    line = lax.axis_size("ctx") // 2
    cache_rows = cache_latents.shape[0]
    move = mover(line)
    own = pack(span_latents, cache_latents, latent_gain)
    across = move(own, lambda p, s, c: (p, 1 - s, c))
    along = [move(own, lambda p, s, c, k=k: (p + k, s ^ c, c)) for k in range(1, line)]
    turned, early_keys = start(key_weight, [own, across], queries.shape[0])
    along, turned, early_keys = lax.optimization_barrier((along, turned, early_keys))
    swapped = [move(a, lambda p, s, c: (p, s, 1 - c)) for a in along]
    blocks = [(("own", 0), own), (("across", 0), across)]
    blocks += [(("along", k + 1), a) for k, a in enumerate(along)]
    blocks += [(("swapped", k + 1), w) for k, w in enumerate(swapped)]
    scalars = (block_order, prefix_length)
    return attend(scalars, queries, turned, early_keys, value_weight, blocks, 2, line, cache_rows)


def solution(mesh):
    return jax.shard_map(
        per_device,
        mesh=mesh,
        in_specs=(
            P(("groups", "ctx"), "head"),
            P(("groups", "ctx"), None),
            P(("groups", "ctx"), None),
            P(),
            P(None, "head"),
            P(None, "head"),
            P("groups"),
            P("groups"),
        ),
        out_specs=P(("groups", "ctx"), "head"),
        check_vma=False,
    )
```

```python
import functools
import math

import jax
import jax.numpy as jnp
from jax import lax
from jax.experimental import pallas as pl
from jax.experimental.pallas import tpu as pltpu
from jax.sharding import PartitionSpec as P

LATENT = 512
ROPE = 64
NOPE = 128
VDIM = 128
PACKED = 640
QK = 256
NEG = -1e30
VMEM_BYTES = 50 * 1024 * 1024
AXES = ("ctx", "head")
BF = jnp.bfloat16
F32 = jnp.float32


def vmem_spec():
    return pl.BlockSpec(memory_space=pltpu.VMEM)


def smem_spec():
    return pl.BlockSpec(memory_space=pltpu.SMEM)


def pack_kernel(span_ref, cache_ref, gain_ref, out_ref):
    tok_rows = span_ref.shape[1]
    cache_rows = cache_ref.shape[0]
    latent = span_ref[:LATENT, :].astype(F32)
    mean_square = jnp.mean(latent * latent, axis=0, keepdims=True)
    normed = ((latent * lax.rsqrt(mean_square + 1e-06)).T * gain_ref[...]).astype(BF)
    tiles = LATENT // 128
    for tile in range(tiles):
        out_ref[tile * tok_rows : (tile + 1) * tok_rows, :] = normed[:, tile * 128 : (tile + 1) * 128]
    at = tiles * tok_rows
    out_ref[at : at + ROPE, :] = span_ref[LATENT:, :]
    at += ROPE
    for tile in range(tiles):
        out_ref[at : at + cache_rows, :] = cache_ref[:, tile * 128 : (tile + 1) * 128]
        at += cache_rows
    out_ref[at:, :] = jnp.zeros((cache_rows, 128), BF)
    out_ref[at:, :ROPE] = cache_ref[:, LATENT:]


def pack(span_latents, cache_latents, gain):
    tok_rows = span_latents.shape[0]
    cache_rows = cache_latents.shape[0]
    rows = (LATENT // 128) * (tok_rows + cache_rows) + ROPE + cache_rows
    return pl.pallas_call(
        pack_kernel,
        out_shape=jax.ShapeDtypeStruct((rows, 128), BF),
        in_specs=[vmem_spec(), vmem_spec(), vmem_spec()],
        out_specs=vmem_spec(),
        name="pack_rows",
    )(span_latents.T, cache_latents, gain.reshape(1, LATENT))


def origin(route, place, side, core, line):
    kind, step = route
    if kind == "own":
        return place * 2 + side
    if kind == "across":
        return place * 2 + 1 - side
    came = lax.rem(place + line - step, line)
    lane_side = lax.rem(side + core, 2) if kind == "along" else lax.rem(side + 1 - core, 2)
    return came * 2 + lane_side


def prepare_kernel(heads, q_ref, wk_ref, wv_ref, latent_ref, wvt_ref):
    rows = q_ref.shape[0]
    turned = q_ref[...].T
    ids = lax.broadcasted_iota(jnp.int32, (PACKED - LATENT - ROPE, rows), 0)
    flags = jnp.where(ids == 0, NEG, 0.0).astype(BF)
    for head in range(heads):
        at = head * (NOPE + ROPE)
        here = slice(head * rows, (head + 1) * rows)
        wk = wk_ref[:, head * NOPE : (head + 1) * NOPE]
        latent_ref[:LATENT, here] = jnp.dot(wk, turned[at : at + NOPE], preferred_element_type=F32).astype(BF)
        latent_ref[LATENT : LATENT + ROPE, here] = turned[at + NOPE : at + NOPE + ROPE]
        latent_ref[LATENT + ROPE :, here] = flags
    wvt_ref[...] = wv_ref[...].T


def prepare(queries, key_weight, value_weight, heads):
    rows = queries.shape[0]
    depth, width = key_weight.shape
    steps = width // (heads * NOPE)
    return pl.pallas_call(
        functools.partial(prepare_kernel, heads),
        out_shape=(
            jax.ShapeDtypeStruct((steps * PACKED, heads * rows), BF),
            jax.ShapeDtypeStruct((steps * heads * VDIM, depth), BF),
        ),
        grid=(steps,),
        in_specs=[
            pl.BlockSpec((rows, heads * (NOPE + ROPE)), lambda i: (0, i)),
            pl.BlockSpec((depth, heads * NOPE), lambda i: (0, i)),
            pl.BlockSpec((depth, heads * VDIM), lambda i: (0, i)),
        ],
        out_specs=(
            pl.BlockSpec((PACKED, heads * rows), lambda i: (i, 0)),
            pl.BlockSpec((heads * VDIM, depth), lambda i: (i, 0)),
        ),
        compiler_params=pltpu.CompilerParams(vmem_limit_bytes=VMEM_BYTES),
        cost_estimate=pl.CostEstimate(
            flops=2 * rows * depth * width, bytes_accessed=depth * width * 8, transcendentals=0
        ),
        name="prepare",
    )(queries, key_weight, value_weight)


def gather_rows(cfg, order_ref, prefix_ref, blocks, rows_ref, turned_ref):
    routes, line, cache_rows, tok_rows = cfg
    tiles = LATENT // 128
    me = lax.axis_index("ctx")
    core = lax.axis_index("head")
    place = lax.div(me, 2)
    side = lax.rem(me, 2)
    lanes = lax.broadcasted_iota(jnp.int32, (tok_rows, ROPE), 1)
    slots = lax.broadcasted_iota(jnp.int32, (cache_rows, 128), 0)
    flag_lane = lax.broadcasted_iota(jnp.int32, (cache_rows, 128), 1) == ROPE
    base = tiles * tok_rows + ROPE
    for slot, route in enumerate(routes):
        block = blocks[slot]
        to = slice(slot * tok_rows, (slot + 1) * tok_rows)
        for tile in range(tiles):
            part = block[tile * tok_rows : (tile + 1) * tok_rows, :]
            rows_ref[to, tile * 128 : (tile + 1) * 128] = part
            turned_ref[tile * 128 : (tile + 1) * 128, to] = part.T
        source = origin(route, place, side, core, line)
        hidden = jnp.where(order_ref[source] > order_ref[me], 1.0, 0.0)
        flags = jnp.where(lanes == 0, hidden, 0.0)
        rotary = block[tiles * tok_rows : base, :].astype(F32).T
        rows_ref[to, LATENT:] = jnp.concatenate([rotary, flags], axis=1).astype(BF)
        at = len(routes) * tok_rows + slot * cache_rows
        to = slice(at, at + cache_rows)
        for tile in range(tiles):
            begin = base + tile * cache_rows
            rows_ref[to, tile * 128 : (tile + 1) * 128] = block[begin : begin + cache_rows, :]
        unused = jnp.logical_and(flag_lane, slots + source * cache_rows >= prefix_ref[0])
        rotary = block[base + tiles * cache_rows :, :].astype(F32)
        rows_ref[to, LATENT:] = jnp.where(unused, 1.0, rotary).astype(BF)
    at = len(routes) * tok_rows
    turned_ref[:, at:] = rows_ref[at:, :LATENT].T


def attend_kernel(cfg, heads, order_ref, prefix_ref, latent_ref, wvt_ref, *rest):
    routes = cfg[0]
    tok_rows = cfg[3]
    blocks = rest[: len(routes)]
    out_ref, rows_ref, turned_ref = rest[len(routes) :]
    scale = math.log2(math.e) / math.sqrt(NOPE + ROPE)

    @pl.when(pl.program_id(0) == 0)
    def _():
        gather_rows(cfg, order_ref, prefix_ref, blocks, rows_ref, turned_ref)

    key_ids = lax.broadcasted_iota(jnp.int32, (tok_rows, heads * tok_rows), 0)
    query_ids = lax.broadcasted_iota(jnp.int32, (tok_rows, heads * tok_rows), 1) % tok_rows
    causal = jnp.where(key_ids <= query_ids, 0.0, NEG)
    scores = jnp.dot(rows_ref[...], latent_ref[...], preferred_element_type=F32)
    scores = jnp.concatenate([scores[:tok_rows] + causal, scores[tok_rows:]], axis=0)
    peak = jnp.max(scores, axis=0, keepdims=True)
    exponent = jnp.exp2((scores - peak) * scale)
    total = jnp.sum(exponent, axis=0, keepdims=True)
    mixed = jnp.dot(turned_ref[...], exponent.astype(BF), preferred_element_type=F32).astype(BF)
    for head in range(heads):
        here = slice(head * tok_rows, (head + 1) * tok_rows)
        wvt = wvt_ref[head * VDIM : (head + 1) * VDIM, :]
        out = jnp.dot(wvt, mixed[:, here], preferred_element_type=F32) / total[:, here]
        out_ref[:, head * VDIM : (head + 1) * VDIM] = out.astype(BF).T


def attend(scalars, latent_queries, wvt, blocks, line, cache_rows, heads):
    tok_rows = latent_queries.shape[1] // heads
    all_heads = wvt.shape[0] // VDIM
    routes = tuple(route for route, _ in blocks)
    keys = len(routes) * (tok_rows + cache_rows)
    cfg = (routes, line, cache_rows, tok_rows)
    return pl.pallas_call(
        functools.partial(attend_kernel, cfg, heads),
        out_shape=jax.ShapeDtypeStruct((tok_rows, all_heads * VDIM), BF),
        grid=(all_heads // heads,),
        in_specs=[
            smem_spec(),
            smem_spec(),
            pl.BlockSpec((PACKED, heads * tok_rows), lambda i: (i, 0)),
            pl.BlockSpec((heads * VDIM, LATENT), lambda i: (i, 0)),
        ]
        + [vmem_spec()] * len(blocks),
        out_specs=pl.BlockSpec((tok_rows, heads * VDIM), lambda i: (0, i)),
        scratch_shapes=[pltpu.VMEM((keys, PACKED), BF), pltpu.VMEM((LATENT, keys), BF)],
        compiler_params=pltpu.CompilerParams(vmem_limit_bytes=VMEM_BYTES),
        cost_estimate=pl.CostEstimate(
            flops=2 * keys * all_heads * tok_rows * (PACKED + LATENT),
            bytes_accessed=LATENT * all_heads * 512,
            transcendentals=keys * tok_rows * all_heads,
        ),
        name="attend",
    )(*scalars, latent_queries, wvt, *[x for _, x in blocks])


def mover(line):
    def move(value, route):
        pairs = []
        for place in range(line):
            for side in range(2):
                for core in range(2):
                    to_place, to_side, to_core = route(place, side, core)
                    source = (place * 2 + side) * 2 + core
                    target = ((to_place % line) * 2 + to_side) * 2 + to_core
                    pairs.append((source, target))
        return lax.ppermute(value, AXES, pairs)

    return move


def per_device(
    queries,
    span_latents,
    cache_latents,
    latent_gain,
    key_weight,
    value_weight,
    prefix_length,
    block_order,
):
    line = lax.axis_size("ctx") // 2
    cache_rows = cache_latents.shape[0]
    move = mover(line)
    own = pack(span_latents, cache_latents, latent_gain)
    heads = 4 if line <= 8 else 2
    across = move(own, lambda p, s, c: (p, 1 - s, c))
    along = [move(own, lambda p, s, c, k=k: (p + k, s ^ c, c)) for k in range(1, line)]
    latent_queries, wvt = prepare(queries, key_weight, value_weight, heads)
    along, latent_queries, wvt = lax.optimization_barrier((along, latent_queries, wvt))
    swapped = [move(a, lambda p, s, c: (p, s, 1 - c)) for a in along]
    blocks = [(("own", 0), own), (("across", 0), across)]
    blocks += [(("along", k + 1), a) for k, a in enumerate(along)]
    blocks += [(("swapped", k + 1), w) for k, w in enumerate(swapped)]
    return attend((block_order, prefix_length), latent_queries, wvt, blocks, line, cache_rows, heads)


def solution(mesh):
    return jax.shard_map(
        per_device,
        mesh=mesh,
        in_specs=(
            P(("groups", "ctx"), "head"),
            P(("groups", "ctx"), None),
            P(("groups", "ctx"), None),
            P(),
            P(None, "head"),
            P(None, "head"),
            P("groups"),
            P("groups"),
        ),
        out_specs=P(("groups", "ctx"), "head"),
        check_vma=False,
    )
```

```python
import functools
import math

import jax
import jax.numpy as jnp
from jax import lax
from jax.experimental import pallas as pl
from jax.experimental.pallas import tpu as pltpu
from jax.sharding import PartitionSpec as P

LATENT = 512
ROPE = 64
NOPE = 128
VDIM = 128
PACKED = 640
QK = 256
NEG = -1e30
VMEM_BYTES = 50 * 1024 * 1024
AXES = ("ctx", "head")
BF = jnp.bfloat16
F32 = jnp.float32


def vmem_spec():
    return pl.BlockSpec(memory_space=pltpu.VMEM)


def smem_spec():
    return pl.BlockSpec(memory_space=pltpu.SMEM)


def pack_kernel(span_ref, cache_ref, gain_ref, out_ref):
    tok_rows = span_ref.shape[1]
    cache_rows = cache_ref.shape[0]
    latent = span_ref[:LATENT, :].astype(F32)
    mean_square = jnp.mean(latent * latent, axis=0, keepdims=True)
    normed = ((latent * lax.rsqrt(mean_square + 1e-06)).T * gain_ref[...]).astype(BF)
    tiles = LATENT // 128
    for tile in range(tiles):
        out_ref[tile * tok_rows : (tile + 1) * tok_rows, :] = normed[:, tile * 128 : (tile + 1) * 128]
    at = tiles * tok_rows
    out_ref[at : at + ROPE, :] = span_ref[LATENT:, :]
    at += ROPE
    for tile in range(tiles):
        out_ref[at : at + cache_rows, :] = cache_ref[:, tile * 128 : (tile + 1) * 128]
        at += cache_rows
    out_ref[at:, :] = jnp.zeros((cache_rows, 128), BF)
    out_ref[at:, :ROPE] = cache_ref[:, LATENT:]


def pack(span_latents, cache_latents, gain):
    tok_rows = span_latents.shape[0]
    cache_rows = cache_latents.shape[0]
    rows = (LATENT // 128) * (tok_rows + cache_rows) + ROPE + cache_rows
    return pl.pallas_call(
        pack_kernel,
        out_shape=jax.ShapeDtypeStruct((rows, 128), BF),
        in_specs=[vmem_spec(), vmem_spec(), vmem_spec()],
        out_specs=vmem_spec(),
        name="pack_rows",
    )(span_latents.T, cache_latents, gain.reshape(1, LATENT))


def origin(route, place, side, core, line):
    kind, step = route
    if kind == "own":
        return place * 2 + side
    if kind == "across":
        return place * 2 + 1 - side
    came = lax.rem(place + line - step, line)
    lane_side = lax.rem(side + core, 2) if kind == "along" else lax.rem(side + 1 - core, 2)
    return came * 2 + lane_side


def prepare_kernel(heads, q_ref, wk_ref, wv_ref, latent_ref, wvt_ref):
    rows = q_ref.shape[0]
    turned = q_ref[...].T
    ids = lax.broadcasted_iota(jnp.int32, (PACKED - LATENT - ROPE, rows), 0)
    flags = jnp.where(ids == 0, NEG, 0.0).astype(BF)
    for head in range(heads):
        at = head * (NOPE + ROPE)
        here = slice(head * rows, (head + 1) * rows)
        wk = wk_ref[:, head * NOPE : (head + 1) * NOPE]
        latent_ref[:LATENT, here] = jnp.dot(wk, turned[at : at + NOPE], preferred_element_type=F32).astype(BF)
        latent_ref[LATENT : LATENT + ROPE, here] = turned[at + NOPE : at + NOPE + ROPE]
        latent_ref[LATENT + ROPE :, here] = flags
    wvt_ref[...] = wv_ref[...].T


def prepare(queries, key_weight, value_weight, heads):
    rows = queries.shape[0]
    depth, width = key_weight.shape
    steps = width // (heads * NOPE)
    return pl.pallas_call(
        functools.partial(prepare_kernel, heads),
        out_shape=(
            jax.ShapeDtypeStruct((steps * PACKED, heads * rows), BF),
            jax.ShapeDtypeStruct((steps * heads * VDIM, depth), BF),
        ),
        grid=(steps,),
        in_specs=[
            pl.BlockSpec((rows, heads * (NOPE + ROPE)), lambda i: (0, i)),
            pl.BlockSpec((depth, heads * NOPE), lambda i: (0, i)),
            pl.BlockSpec((depth, heads * VDIM), lambda i: (0, i)),
        ],
        out_specs=(
            pl.BlockSpec((PACKED, heads * rows), lambda i: (i, 0)),
            pl.BlockSpec((heads * VDIM, depth), lambda i: (i, 0)),
        ),
        compiler_params=pltpu.CompilerParams(vmem_limit_bytes=58 * 1024 * 1024),
        cost_estimate=pl.CostEstimate(
            flops=2 * rows * depth * width, bytes_accessed=depth * width * 8, transcendentals=0
        ),
        name="prepare",
    )(queries, key_weight, value_weight)


def gather_rows(cfg, order_ref, prefix_ref, blocks, rows_ref, turned_ref):
    routes, line, cache_rows, tok_rows = cfg
    tiles = LATENT // 128
    me = lax.axis_index("ctx")
    core = lax.axis_index("head")
    place = lax.div(me, 2)
    side = lax.rem(me, 2)
    lanes = lax.broadcasted_iota(jnp.int32, (tok_rows, ROPE), 1)
    slots = lax.broadcasted_iota(jnp.int32, (cache_rows, 128), 0)
    flag_lane = lax.broadcasted_iota(jnp.int32, (cache_rows, 128), 1) == ROPE
    base = tiles * tok_rows + ROPE
    for slot, route in enumerate(routes):
        block = blocks[slot]
        to = slice(slot * tok_rows, (slot + 1) * tok_rows)
        for tile in range(tiles):
            part = block[tile * tok_rows : (tile + 1) * tok_rows, :]
            rows_ref[to, tile * 128 : (tile + 1) * 128] = part
        source = origin(route, place, side, core, line)
        hidden = jnp.where(order_ref[source] > order_ref[me], 1.0, 0.0)
        flags = jnp.where(lanes == 0, hidden, 0.0)
        rotary = block[tiles * tok_rows : base, :].astype(F32).T
        rows_ref[to, LATENT:] = jnp.concatenate([rotary, flags], axis=1).astype(BF)
        at = len(routes) * tok_rows + slot * cache_rows
        to = slice(at, at + cache_rows)
        for tile in range(tiles):
            begin = base + tile * cache_rows
            rows_ref[to, tile * 128 : (tile + 1) * 128] = block[begin : begin + cache_rows, :]
        unused = jnp.logical_and(flag_lane, slots + source * cache_rows >= prefix_ref[0])
        rotary = block[base + tiles * cache_rows :, :].astype(F32)
        rows_ref[to, LATENT:] = jnp.where(unused, 1.0, rotary).astype(BF)

    def turn(here):
        turned_ref[:, here] = rows_ref[here, :LATENT].T

    total = rows_ref.shape[0]
    return [functools.partial(turn, slice(at, at + 128)) for at in range(0, total, 128)]


def weave(*lanes):
    longest = max(len(lane) for lane in lanes)
    done = [0] * len(lanes)
    for turn in range(1, longest + 1):
        for index, lane in enumerate(lanes):
            while done[index] < len(lane) and done[index] * longest < turn * len(lane):
                lane[done[index]]()
                done[index] += 1


def attend_kernel(cfg, heads, steps, order_ref, prefix_ref, latent_ref, wvt_ref, *rest):
    routes = cfg[0]
    tok_rows = cfg[3]
    blocks = rest[: len(routes)]
    out_ref, rows_ref, turned_ref = rest[len(routes) : len(routes) + 3]
    scratch = rest[len(routes) + 3 :]
    score_refs, weight_refs, peak_refs, total_refs = (scratch[at : at + 2] for at in (0, 2, 4, 6))
    keys = rows_ref.shape[0]
    width = heads * tok_rows
    scale = math.log2(math.e) / math.sqrt(NOPE + ROPE)
    step = pl.program_id(0)
    pieces = [slice(at, min(at + 256, keys)) for at in range(0, keys, 256)]

    def by_eights(value):
        return value.reshape(-1, 8, width)

    def scores(buffer):
        def piece(index):
            here = pieces[index]
            query = latent_ref[buffer * PACKED : (buffer + 1) * PACKED, :]
            result = jnp.dot(rows_ref[here, :], query, preferred_element_type=F32)
            if index == 0:
                key_ids = lax.broadcasted_iota(jnp.int32, (tok_rows, width), 0)
                query_ids = lax.broadcasted_iota(jnp.int32, (tok_rows, width), 1) % tok_rows
                causal = jnp.where(key_ids <= query_ids, 0.0, NEG)
                result = jnp.concatenate([result[:tok_rows] + causal, result[tok_rows:]], axis=0)
            score_refs[buffer][here, :] = result
            peak = jnp.max(by_eights(result), axis=0)
            if index:
                peak = jnp.maximum(peak, peak_refs[buffer][...])
            peak_refs[buffer][...] = peak

        return [functools.partial(piece, index) for index in range(len(pieces))]

    def weights(buffer):
        def piece(index):
            here = pieces[index]
            peak = jnp.max(peak_refs[buffer][...], axis=0, keepdims=True)
            exponent = jnp.exp2((score_refs[buffer][here, :] - peak) * scale)
            total = jnp.sum(by_eights(exponent), axis=0)
            if index:
                total = total + total_refs[buffer][...]
            total_refs[buffer][...] = total
            weight_refs[buffer][here, :] = exponent.astype(BF)

        return [functools.partial(piece, index) for index in range(len(pieces))]

    def outputs(buffer):
        total = jnp.sum(total_refs[buffer][...], axis=0, keepdims=True)
        parts = []

        def mix(index):
            here = slice(index * 256, (index + 1) * 256)
            mixed = jnp.dot(turned_ref[here, :], weight_refs[buffer][...], preferred_element_type=F32)
            parts.append(mixed.astype(BF))

        def finish():
            mixed = jnp.concatenate(parts, axis=0)
            for head in range(heads):
                here = slice(head * tok_rows, (head + 1) * tok_rows)
                place = buffer * heads + head
                wvt = wvt_ref[place * VDIM : (place + 1) * VDIM, :]
                out = jnp.dot(wvt, mixed[:, here], preferred_element_type=F32) / total[:, here]
                out_ref[:, place * VDIM : (place + 1) * VDIM] = out.astype(BF).T

        return [functools.partial(mix, index) for index in range(LATENT // 256)] + [finish]

    @pl.when(step == 0)
    def _():
        turns = gather_rows(cfg, order_ref, prefix_ref, blocks, rows_ref, turned_ref)
        weave(scores(0), turns)
        weave(scores(1), weights(0))

    @pl.when(jnp.logical_and(step > 0, step < steps))
    def _():
        weave(scores(0), weights(1), outputs(0))
        weave(scores(1), weights(0), outputs(1))

    @pl.when(step == steps)
    def _():
        weave(weights(1), outputs(0))
        weave(outputs(1))


def attend(scalars, latent_queries, wvt, blocks, line, cache_rows, heads):
    tok_rows = latent_queries.shape[1] // heads
    all_heads = wvt.shape[0] // VDIM
    routes = tuple(route for route, _ in blocks)
    keys = len(routes) * (tok_rows + cache_rows)
    cfg = (routes, line, cache_rows, tok_rows)
    steps = all_heads // (2 * heads)
    width = heads * tok_rows
    return pl.pallas_call(
        functools.partial(attend_kernel, cfg, heads, steps),
        out_shape=jax.ShapeDtypeStruct((tok_rows, all_heads * VDIM), BF),
        grid=(steps + 1,),
        in_specs=[
            smem_spec(),
            smem_spec(),
            pl.BlockSpec((2 * PACKED, width), lambda i: (jnp.minimum(i, steps - 1), 0)),
            pl.BlockSpec((2 * heads * VDIM, LATENT), lambda i: (jnp.maximum(i - 1, 0), 0)),
        ]
        + [vmem_spec()] * len(blocks),
        out_specs=pl.BlockSpec((tok_rows, 2 * heads * VDIM), lambda i: (0, jnp.maximum(i - 1, 0))),
        scratch_shapes=[pltpu.VMEM((keys, PACKED), BF), pltpu.VMEM((LATENT, keys), BF)]
        + [pltpu.VMEM((keys, width), F32)] * 2
        + [pltpu.VMEM((keys, width), BF)] * 2
        + [pltpu.VMEM((8, width), F32)] * 4,
        compiler_params=pltpu.CompilerParams(vmem_limit_bytes=VMEM_BYTES),
        cost_estimate=pl.CostEstimate(
            flops=2 * keys * all_heads * tok_rows * (PACKED + LATENT),
            bytes_accessed=LATENT * all_heads * 512,
            transcendentals=keys * tok_rows * all_heads,
        ),
        name="attend",
    )(*scalars, latent_queries, wvt, *[x for _, x in blocks])


def mover(line):
    def move(value, route):
        pairs = []
        for place in range(line):
            for side in range(2):
                for core in range(2):
                    to_place, to_side, to_core = route(place, side, core)
                    source = (place * 2 + side) * 2 + core
                    target = ((to_place % line) * 2 + to_side) * 2 + to_core
                    pairs.append((source, target))
        return lax.ppermute(value, AXES, pairs)

    return move


def per_device(
    queries,
    span_latents,
    cache_latents,
    latent_gain,
    key_weight,
    value_weight,
    prefix_length,
    block_order,
):
    line = lax.axis_size("ctx") // 2
    cache_rows = cache_latents.shape[0]
    move = mover(line)
    own = pack(span_latents, cache_latents, latent_gain)
    heads = 4 if line <= 8 else 2
    across = move(own, lambda p, s, c: (p, 1 - s, c))
    along = [move(own, lambda p, s, c, k=k: (p + k, s ^ c, c)) for k in range(1, line)]
    latent_queries, wvt = prepare(queries, key_weight, value_weight, heads)
    along, latent_queries, wvt = lax.optimization_barrier((along, latent_queries, wvt))
    swapped = [move(a, lambda p, s, c: (p, s, 1 - c)) for a in along]
    blocks = [(("own", 0), own), (("across", 0), across)]
    blocks += [(("along", k + 1), a) for k, a in enumerate(along)]
    blocks += [(("swapped", k + 1), w) for k, w in enumerate(swapped)]
    return attend((block_order, prefix_length), latent_queries, wvt, blocks, line, cache_rows, heads)


def solution(mesh):
    return jax.shard_map(
        per_device,
        mesh=mesh,
        in_specs=(
            P(("groups", "ctx"), "head"),
            P(("groups", "ctx"), None),
            P(("groups", "ctx"), None),
            P(),
            P(None, "head"),
            P(None, "head"),
            P("groups"),
            P("groups"),
        ),
        out_specs=P(("groups", "ctx"), "head"),
        check_vma=False,
    )
```

```python
import functools
import math

import jax
import jax.numpy as jnp
from jax import lax
from jax.experimental import pallas as pl
from jax.experimental.pallas import tpu as pltpu
from jax.sharding import PartitionSpec as P

LATENT = 512
ROPE = 64
NOPE = 128
VDIM = 128
PACKED = 640
QK = 256
NEG = -1e30
VMEM_BYTES = 50 * 1024 * 1024
AXES = ("ctx", "head")
BF = jnp.bfloat16
F32 = jnp.float32


def vmem_spec():
    return pl.BlockSpec(memory_space=pltpu.VMEM)


def smem_spec():
    return pl.BlockSpec(memory_space=pltpu.SMEM)


def pack_kernel(span_ref, cache_ref, gain_ref, out_ref):
    tok_rows = span_ref.shape[1]
    cache_rows = cache_ref.shape[0]
    latent = span_ref[:LATENT, :].astype(F32)
    mean_square = jnp.mean(latent * latent, axis=0, keepdims=True)
    normed = ((latent * lax.rsqrt(mean_square + 1e-06)).T * gain_ref[...]).astype(BF)
    tiles = LATENT // 128
    for tile in range(tiles):
        out_ref[tile * tok_rows : (tile + 1) * tok_rows, :] = normed[:, tile * 128 : (tile + 1) * 128]
    at = tiles * tok_rows
    out_ref[at : at + ROPE, :] = span_ref[LATENT:, :]
    at += ROPE
    for tile in range(tiles):
        out_ref[at : at + cache_rows, :] = cache_ref[:, tile * 128 : (tile + 1) * 128]
        at += cache_rows
    out_ref[at:, :] = jnp.zeros((cache_rows, 128), BF)
    out_ref[at:, :ROPE] = cache_ref[:, LATENT:]


def pack(span_latents, cache_latents, gain):
    tok_rows = span_latents.shape[0]
    cache_rows = cache_latents.shape[0]
    rows = (LATENT // 128) * (tok_rows + cache_rows) + ROPE + cache_rows
    return pl.pallas_call(
        pack_kernel,
        out_shape=jax.ShapeDtypeStruct((rows, 128), BF),
        in_specs=[vmem_spec(), vmem_spec(), vmem_spec()],
        out_specs=vmem_spec(),
        name="pack_rows",
    )(span_latents.T, cache_latents, gain.reshape(1, LATENT))


def origin(route, place, side, core, line):
    kind, step = route
    if kind == "own":
        return place * 2 + side
    if kind == "across":
        return place * 2 + 1 - side
    came = lax.rem(place + line - step, line)
    lane_side = lax.rem(side + core, 2) if kind == "along" else lax.rem(side + 1 - core, 2)
    return came * 2 + lane_side


def prepare_kernel(heads, q_ref, wk_ref, wv_ref, latent_ref, wvt_ref):
    rows = q_ref.shape[0]
    turned = q_ref[...].T
    ids = lax.broadcasted_iota(jnp.int32, (PACKED - LATENT - ROPE, rows), 0)
    flags = jnp.where(ids == 0, NEG, 0.0).astype(BF)
    for head in range(heads):
        at = head * (NOPE + ROPE)
        here = slice(head * rows, (head + 1) * rows)
        wk = wk_ref[:, head * NOPE : (head + 1) * NOPE]
        latent_ref[:LATENT, here] = jnp.dot(wk, turned[at : at + NOPE], preferred_element_type=F32).astype(BF)
        latent_ref[LATENT : LATENT + ROPE, here] = turned[at + NOPE : at + NOPE + ROPE]
        latent_ref[LATENT + ROPE :, here] = flags
    wvt_ref[...] = wv_ref[...].T


def prepare(queries, key_weight, value_weight, heads):
    rows = queries.shape[0]
    depth, width = key_weight.shape
    steps = width // (heads * NOPE)
    return pl.pallas_call(
        functools.partial(prepare_kernel, heads),
        out_shape=(
            jax.ShapeDtypeStruct((steps * PACKED, heads * rows), BF),
            jax.ShapeDtypeStruct((steps * heads * VDIM, depth), BF),
        ),
        grid=(steps,),
        in_specs=[
            pl.BlockSpec((rows, heads * (NOPE + ROPE)), lambda i: (0, i)),
            pl.BlockSpec((depth, heads * NOPE), lambda i: (0, i)),
            pl.BlockSpec((depth, heads * VDIM), lambda i: (0, i)),
        ],
        out_specs=(
            pl.BlockSpec((PACKED, heads * rows), lambda i: (i, 0)),
            pl.BlockSpec((heads * VDIM, depth), lambda i: (i, 0)),
        ),
        compiler_params=pltpu.CompilerParams(vmem_limit_bytes=58 * 1024 * 1024),
        cost_estimate=pl.CostEstimate(
            flops=2 * rows * depth * width, bytes_accessed=depth * width * 8, transcendentals=0
        ),
        name="prepare",
    )(queries, key_weight, value_weight)


def gather_rows(cfg, order_ref, prefix_ref, blocks, rows_ref, turned_ref):
    routes, line, cache_rows, tok_rows = cfg
    tiles = LATENT // 128
    me = lax.axis_index("ctx")
    core = lax.axis_index("head")
    place = lax.div(me, 2)
    side = lax.rem(me, 2)
    lanes = lax.broadcasted_iota(jnp.int32, (tok_rows, ROPE), 1)
    slots = lax.broadcasted_iota(jnp.int32, (cache_rows, 128), 0)
    flag_lane = lax.broadcasted_iota(jnp.int32, (cache_rows, 128), 1) == ROPE
    base = tiles * tok_rows + ROPE
    for slot, route in enumerate(routes):
        block = blocks[slot]
        to = slice(slot * tok_rows, (slot + 1) * tok_rows)
        for tile in range(tiles):
            part = block[tile * tok_rows : (tile + 1) * tok_rows, :]
            rows_ref[to, tile * 128 : (tile + 1) * 128] = part
        source = origin(route, place, side, core, line)
        hidden = jnp.where(order_ref[source] > order_ref[me], 1.0, 0.0)
        flags = jnp.where(lanes == 0, hidden, 0.0)
        rotary = block[tiles * tok_rows : base, :].astype(F32).T
        rows_ref[to, LATENT:] = jnp.concatenate([rotary, flags], axis=1).astype(BF)
        at = len(routes) * tok_rows + slot * cache_rows
        to = slice(at, at + cache_rows)
        for tile in range(tiles):
            begin = base + tile * cache_rows
            rows_ref[to, tile * 128 : (tile + 1) * 128] = block[begin : begin + cache_rows, :]
        unused = jnp.logical_and(flag_lane, slots + source * cache_rows >= prefix_ref[0])
        rotary = block[base + tiles * cache_rows :, :].astype(F32)
        rows_ref[to, LATENT:] = jnp.where(unused, 1.0, rotary).astype(BF)

    def turn(here):
        turned_ref[:, here] = rows_ref[here, :LATENT].T

    total = rows_ref.shape[0]
    return [functools.partial(turn, slice(at, at + 128)) for at in range(0, total, 128)]


def weave(*lanes):
    longest = max(len(lane) for lane in lanes)
    done = [0] * len(lanes)
    for turn in range(1, longest + 1):
        for index, lane in enumerate(lanes):
            while done[index] < len(lane) and done[index] * longest < turn * len(lane):
                lane[done[index]]()
                done[index] += 1


def attend_kernel(cfg, heads, steps, order_ref, prefix_ref, latent_ref, wvt_ref, *rest):
    routes = cfg[0]
    tok_rows = cfg[3]
    blocks = rest[: len(routes)]
    out_ref, rows_ref, turned_ref = rest[len(routes) : len(routes) + 3]
    scratch = rest[len(routes) + 3 :]
    score_refs, weight_refs, peak_refs, total_refs = (scratch[at : at + 2] for at in (0, 2, 4, 6))
    keys = rows_ref.shape[0]
    width = heads * tok_rows
    scale = 1.0 / math.sqrt(NOPE + ROPE)
    step = pl.program_id(0)
    pieces = [slice(at, min(at + 256, keys)) for at in range(0, keys, 256)]

    def by_eights(value):
        return value.reshape(-1, 8, width)

    def scores(buffer):
        def piece(index):
            here = pieces[index]
            query = latent_ref[buffer * PACKED : (buffer + 1) * PACKED, :]
            result = jnp.dot(rows_ref[here, :], query, preferred_element_type=F32)
            if index == 0:
                key_ids = lax.broadcasted_iota(jnp.int32, (tok_rows, width), 0)
                query_ids = lax.broadcasted_iota(jnp.int32, (tok_rows, width), 1) % tok_rows
                causal = jnp.where(key_ids <= query_ids, 0.0, NEG)
                result = jnp.concatenate([result[:tok_rows] + causal, result[tok_rows:]], axis=0)
            score_refs[buffer][here, :] = result
            peak = jnp.max(by_eights(result), axis=0)
            if index:
                peak = jnp.maximum(peak, peak_refs[buffer][...])
            peak_refs[buffer][...] = peak

        return [functools.partial(piece, index) for index in range(len(pieces))]

    def weights(buffer):
        def piece(index):
            here = pieces[index]
            peak = jnp.max(peak_refs[buffer][...], axis=0, keepdims=True)
            exponent = jnp.exp((score_refs[buffer][here, :] - peak) * scale)
            total = jnp.sum(by_eights(exponent), axis=0)
            if index:
                total = total + total_refs[buffer][...]
            total_refs[buffer][...] = total
            weight_refs[buffer][here, :] = exponent.astype(BF)

        return [functools.partial(piece, index) for index in range(len(pieces))]

    def outputs(buffer):
        total = jnp.sum(total_refs[buffer][...], axis=0, keepdims=True)
        parts = []

        def mix(index):
            here = slice(index * 256, (index + 1) * 256)
            mixed = jnp.dot(turned_ref[here, :], weight_refs[buffer][...], preferred_element_type=F32)
            parts.append(mixed.astype(BF))

        def finish():
            mixed = jnp.concatenate(parts, axis=0)
            for head in range(heads):
                here = slice(head * tok_rows, (head + 1) * tok_rows)
                place = buffer * heads + head
                wvt = wvt_ref[place * VDIM : (place + 1) * VDIM, :]
                out = jnp.dot(wvt, mixed[:, here], preferred_element_type=F32) / total[:, here]
                out_ref[:, place * VDIM : (place + 1) * VDIM] = out.astype(BF).T

        return [functools.partial(mix, index) for index in range(LATENT // 256)] + [finish]

    @pl.when(step == 0)
    def _():
        turns = gather_rows(cfg, order_ref, prefix_ref, blocks, rows_ref, turned_ref)
        cut = len(turns) // 3
        weave(scores(0), turns[:cut])
        weave(scores(1), weights(0), turns[cut:])

    @pl.when(jnp.logical_and(step > 0, step < steps))
    def _():
        weave(scores(0), weights(1), outputs(0))
        weave(scores(1), weights(0), outputs(1))

    @pl.when(step == steps)
    def _():
        weave(weights(1), outputs(0))
        weave(outputs(1))


def attend(scalars, latent_queries, wvt, blocks, line, cache_rows, heads):
    tok_rows = latent_queries.shape[1] // heads
    all_heads = wvt.shape[0] // VDIM
    routes = tuple(route for route, _ in blocks)
    keys = len(routes) * (tok_rows + cache_rows)
    cfg = (routes, line, cache_rows, tok_rows)
    steps = all_heads // (2 * heads)
    width = heads * tok_rows
    return pl.pallas_call(
        functools.partial(attend_kernel, cfg, heads, steps),
        out_shape=jax.ShapeDtypeStruct((tok_rows, all_heads * VDIM), BF),
        grid=(steps + 1,),
        in_specs=[
            smem_spec(),
            smem_spec(),
            pl.BlockSpec((2 * PACKED, width), lambda i: (jnp.minimum(i, steps - 1), 0)),
            pl.BlockSpec((2 * heads * VDIM, LATENT), lambda i: (jnp.maximum(i - 1, 0), 0)),
        ]
        + [vmem_spec()] * len(blocks),
        out_specs=pl.BlockSpec((tok_rows, 2 * heads * VDIM), lambda i: (0, jnp.maximum(i - 1, 0))),
        scratch_shapes=[pltpu.VMEM((keys, PACKED), BF), pltpu.VMEM((LATENT, keys), BF)]
        + [pltpu.VMEM((keys, width), F32)] * 2
        + [pltpu.VMEM((keys, width), BF)] * 2
        + [pltpu.VMEM((8, width), F32)] * 4,
        compiler_params=pltpu.CompilerParams(vmem_limit_bytes=VMEM_BYTES),
        cost_estimate=pl.CostEstimate(
            flops=2 * keys * all_heads * tok_rows * (PACKED + LATENT),
            bytes_accessed=LATENT * all_heads * 512,
            transcendentals=keys * tok_rows * all_heads,
        ),
        name="attend",
    )(*scalars, latent_queries, wvt, *[x for _, x in blocks])


def mover(line):
    def move(value, route):
        pairs = []
        for place in range(line):
            for side in range(2):
                for core in range(2):
                    to_place, to_side, to_core = route(place, side, core)
                    source = (place * 2 + side) * 2 + core
                    target = ((to_place % line) * 2 + to_side) * 2 + to_core
                    pairs.append((source, target))
        return lax.ppermute(value, AXES, pairs)

    return move


def per_device(
    queries,
    span_latents,
    cache_latents,
    latent_gain,
    key_weight,
    value_weight,
    prefix_length,
    block_order,
):
    line = lax.axis_size("ctx") // 2
    cache_rows = cache_latents.shape[0]
    move = mover(line)
    own = pack(span_latents, cache_latents, latent_gain)
    heads = 4 if line <= 8 else 2
    across = move(own, lambda p, s, c: (p, 1 - s, c))
    along = [move(own, lambda p, s, c, k=k: (p + k, s ^ c, c)) for k in range(1, line)]
    latent_queries, wvt = prepare(queries, key_weight, value_weight, heads)
    along, latent_queries, wvt = lax.optimization_barrier((along, latent_queries, wvt))
    swapped = [move(a, lambda p, s, c: (p, s, 1 - c)) for a in along]
    blocks = [(("own", 0), own), (("across", 0), across)]
    blocks += [(("along", k + 1), a) for k, a in enumerate(along)]
    blocks += [(("swapped", k + 1), w) for k, w in enumerate(swapped)]
    return attend((block_order, prefix_length), latent_queries, wvt, blocks, line, cache_rows, heads)


def solution(mesh):
    return jax.shard_map(
        per_device,
        mesh=mesh,
        in_specs=(
            P(("groups", "ctx"), "head"),
            P(("groups", "ctx"), None),
            P(("groups", "ctx"), None),
            P(),
            P(None, "head"),
            P(None, "head"),
            P("groups"),
            P("groups"),
        ),
        out_specs=P(("groups", "ctx"), "head"),
        check_vma=False,
    )
```

```python
import functools
import math

import jax
import jax.numpy as jnp
from jax import lax
from jax.experimental import pallas as pl
from jax.experimental.pallas import tpu as pltpu
from jax.sharding import PartitionSpec as P

LATENT = 512
ROPE = 64
NOPE = 128
VDIM = 128
PACKED = 768
ONES = 16
QK = 256
NEG = -1e30
VMEM_BYTES = 50 * 1024 * 1024
AXES = ("ctx", "head")
BF = jnp.bfloat16
F32 = jnp.float32


def vmem_spec():
    return pl.BlockSpec(memory_space=pltpu.VMEM)


def smem_spec():
    return pl.BlockSpec(memory_space=pltpu.SMEM)


def pack_kernel(span_ref, cache_ref, gain_ref, out_ref):
    tok_rows = span_ref.shape[1]
    cache_rows = cache_ref.shape[0]
    latent = span_ref[:LATENT, :].astype(F32)
    mean_square = jnp.mean(latent * latent, axis=0, keepdims=True)
    normed = ((latent * lax.rsqrt(mean_square + 1e-06)).T * gain_ref[...]).astype(BF)
    tiles = LATENT // 128
    for tile in range(tiles):
        out_ref[tile * tok_rows : (tile + 1) * tok_rows, :] = normed[:, tile * 128 : (tile + 1) * 128]
    at = tiles * tok_rows
    out_ref[at : at + ROPE, :] = span_ref[LATENT:, :]
    at += ROPE
    for tile in range(tiles):
        out_ref[at : at + cache_rows, :] = cache_ref[:, tile * 128 : (tile + 1) * 128]
        at += cache_rows
    out_ref[at:, :ROPE] = cache_ref[:, LATENT:]
    out_ref[at:, ROPE:] = cache_ref[:, LATENT:]


def pack(span_latents, cache_latents, gain):
    tok_rows = span_latents.shape[0]
    cache_rows = cache_latents.shape[0]
    rows = (LATENT // 128) * (tok_rows + cache_rows) + ROPE + cache_rows
    return pl.pallas_call(
        pack_kernel,
        out_shape=jax.ShapeDtypeStruct((rows, 128), BF),
        in_specs=[vmem_spec(), vmem_spec(), vmem_spec()],
        out_specs=vmem_spec(),
        name="pack_rows",
    )(span_latents.T, cache_latents, gain.reshape(1, LATENT))


def origin(route, place, side, core, line):
    kind, step = route
    if kind == "own":
        return place * 2 + side
    if kind == "across":
        return place * 2 + 1 - side
    came = lax.rem(place + line - step, line)
    lane_side = lax.rem(side + core, 2) if kind == "along" else lax.rem(side + 1 - core, 2)
    return came * 2 + lane_side


def prepare_kernel(heads, q_ref, wk_ref, wv_ref, latent_ref, wvt_ref):
    scale = math.log2(math.e) / math.sqrt(NOPE + ROPE)
    rows = q_ref.shape[0]
    turned = q_ref[...].T
    ids = lax.broadcasted_iota(jnp.int32, (PACKED - LATENT - 2 * ROPE, rows), 0)
    flags = jnp.where(ids == 0, NEG, 0.0).astype(BF)
    for head in range(heads):
        at = head * (NOPE + ROPE)
        here = slice(head * rows, (head + 1) * rows)
        wk = wk_ref[:, head * NOPE : (head + 1) * NOPE]
        latent = jnp.dot(wk, turned[at : at + NOPE], preferred_element_type=F32)
        latent_ref[:LATENT, here] = (latent * scale).astype(BF)
        rotary = turned[at + NOPE : at + NOPE + ROPE].astype(F32) * scale
        rounded = rotary.astype(BF)
        latent_ref[LATENT : LATENT + ROPE, here] = rounded
        latent_ref[LATENT + ROPE : LATENT + 2 * ROPE, here] = (rotary - rounded.astype(F32)).astype(BF)
        latent_ref[LATENT + 2 * ROPE :, here] = flags
    wvt_ref[...] = wv_ref[...].T


def prepare(queries, key_weight, value_weight, heads):
    rows = queries.shape[0]
    depth, width = key_weight.shape
    steps = width // (heads * NOPE)
    return pl.pallas_call(
        functools.partial(prepare_kernel, heads),
        out_shape=(
            jax.ShapeDtypeStruct((steps * PACKED, heads * rows), BF),
            jax.ShapeDtypeStruct((steps * heads * VDIM, depth), BF),
        ),
        grid=(steps,),
        in_specs=[
            pl.BlockSpec((rows, heads * (NOPE + ROPE)), lambda i: (0, i)),
            pl.BlockSpec((depth, heads * NOPE), lambda i: (0, i)),
            pl.BlockSpec((depth, heads * VDIM), lambda i: (0, i)),
        ],
        out_specs=(
            pl.BlockSpec((PACKED, heads * rows), lambda i: (i, 0)),
            pl.BlockSpec((heads * VDIM, depth), lambda i: (i, 0)),
        ),
        compiler_params=pltpu.CompilerParams(vmem_limit_bytes=58 * 1024 * 1024),
        cost_estimate=pl.CostEstimate(
            flops=2 * rows * depth * width, bytes_accessed=depth * width * 8, transcendentals=0
        ),
        name="prepare",
    )(queries, key_weight, value_weight)


def gather_rows(cfg, order_ref, prefix_ref, blocks, rows_ref, turned_ref):
    routes, line, cache_rows, tok_rows = cfg
    tiles = LATENT // 128
    me = lax.axis_index("ctx")
    core = lax.axis_index("head")
    place = lax.div(me, 2)
    side = lax.rem(me, 2)
    lanes = lax.broadcasted_iota(jnp.int32, (tok_rows, 128), 1)
    slots = lax.broadcasted_iota(jnp.int32, (cache_rows, 128), 0)
    flag_lane = lax.broadcasted_iota(jnp.int32, (cache_rows, 128), 1) == 0
    base = tiles * tok_rows + ROPE
    for slot, route in enumerate(routes):
        block = blocks[slot]
        to = slice(slot * tok_rows, (slot + 1) * tok_rows)
        for tile in range(tiles):
            part = block[tile * tok_rows : (tile + 1) * tok_rows, :]
            rows_ref[to, tile * 128 : (tile + 1) * 128] = part
        source = origin(route, place, side, core, line)
        hidden = jnp.where(order_ref[source] > order_ref[me], 1.0, 0.0)
        flags = jnp.where(lanes == 0, hidden, 0.0)
        rotary = block[tiles * tok_rows : base, :]
        rows_ref[to, LATENT : LATENT + 128] = jnp.concatenate([rotary, rotary], axis=0).T
        rows_ref[to, LATENT + 128 :] = flags.astype(BF)
        at = len(routes) * tok_rows + slot * cache_rows
        to = slice(at, at + cache_rows)
        for tile in range(tiles):
            begin = base + tile * cache_rows
            rows_ref[to, tile * 128 : (tile + 1) * 128] = block[begin : begin + cache_rows, :]
        unused = jnp.logical_and(flag_lane, slots + source * cache_rows >= prefix_ref[0])
        rows_ref[to, LATENT : LATENT + 128] = block[base + tiles * cache_rows :, :]
        rows_ref[to, LATENT + 128 :] = jnp.where(unused, 1.0, 0.0).astype(BF)

    def turn(here):
        turned_ref[:LATENT, here] = rows_ref[here, :LATENT].T

    total = rows_ref.shape[0]
    turned_ref[LATENT:, :] = jnp.ones((ONES, total), BF)
    return [functools.partial(turn, slice(at, at + 128)) for at in range(0, total, 128)]


def weave(*lanes):
    longest = max(len(lane) for lane in lanes)
    done = [0] * len(lanes)
    for turn in range(1, longest + 1):
        for index, lane in enumerate(lanes):
            while done[index] < len(lane) and done[index] * longest < turn * len(lane):
                lane[done[index]]()
                done[index] += 1


def attend_kernel(cfg, heads, steps, order_ref, prefix_ref, latent_ref, wvt_ref, *rest):
    routes = cfg[0]
    tok_rows = cfg[3]
    blocks = rest[: len(routes)]
    out_ref, rows_ref, turned_ref = rest[len(routes) : len(routes) + 3]
    scratch = rest[len(routes) + 3 :]
    score_refs, weight_refs, peak_refs = (scratch[at : at + 2] for at in (0, 2, 4))
    keys = rows_ref.shape[0]
    width = heads * tok_rows
    step = pl.program_id(0)
    pieces = [slice(at, min(at + 256, keys)) for at in range(0, keys, 256)]

    def by_eights(value):
        return value.reshape(-1, 8, width)

    def scores(buffer):
        def piece(index):
            here = pieces[index]
            query = latent_ref[buffer * PACKED : (buffer + 1) * PACKED, :]
            result = jnp.dot(rows_ref[here, :], query, preferred_element_type=F32)
            if index == 0:
                key_ids = lax.broadcasted_iota(jnp.int32, (tok_rows, width), 0)
                query_ids = lax.broadcasted_iota(jnp.int32, (tok_rows, width), 1) % tok_rows
                causal = jnp.where(key_ids <= query_ids, 0.0, NEG)
                result = jnp.concatenate([result[:tok_rows] + causal, result[tok_rows:]], axis=0)
            score_refs[buffer][here, :] = result
            peak = jnp.max(by_eights(result), axis=0)
            if index:
                peak = jnp.maximum(peak, peak_refs[buffer][...])
            peak_refs[buffer][...] = peak

        return [functools.partial(piece, index) for index in range(len(pieces))]

    def weights(buffer):
        def piece(index):
            here = pieces[index]
            peak = jnp.max(peak_refs[buffer][...], axis=0, keepdims=True)
            weight_refs[buffer][here, :] = jnp.exp2(score_refs[buffer][here, :] - peak).astype(BF)

        return [functools.partial(piece, index) for index in range(len(pieces))]

    def outputs(buffer):
        parts = []
        totals = []

        def mix(index):
            first = index * 256
            final = index == LATENT // 256 - 1
            here = slice(first, LATENT + ONES if final else first + 256)
            mixed = jnp.dot(turned_ref[here, :], weight_refs[buffer][...], preferred_element_type=F32)
            parts.append(mixed[:256].astype(BF))
            if final:
                totals.append(mixed[256:257])

        def finish():
            total = totals[0]
            mixed = jnp.concatenate(parts, axis=0)
            for head in range(heads):
                here = slice(head * tok_rows, (head + 1) * tok_rows)
                place = buffer * heads + head
                wvt = wvt_ref[place * VDIM : (place + 1) * VDIM, :]
                out = jnp.dot(wvt, mixed[:, here], preferred_element_type=F32) / total[:, here]
                out_ref[:, place * VDIM : (place + 1) * VDIM] = out.astype(BF).T

        return [functools.partial(mix, index) for index in range(LATENT // 256)] + [finish]

    @pl.when(step == 0)
    def _():
        turns = gather_rows(cfg, order_ref, prefix_ref, blocks, rows_ref, turned_ref)
        cut = len(turns) // 3
        weave(scores(0), turns[:cut])
        weave(scores(1), weights(0), turns[cut:])

    @pl.when(jnp.logical_and(step > 0, step < steps))
    def _():
        weave(scores(0), weights(1), outputs(0))
        weave(scores(1), weights(0), outputs(1))

    @pl.when(step == steps)
    def _():
        weave(weights(1), outputs(0))
        weave(outputs(1))


def attend(scalars, latent_queries, wvt, blocks, line, cache_rows, heads):
    tok_rows = latent_queries.shape[1] // heads
    all_heads = wvt.shape[0] // VDIM
    routes = tuple(route for route, _ in blocks)
    keys = len(routes) * (tok_rows + cache_rows)
    cfg = (routes, line, cache_rows, tok_rows)
    steps = all_heads // (2 * heads)
    width = heads * tok_rows
    return pl.pallas_call(
        functools.partial(attend_kernel, cfg, heads, steps),
        out_shape=jax.ShapeDtypeStruct((tok_rows, all_heads * VDIM), BF),
        grid=(steps + 1,),
        in_specs=[
            smem_spec(),
            smem_spec(),
            pl.BlockSpec((2 * PACKED, width), lambda i: (jnp.minimum(i, steps - 1), 0)),
            pl.BlockSpec((2 * heads * VDIM, LATENT), lambda i: (jnp.maximum(i - 1, 0), 0)),
        ]
        + [vmem_spec()] * len(blocks),
        out_specs=pl.BlockSpec((tok_rows, 2 * heads * VDIM), lambda i: (0, jnp.maximum(i - 1, 0))),
        scratch_shapes=[pltpu.VMEM((keys, PACKED), BF), pltpu.VMEM((LATENT + ONES, keys), BF)]
        + [pltpu.VMEM((keys, width), F32)] * 2
        + [pltpu.VMEM((keys, width), BF)] * 2
        + [pltpu.VMEM((8, width), F32)] * 2,
        compiler_params=pltpu.CompilerParams(vmem_limit_bytes=VMEM_BYTES),
        cost_estimate=pl.CostEstimate(
            flops=2 * keys * all_heads * tok_rows * (PACKED + LATENT),
            bytes_accessed=LATENT * all_heads * 512,
            transcendentals=keys * tok_rows * all_heads,
        ),
        name="attend",
    )(*scalars, latent_queries, wvt, *[x for _, x in blocks])


def mover(line):
    def move(value, route):
        pairs = []
        for place in range(line):
            for side in range(2):
                for core in range(2):
                    to_place, to_side, to_core = route(place, side, core)
                    source = (place * 2 + side) * 2 + core
                    target = ((to_place % line) * 2 + to_side) * 2 + to_core
                    pairs.append((source, target))
        return lax.ppermute(value, AXES, pairs)

    return move


def per_device(
    queries,
    span_latents,
    cache_latents,
    latent_gain,
    key_weight,
    value_weight,
    prefix_length,
    block_order,
):
    line = lax.axis_size("ctx") // 2
    cache_rows = cache_latents.shape[0]
    move = mover(line)
    own = pack(span_latents, cache_latents, latent_gain)
    heads = 4 if line <= 8 else 2
    across = move(own, lambda p, s, c: (p, 1 - s, c))
    along = [move(own, lambda p, s, c, k=k: (p + k, s ^ c, c)) for k in range(1, line)]
    latent_queries, wvt = prepare(queries, key_weight, value_weight, heads)
    along, latent_queries, wvt = lax.optimization_barrier((along, latent_queries, wvt))
    swapped = [move(a, lambda p, s, c: (p, s, 1 - c)) for a in along]
    blocks = [(("own", 0), own), (("across", 0), across)]
    blocks += [(("along", k + 1), a) for k, a in enumerate(along)]
    blocks += [(("swapped", k + 1), w) for k, w in enumerate(swapped)]
    return attend((block_order, prefix_length), latent_queries, wvt, blocks, line, cache_rows, heads)


def solution(mesh):
    return jax.shard_map(
        per_device,
        mesh=mesh,
        in_specs=(
            P(("groups", "ctx"), "head"),
            P(("groups", "ctx"), None),
            P(("groups", "ctx"), None),
            P(),
            P(None, "head"),
            P(None, "head"),
            P("groups"),
            P("groups"),
        ),
        out_specs=P(("groups", "ctx"), "head"),
        check_vma=False,
    )
```

```python
import functools
import math

import jax
import jax.numpy as jnp
from jax import lax
from jax.experimental import pallas as pl
from jax.experimental.pallas import tpu as pltpu
from jax.sharding import PartitionSpec as P

LATENT = 512
ROPE = 64
NOPE = 128
VDIM = 128
PACKED = 768
ONES = 16
QK = 256
NEG = -1e30
VMEM_BYTES = 50 * 1024 * 1024
AXES = ("ctx", "head")
BF = jnp.bfloat16
F32 = jnp.float32


def vmem_spec():
    return pl.BlockSpec(memory_space=pltpu.VMEM)


def smem_spec():
    return pl.BlockSpec(memory_space=pltpu.SMEM)


def pack_kernel(span_ref, cache_ref, gain_ref, out_ref):
    tok_rows = span_ref.shape[1]
    cache_rows = cache_ref.shape[0]
    latent = span_ref[:LATENT, :].astype(F32)
    mean_square = jnp.mean(latent * latent, axis=0, keepdims=True)
    normed = ((latent * lax.rsqrt(mean_square + 1e-06)).T * gain_ref[...]).astype(BF)
    tiles = LATENT // 128
    for tile in range(tiles):
        out_ref[tile * tok_rows : (tile + 1) * tok_rows, :] = normed[:, tile * 128 : (tile + 1) * 128]
    at = tiles * tok_rows
    out_ref[at : at + ROPE, :] = span_ref[LATENT:, :]
    at += ROPE
    for tile in range(tiles):
        out_ref[at : at + cache_rows, :] = cache_ref[:, tile * 128 : (tile + 1) * 128]
        at += cache_rows
    out_ref[at:, :ROPE] = cache_ref[:, LATENT:]
    out_ref[at:, ROPE:] = cache_ref[:, LATENT:]


def pack(span_latents, cache_latents, gain):
    tok_rows = span_latents.shape[0]
    cache_rows = cache_latents.shape[0]
    rows = (LATENT // 128) * (tok_rows + cache_rows) + ROPE + cache_rows
    return pl.pallas_call(
        pack_kernel,
        out_shape=jax.ShapeDtypeStruct((rows, 128), BF),
        in_specs=[vmem_spec(), vmem_spec(), vmem_spec()],
        out_specs=vmem_spec(),
        name="pack_rows",
    )(span_latents.T, cache_latents, gain.reshape(1, LATENT))


def origin(route, place, side, core, line):
    kind, step = route
    if kind == "own":
        return place * 2 + side
    if kind == "across":
        return place * 2 + 1 - side
    came = lax.rem(place + line - step, line)
    lane_side = lax.rem(side + core, 2) if kind == "along" else lax.rem(side + 1 - core, 2)
    return came * 2 + lane_side


def prepare_kernel(heads, q_ref, wk_ref, latent_ref):
    scale = math.log2(math.e) / math.sqrt(NOPE + ROPE)
    rows = q_ref.shape[0]
    turned = q_ref[...].T
    ids = lax.broadcasted_iota(jnp.int32, (PACKED - LATENT - 2 * ROPE, rows), 0)
    flags = jnp.where(ids == 0, NEG, 0.0).astype(BF)
    for head in range(heads):
        at = head * (NOPE + ROPE)
        here = slice(head * rows, (head + 1) * rows)
        wk = wk_ref[:, head * NOPE : (head + 1) * NOPE]
        latent = jnp.dot(wk, turned[at : at + NOPE], preferred_element_type=F32)
        latent_ref[:LATENT, here] = (latent * scale).astype(BF)
        rotary = turned[at + NOPE : at + NOPE + ROPE].astype(F32) * scale
        rounded = rotary.astype(BF)
        latent_ref[LATENT : LATENT + ROPE, here] = rounded
        latent_ref[LATENT + ROPE : LATENT + 2 * ROPE, here] = (rotary - rounded.astype(F32)).astype(BF)
        latent_ref[LATENT + 2 * ROPE :, here] = flags


def prepare(queries, key_weight, heads):
    rows = queries.shape[0]
    depth, width = key_weight.shape
    steps = width // (heads * NOPE)
    return pl.pallas_call(
        functools.partial(prepare_kernel, heads),
        out_shape=jax.ShapeDtypeStruct((steps * PACKED, heads * rows), BF),
        grid=(steps,),
        in_specs=[
            pl.BlockSpec((rows, heads * (NOPE + ROPE)), lambda i: (0, i)),
            pl.BlockSpec((depth, heads * NOPE), lambda i: (0, i)),
        ],
        out_specs=pl.BlockSpec((PACKED, heads * rows), lambda i: (i, 0)),
        compiler_params=pltpu.CompilerParams(vmem_limit_bytes=58 * 1024 * 1024),
        cost_estimate=pl.CostEstimate(
            flops=2 * rows * depth * width, bytes_accessed=depth * width * 8, transcendentals=0
        ),
        name="prepare",
    )(queries, key_weight)


def gather_rows(cfg, order_ref, prefix_ref, blocks, rows_ref, turned_ref):
    routes, line, cache_rows, tok_rows = cfg
    tiles = LATENT // 128
    me = lax.axis_index("ctx")
    core = lax.axis_index("head")
    place = lax.div(me, 2)
    side = lax.rem(me, 2)
    lanes = lax.broadcasted_iota(jnp.int32, (tok_rows, 128), 1)
    slots = lax.broadcasted_iota(jnp.int32, (cache_rows, 128), 0)
    flag_lane = lax.broadcasted_iota(jnp.int32, (cache_rows, 128), 1) == 0
    base = tiles * tok_rows + ROPE

    def take(slot, route, block):
        to = slice(slot * tok_rows, (slot + 1) * tok_rows)
        for tile in range(tiles):
            part = block[tile * tok_rows : (tile + 1) * tok_rows, :]
            rows_ref[to, tile * 128 : (tile + 1) * 128] = part
        source = origin(route, place, side, core, line)
        hidden = jnp.where(order_ref[source] > order_ref[me], 1.0, 0.0)
        flags = jnp.where(lanes == 0, hidden, 0.0)
        rotary = block[tiles * tok_rows : base, :]
        rows_ref[to, LATENT : LATENT + 128] = jnp.concatenate([rotary, rotary], axis=0).T
        rows_ref[to, LATENT + 128 :] = flags.astype(BF)
        at = len(routes) * tok_rows + slot * cache_rows
        to = slice(at, at + cache_rows)
        for tile in range(tiles):
            begin = base + tile * cache_rows
            rows_ref[to, tile * 128 : (tile + 1) * 128] = block[begin : begin + cache_rows, :]
        unused = jnp.logical_and(flag_lane, slots + source * cache_rows >= prefix_ref[0])
        rows_ref[to, LATENT : LATENT + 128] = block[base + tiles * cache_rows :, :]
        rows_ref[to, LATENT + 128 :] = jnp.where(unused, 1.0, 0.0).astype(BF)

    for slot, route in enumerate(routes):
        if len(blocks[slot]) == 1:
            take(slot, route, blocks[slot][0])
        else:
            for which in range(2):
                pl.when(core == which)(functools.partial(take, slot, route, blocks[slot][which]))

    def turn(here):
        turned_ref[:LATENT, here] = rows_ref[here, :LATENT].T

    total = rows_ref.shape[0]
    turned_ref[LATENT:, :] = jnp.ones((ONES, total), BF)
    return [functools.partial(turn, slice(at, at + 128)) for at in range(0, total, 128)]


def weave(*lanes):
    longest = max(len(lane) for lane in lanes)
    done = [0] * len(lanes)
    for turn in range(1, longest + 1):
        for index, lane in enumerate(lanes):
            while done[index] < len(lane) and done[index] * longest < turn * len(lane):
                lane[done[index]]()
                done[index] += 1


def attend_kernel(cfg, heads, steps, counts, order_ref, prefix_ref, latent_ref, wv_ref, *rest):
    routes = cfg[0]
    tok_rows = cfg[3]
    blocks = []
    for count in counts:
        blocks.append(rest[:count])
        rest = rest[count:]
    out_ref, rows_ref, turned_ref = rest[:3]
    scratch = rest[3:]
    score_refs, weight_refs, peak_refs = (scratch[at : at + 2] for at in (0, 2, 4))
    wvt_refs = scratch[6:8]
    keys = rows_ref.shape[0]
    width = heads * tok_rows
    step = pl.program_id(0)
    pieces = [slice(at, min(at + 256, keys)) for at in range(0, keys, 256)]

    def by_eights(value):
        return value.reshape(-1, 8, width)

    def scores(buffer):
        def piece(index):
            here = pieces[index]
            query = latent_ref[buffer * PACKED : (buffer + 1) * PACKED, :]
            result = jnp.dot(rows_ref[here, :], query, preferred_element_type=F32)
            if index == 0:
                key_ids = lax.broadcasted_iota(jnp.int32, (tok_rows, width), 0)
                query_ids = lax.broadcasted_iota(jnp.int32, (tok_rows, width), 1) % tok_rows
                causal = jnp.where(key_ids <= query_ids, 0.0, NEG)
                result = jnp.concatenate([result[:tok_rows] + causal, result[tok_rows:]], axis=0)
            score_refs[buffer][here, :] = result
            peak = jnp.max(by_eights(result), axis=0)
            if index:
                peak = jnp.maximum(peak, peak_refs[buffer][...])
            peak_refs[buffer][...] = peak

        return [functools.partial(piece, index) for index in range(len(pieces))]

    def weights(buffer):
        def piece(index):
            here = pieces[index]
            peak = jnp.max(peak_refs[buffer][...], axis=0, keepdims=True)
            weight_refs[buffer][here, :] = jnp.exp2(score_refs[buffer][here, :] - peak).astype(BF)

        return [functools.partial(piece, index) for index in range(len(pieces))]

    def outputs(buffer):
        parts = []
        totals = []

        def mix(index):
            first = index * 256
            final = index == LATENT // 256 - 1
            here = slice(first, LATENT + ONES if final else first + 256)
            mixed = jnp.dot(turned_ref[here, :], weight_refs[buffer][...], preferred_element_type=F32)
            parts.append(mixed[:256].astype(BF))
            if final:
                totals.append(mixed[256:257])

        def turn(head):
            place = buffer * heads + head
            to = slice(head * VDIM, (head + 1) * VDIM)
            wvt_refs[buffer][to, :] = wv_ref[:, place * VDIM : (place + 1) * VDIM].T

        def finish():
            total = totals[0]
            mixed = jnp.concatenate(parts, axis=0)
            for head in range(heads):
                here = slice(head * tok_rows, (head + 1) * tok_rows)
                place = buffer * heads + head
                wvt = wvt_refs[buffer][head * VDIM : (head + 1) * VDIM, :]
                out = jnp.dot(wvt, mixed[:, here], preferred_element_type=F32) / total[:, here]
                out_ref[:, place * VDIM : (place + 1) * VDIM] = out.astype(BF).T

        turns = [functools.partial(turn, head) for head in range(heads)]
        mixes = [functools.partial(mix, index) for index in range(LATENT // 256)]
        return turns[: heads // 2] + mixes[:-1] + turns[heads // 2 :] + [mixes[-1], finish]

    @pl.when(step == 0)
    def _():
        turns = gather_rows(cfg, order_ref, prefix_ref, blocks, rows_ref, turned_ref)
        cut = len(turns) // 3
        weave(scores(0), turns[:cut])
        weave(scores(1), weights(0), turns[cut:])

    @pl.when(jnp.logical_and(step > 0, step < steps))
    def _():
        weave(scores(0), weights(1), outputs(0))
        weave(scores(1), weights(0), outputs(1))

    @pl.when(step == steps)
    def _():
        weave(weights(1), outputs(0))
        weave(outputs(1))


def attend(scalars, latent_queries, wv, blocks, line, cache_rows, heads):
    tok_rows = latent_queries.shape[1] // heads
    all_heads = wv.shape[1] // VDIM
    routes = tuple(route for route, _ in blocks)
    keys = len(routes) * (tok_rows + cache_rows)
    cfg = (routes, line, cache_rows, tok_rows)
    steps = all_heads // (2 * heads)
    width = heads * tok_rows
    return pl.pallas_call(
        functools.partial(attend_kernel, cfg, heads, steps, tuple(len(x) for _, x in blocks)),
        out_shape=jax.ShapeDtypeStruct((tok_rows, all_heads * VDIM), BF),
        grid=(steps + 1,),
        in_specs=[
            smem_spec(),
            smem_spec(),
            pl.BlockSpec((2 * PACKED, width), lambda i: (jnp.minimum(i, steps - 1), 0)),
            pl.BlockSpec((LATENT, 2 * heads * VDIM), lambda i: (0, jnp.maximum(i - 1, 0))),
        ]
        + [vmem_spec()] * sum(len(x) for _, x in blocks),
        out_specs=pl.BlockSpec((tok_rows, 2 * heads * VDIM), lambda i: (0, jnp.maximum(i - 1, 0))),
        scratch_shapes=[pltpu.VMEM((keys, PACKED), BF), pltpu.VMEM((LATENT + ONES, keys), BF)]
        + [pltpu.VMEM((keys, width), F32)] * 2
        + [pltpu.VMEM((keys, width), BF)] * 2
        + [pltpu.VMEM((8, width), F32)] * 2
        + [pltpu.VMEM((heads * VDIM, LATENT), BF)] * 2,
        compiler_params=pltpu.CompilerParams(vmem_limit_bytes=VMEM_BYTES),
        cost_estimate=pl.CostEstimate(
            flops=2 * keys * all_heads * tok_rows * (PACKED + LATENT),
            bytes_accessed=LATENT * all_heads * 512,
            transcendentals=keys * tok_rows * all_heads,
        ),
        name="attend",
    )(*scalars, latent_queries, wv, *[x for _, group in blocks for x in group])


def mover(line):
    def move(value, route):
        pairs = []
        for place in range(line):
            for side in range(2):
                for core in range(2):
                    to_place, to_side, to_core = route(place, side, core)
                    source = (place * 2 + side) * 2 + core
                    target = ((to_place % line) * 2 + to_side) * 2 + to_core
                    pairs.append((source, target))
        return lax.ppermute(value, AXES, pairs)

    return move


def per_device(
    queries,
    span_latents,
    cache_latents,
    latent_gain,
    key_weight,
    value_weight,
    prefix_length,
    block_order,
):
    line = lax.axis_size("ctx") // 2
    cache_rows = cache_latents.shape[0]
    move = mover(line)
    own = pack(span_latents, cache_latents, latent_gain)
    heads = 4 if line <= 8 else 2
    half = line // 2

    def swap(value):
        return move(value, lambda p, s, c: (p, s, 1 - c))

    across = move(own, lambda p, s, c: (p, 1 - s, c))
    along = [move(own, lambda p, s, c, k=k: (p + k, s ^ c, c)) for k in range(1, line) if k != half]
    far = move(own, lambda p, s, c: (p + half * (1 - c), s, c))
    latent_queries = prepare(queries, key_weight, heads)
    across, along, far, latent_queries = lax.optimization_barrier((across, along, far, latent_queries))
    crossed = move(far, lambda p, s, c: (p, s, 0) if c else (p, 1 - s, 1))
    swapped = [swap(a) for a in along]
    shared = swap(far)
    steps = [k for k in range(1, line) if k != half]
    blocks = [(("own", 0), (own,)), (("across", 0), (across,))]
    blocks += [(("along", k), (a,)) for k, a in zip(steps, along)]
    blocks += [(("swapped", k), (w,)) for k, w in zip(steps, swapped)]
    blocks += [(("along", half), (far, crossed)), (("swapped", half), (swap(crossed), shared))]
    return attend((block_order, prefix_length), latent_queries, value_weight, blocks, line, cache_rows, heads)


def solution(mesh):
    return jax.shard_map(
        per_device,
        mesh=mesh,
        in_specs=(
            P(("groups", "ctx"), "head"),
            P(("groups", "ctx"), None),
            P(("groups", "ctx"), None),
            P(),
            P(None, "head"),
            P(None, "head"),
            P("groups"),
            P("groups"),
        ),
        out_specs=P(("groups", "ctx"), "head"),
        check_vma=False,
    )
```

```python
import functools
import math

import jax
import jax.numpy as jnp
from jax import lax
from jax.experimental import pallas as pl
from jax.experimental.pallas import tpu as pltpu
from jax.sharding import PartitionSpec as P

LATENT = 512
ROPE = 64
NOPE = 128
VDIM = 128
PACKED = 768
ONES = 16
QK = 256
NEG = -1e30
VMEM_BYTES = 50 * 1024 * 1024
AXES = ("ctx", "head")
BF = jnp.bfloat16
F32 = jnp.float32


def vmem_spec():
    return pl.BlockSpec(memory_space=pltpu.VMEM)


def smem_spec():
    return pl.BlockSpec(memory_space=pltpu.SMEM)


def pack_kernel(span_ref, cache_ref, gain_ref, out_ref):
    tok_rows = span_ref.shape[1]
    cache_rows = cache_ref.shape[0]
    latent = span_ref[:LATENT, :].astype(F32)
    mean_square = jnp.mean(latent * latent, axis=0, keepdims=True)
    normed = ((latent * lax.rsqrt(mean_square + 1e-06)).T * gain_ref[...]).astype(BF)
    tiles = LATENT // 128
    for tile in range(tiles):
        out_ref[tile * tok_rows : (tile + 1) * tok_rows, :] = normed[:, tile * 128 : (tile + 1) * 128]
    at = tiles * tok_rows
    out_ref[at : at + ROPE, :] = span_ref[LATENT:, :]
    at += ROPE
    for tile in range(tiles):
        out_ref[at : at + cache_rows, :] = cache_ref[:, tile * 128 : (tile + 1) * 128]
        at += cache_rows
    out_ref[at:, :ROPE] = cache_ref[:, LATENT:]
    out_ref[at:, ROPE:] = cache_ref[:, LATENT:]


def pack(span_latents, cache_latents, gain):
    tok_rows = span_latents.shape[0]
    cache_rows = cache_latents.shape[0]
    rows = (LATENT // 128) * (tok_rows + cache_rows) + ROPE + cache_rows
    return pl.pallas_call(
        pack_kernel,
        out_shape=jax.ShapeDtypeStruct((rows, 128), BF),
        in_specs=[vmem_spec(), vmem_spec(), vmem_spec()],
        out_specs=vmem_spec(),
        name="pack_rows",
    )(span_latents.T, cache_latents, gain.reshape(1, LATENT))


def origin(route, place, side, core, line):
    kind, step = route
    if kind == "own":
        return place * 2 + side
    if kind == "across":
        return place * 2 + 1 - side
    came = lax.rem(place + line - step, line)
    lane_side = lax.rem(side + core, 2) if kind == "along" else lax.rem(side + 1 - core, 2)
    return came * 2 + lane_side


def prepare_kernel(heads, q_ref, wk_ref, wv_ref, latent_ref, wvt_ref):
    scale = math.log2(math.e) / math.sqrt(NOPE + ROPE)
    rows = q_ref.shape[0]
    turned = q_ref[...].T
    ids = lax.broadcasted_iota(jnp.int32, (PACKED - LATENT - 2 * ROPE, rows), 0)
    flags = jnp.where(ids == 0, NEG, 0.0).astype(BF)
    for head in range(heads):
        at = head * (NOPE + ROPE)
        here = slice(head * rows, (head + 1) * rows)
        wk = wk_ref[:, head * NOPE : (head + 1) * NOPE]
        latent = jnp.dot(wk, turned[at : at + NOPE], preferred_element_type=F32)
        latent_ref[:LATENT, here] = (latent * scale).astype(BF)
        rotary = turned[at + NOPE : at + NOPE + ROPE].astype(F32) * scale
        rounded = rotary.astype(BF)
        latent_ref[LATENT : LATENT + ROPE, here] = rounded
        latent_ref[LATENT + ROPE : LATENT + 2 * ROPE, here] = (rotary - rounded.astype(F32)).astype(BF)
        latent_ref[LATENT + 2 * ROPE :, here] = flags
    wvt_ref[...] = wv_ref[...].T


def prepare(queries, key_weight, value_weight, heads):
    rows = queries.shape[0]
    depth, width = key_weight.shape
    steps = width // (heads * NOPE)
    return pl.pallas_call(
        functools.partial(prepare_kernel, heads),
        out_shape=(
            jax.ShapeDtypeStruct((steps * PACKED, heads * rows), BF),
            jax.ShapeDtypeStruct((steps * heads * VDIM, depth), BF),
        ),
        grid=(steps,),
        in_specs=[
            pl.BlockSpec((rows, heads * (NOPE + ROPE)), lambda i: (0, i)),
            pl.BlockSpec((depth, heads * NOPE), lambda i: (0, i)),
            pl.BlockSpec((depth, heads * VDIM), lambda i: (0, i)),
        ],
        out_specs=(
            pl.BlockSpec((PACKED, heads * rows), lambda i: (i, 0)),
            pl.BlockSpec((heads * VDIM, depth), lambda i: (i, 0)),
        ),
        compiler_params=pltpu.CompilerParams(vmem_limit_bytes=58 * 1024 * 1024),
        cost_estimate=pl.CostEstimate(
            flops=2 * rows * depth * width, bytes_accessed=depth * width * 8, transcendentals=0
        ),
        name="prepare",
    )(queries, key_weight, value_weight)


def gather_rows(cfg, order_ref, prefix_ref, blocks, rows_ref, turned_ref):
    routes, line, cache_rows, tok_rows = cfg
    tiles = LATENT // 128
    me = lax.axis_index("ctx")
    core = lax.axis_index("head")
    place = lax.div(me, 2)
    side = lax.rem(me, 2)
    lanes = lax.broadcasted_iota(jnp.int32, (tok_rows, 128), 1)
    slots = lax.broadcasted_iota(jnp.int32, (cache_rows, 128), 0)
    flag_lane = lax.broadcasted_iota(jnp.int32, (cache_rows, 128), 1) == 0
    base = tiles * tok_rows + ROPE
    for slot, route in enumerate(routes):
        block = blocks[slot]
        to = slice(slot * tok_rows, (slot + 1) * tok_rows)
        for tile in range(tiles):
            part = block[tile * tok_rows : (tile + 1) * tok_rows, :]
            rows_ref[to, tile * 128 : (tile + 1) * 128] = part
        source = origin(route, place, side, core, line)
        hidden = jnp.where(order_ref[source] > order_ref[me], 1.0, 0.0)
        flags = jnp.where(lanes == 0, hidden, 0.0)
        rotary = block[tiles * tok_rows : base, :]
        rows_ref[to, LATENT : LATENT + 128] = jnp.concatenate([rotary, rotary], axis=0).T
        rows_ref[to, LATENT + 128 :] = flags.astype(BF)
        at = len(routes) * tok_rows + slot * cache_rows
        to = slice(at, at + cache_rows)
        for tile in range(tiles):
            begin = base + tile * cache_rows
            rows_ref[to, tile * 128 : (tile + 1) * 128] = block[begin : begin + cache_rows, :]
        unused = jnp.logical_and(flag_lane, slots + source * cache_rows >= prefix_ref[0])
        rows_ref[to, LATENT : LATENT + 128] = block[base + tiles * cache_rows :, :]
        rows_ref[to, LATENT + 128 :] = jnp.where(unused, 1.0, 0.0).astype(BF)

    def turn(here):
        turned_ref[:LATENT, here] = rows_ref[here, :LATENT].T

    total = rows_ref.shape[0]
    turned_ref[LATENT:, :] = jnp.ones((ONES, total), BF)
    return [functools.partial(turn, slice(at, at + 128)) for at in range(0, total, 128)]


def weave(*lanes):
    longest = max(len(lane) for lane in lanes)
    done = [0] * len(lanes)
    for turn in range(1, longest + 1):
        for index, lane in enumerate(lanes):
            while done[index] < len(lane) and done[index] * longest < turn * len(lane):
                lane[done[index]]()
                done[index] += 1


def attend_kernel(cfg, heads, steps, order_ref, prefix_ref, latent_ref, wvt_ref, *rest):
    routes = cfg[0]
    tok_rows = cfg[3]
    blocks = rest[: len(routes)]
    out_ref, rows_ref, turned_ref = rest[len(routes) : len(routes) + 3]
    scratch = rest[len(routes) + 3 :]
    score_refs, weight_refs, peak_refs = (scratch[at : at + 2] for at in (0, 2, 4))
    keys = rows_ref.shape[0]
    width = heads * tok_rows
    step = pl.program_id(0)
    pieces = [slice(at, min(at + 384, keys)) for at in range(0, keys, 384)]

    def by_eights(value):
        return value.reshape(-1, 8, width)

    def scores(buffer):
        def piece(index):
            here = pieces[index]
            query = latent_ref[buffer * PACKED : (buffer + 1) * PACKED, :]
            result = jnp.dot(rows_ref[here, :], query, preferred_element_type=F32)
            if index == 0:
                key_ids = lax.broadcasted_iota(jnp.int32, (tok_rows, width), 0)
                query_ids = lax.broadcasted_iota(jnp.int32, (tok_rows, width), 1) % tok_rows
                causal = jnp.where(key_ids <= query_ids, 0.0, NEG)
                result = jnp.concatenate([result[:tok_rows] + causal, result[tok_rows:]], axis=0)
            score_refs[buffer][here, :] = result
            peak = jnp.max(by_eights(result), axis=0)
            if index:
                peak = jnp.maximum(peak, peak_refs[buffer][...])
            peak_refs[buffer][...] = peak

        return [functools.partial(piece, index) for index in range(len(pieces))]

    def weights(buffer):
        def piece(index):
            here = pieces[index]
            peak = jnp.max(peak_refs[buffer][...], axis=0, keepdims=True)
            weight_refs[buffer][here, :] = jnp.exp2(score_refs[buffer][here, :] - peak).astype(BF)

        return [functools.partial(piece, index) for index in range(len(pieces))]

    def outputs(buffer):
        held = []

        def mix():
            mixed = jnp.dot(turned_ref[...], weight_refs[buffer][...], preferred_element_type=F32)
            held.append(mixed[:LATENT].astype(BF))
            held.append(mixed[LATENT : LATENT + 1])

        def finish():
            mixed, total = held
            for head in range(heads):
                here = slice(head * tok_rows, (head + 1) * tok_rows)
                place = buffer * heads + head
                wvt = wvt_ref[place * VDIM : (place + 1) * VDIM, :]
                out = jnp.dot(wvt, mixed[:, here], preferred_element_type=F32) / total[:, here]
                out_ref[:, place * VDIM : (place + 1) * VDIM] = out.astype(BF).T

        return [mix, finish]

    @pl.when(step == 0)
    def _():
        turns = gather_rows(cfg, order_ref, prefix_ref, blocks, rows_ref, turned_ref)
        cut = len(turns) // 3
        weave(scores(0), turns[:cut])
        weave(scores(1), weights(0), turns[cut:])

    @pl.when(jnp.logical_and(step > 0, step < steps))
    def _():
        weave(scores(0), weights(1), outputs(0))
        weave(scores(1), weights(0), outputs(1))

    @pl.when(step == steps)
    def _():
        weave(weights(1), outputs(0))
        weave(outputs(1))


def attend(scalars, latent_queries, wvt, blocks, line, cache_rows, heads):
    tok_rows = latent_queries.shape[1] // heads
    all_heads = wvt.shape[0] // VDIM
    routes = tuple(route for route, _ in blocks)
    keys = len(routes) * (tok_rows + cache_rows)
    cfg = (routes, line, cache_rows, tok_rows)
    steps = all_heads // (2 * heads)
    width = heads * tok_rows
    return pl.pallas_call(
        functools.partial(attend_kernel, cfg, heads, steps),
        out_shape=jax.ShapeDtypeStruct((tok_rows, all_heads * VDIM), BF),
        grid=(steps + 1,),
        in_specs=[
            smem_spec(),
            smem_spec(),
            pl.BlockSpec((2 * PACKED, width), lambda i: (jnp.minimum(i, steps - 1), 0)),
            pl.BlockSpec((2 * heads * VDIM, LATENT), lambda i: (jnp.maximum(i - 1, 0), 0)),
        ]
        + [vmem_spec()] * len(blocks),
        out_specs=pl.BlockSpec((tok_rows, 2 * heads * VDIM), lambda i: (0, jnp.maximum(i - 1, 0))),
        scratch_shapes=[pltpu.VMEM((keys, PACKED), BF), pltpu.VMEM((LATENT + ONES, keys), BF)]
        + [pltpu.VMEM((keys, width), F32)] * 2
        + [pltpu.VMEM((keys, width), BF)] * 2
        + [pltpu.VMEM((8, width), F32)] * 2,
        compiler_params=pltpu.CompilerParams(vmem_limit_bytes=VMEM_BYTES),
        cost_estimate=pl.CostEstimate(
            flops=2 * keys * all_heads * tok_rows * (PACKED + LATENT),
            bytes_accessed=LATENT * all_heads * 512,
            transcendentals=keys * tok_rows * all_heads,
        ),
        name="attend",
    )(*scalars, latent_queries, wvt, *[x for _, x in blocks])


def mover(line):
    def move(value, route):
        pairs = []
        for place in range(line):
            for side in range(2):
                for core in range(2):
                    to_place, to_side, to_core = route(place, side, core)
                    source = (place * 2 + side) * 2 + core
                    target = ((to_place % line) * 2 + to_side) * 2 + to_core
                    pairs.append((source, target))
        return lax.ppermute(value, AXES, pairs)

    return move


def per_device(
    queries,
    span_latents,
    cache_latents,
    latent_gain,
    key_weight,
    value_weight,
    prefix_length,
    block_order,
):
    line = lax.axis_size("ctx") // 2
    cache_rows = cache_latents.shape[0]
    move = mover(line)
    own = pack(span_latents, cache_latents, latent_gain)
    heads = 4 if line <= 8 else 2
    across = move(own, lambda p, s, c: (p, 1 - s, c))
    along = [move(own, lambda p, s, c, k=k: (p + k, s ^ c, c)) for k in range(1, line)]
    latent_queries, wvt = prepare(queries, key_weight, value_weight, heads)
    along, latent_queries, wvt = lax.optimization_barrier((along, latent_queries, wvt))
    swapped = [move(a, lambda p, s, c: (p, s, 1 - c)) for a in along]
    blocks = [(("own", 0), own), (("across", 0), across)]
    blocks += [(("along", k + 1), a) for k, a in enumerate(along)]
    blocks += [(("swapped", k + 1), w) for k, w in enumerate(swapped)]
    return attend((block_order, prefix_length), latent_queries, wvt, blocks, line, cache_rows, heads)


def solution(mesh):
    return jax.shard_map(
        per_device,
        mesh=mesh,
        in_specs=(
            P(("groups", "ctx"), "head"),
            P(("groups", "ctx"), None),
            P(("groups", "ctx"), None),
            P(),
            P(None, "head"),
            P(None, "head"),
            P("groups"),
            P("groups"),
        ),
        out_specs=P(("groups", "ctx"), "head"),
        check_vma=False,
    )
```

```python
import functools
import math

import jax
import jax.numpy as jnp
from jax import lax
from jax.experimental import pallas as pl
from jax.experimental.pallas import tpu as pltpu
from jax.sharding import PartitionSpec as P

LATENT = 512
ROPE = 64
NOPE = 128
VDIM = 128
PACKED = 768
ONES = 16
QK = 256
NEG = -1e30
VMEM_BYTES = 50 * 1024 * 1024
AXES = ("ctx", "head")
BF = jnp.bfloat16
F32 = jnp.float32


def vmem_spec():
    return pl.BlockSpec(memory_space=pltpu.VMEM)


def smem_spec():
    return pl.BlockSpec(memory_space=pltpu.SMEM)


def pack_kernel(span_ref, cache_ref, gain_ref, out_ref):
    tok_rows = span_ref.shape[1]
    cache_rows = cache_ref.shape[0]
    latent = span_ref[:LATENT, :].astype(F32)
    mean_square = jnp.mean(latent * latent, axis=0, keepdims=True)
    normed = ((latent * lax.rsqrt(mean_square + 1e-06)).T * gain_ref[...]).astype(BF)
    tiles = LATENT // 128
    for tile in range(tiles):
        out_ref[tile * tok_rows : (tile + 1) * tok_rows, :] = normed[:, tile * 128 : (tile + 1) * 128]
    at = tiles * tok_rows
    out_ref[at : at + ROPE, :] = span_ref[LATENT:, :]
    at += ROPE
    for tile in range(tiles):
        out_ref[at : at + cache_rows, :] = cache_ref[:, tile * 128 : (tile + 1) * 128]
        at += cache_rows
    out_ref[at:, :ROPE] = cache_ref[:, LATENT:]
    out_ref[at:, ROPE:] = cache_ref[:, LATENT:]


def pack(span_latents, cache_latents, gain):
    tok_rows = span_latents.shape[0]
    cache_rows = cache_latents.shape[0]
    rows = (LATENT // 128) * (tok_rows + cache_rows) + ROPE + cache_rows
    return pl.pallas_call(
        pack_kernel,
        out_shape=jax.ShapeDtypeStruct((rows, 128), BF),
        in_specs=[vmem_spec(), vmem_spec(), vmem_spec()],
        out_specs=vmem_spec(),
        name="pack_rows",
    )(span_latents.T, cache_latents, gain.reshape(1, LATENT))


def origin(route, place, side, core, line):
    kind, step = route
    if kind == "own":
        return place * 2 + side
    if kind == "across":
        return place * 2 + 1 - side
    came = lax.rem(place + line - step, line)
    lane_side = lax.rem(side + core, 2) if kind == "along" else lax.rem(side + 1 - core, 2)
    return came * 2 + lane_side


def prepare_kernel(heads, q_ref, wk_ref, latent_ref):
    scale = math.log2(math.e) / math.sqrt(NOPE + ROPE)
    rows = q_ref.shape[0]
    ids = lax.broadcasted_iota(jnp.int32, (PACKED - LATENT - 2 * ROPE, rows), 0)
    flags = jnp.where(ids == 0, NEG, 0.0).astype(BF)
    nothing = jnp.zeros((NOPE, rows), BF)
    for pair in range(q_ref.shape[1] // (2 * (NOPE + ROPE))):
        turned = q_ref[:, pair * 384 : pair * 384 + 384].T
        left = jnp.concatenate([turned[:NOPE], nothing], axis=0)
        right = jnp.concatenate([nothing, turned[192 : 192 + NOPE]], axis=0)
        both = jnp.concatenate([left, right], axis=1)
        wk = wk_ref[:, pair * 2 * NOPE : (pair + 1) * 2 * NOPE]
        latent = (jnp.dot(wk, both, preferred_element_type=F32) * scale).astype(BF)
        group, head = divmod(2 * pair, heads)
        at = group * PACKED
        latent_ref[at : at + LATENT, head * rows : (head + 2) * rows] = latent
        for side in range(2):
            here = slice((head + side) * rows, (head + side + 1) * rows)
            begin = side * 192 + NOPE
            rotary = turned[begin : begin + ROPE].astype(F32) * scale
            rounded = rotary.astype(BF)
            latent_ref[at + LATENT : at + LATENT + ROPE, here] = rounded
            rest = (rotary - rounded.astype(F32)).astype(BF)
            latent_ref[at + LATENT + ROPE : at + LATENT + 2 * ROPE, here] = rest
            latent_ref[at + LATENT + 2 * ROPE : at + PACKED, here] = flags


def prepare(queries, key_weight, heads):
    rows = queries.shape[0]
    depth, width = key_weight.shape
    steps = width // (heads * NOPE)
    return pl.pallas_call(
        functools.partial(prepare_kernel, heads),
        out_shape=jax.ShapeDtypeStruct((steps * PACKED, heads * rows), BF),
        grid=(steps // 2,),
        in_specs=[
            pl.BlockSpec((rows, 2 * heads * (NOPE + ROPE)), lambda i: (0, i)),
            pl.BlockSpec((depth, 2 * heads * NOPE), lambda i: (0, i)),
        ],
        out_specs=pl.BlockSpec((2 * PACKED, heads * rows), lambda i: (i, 0)),
        compiler_params=pltpu.CompilerParams(vmem_limit_bytes=58 * 1024 * 1024),
        cost_estimate=pl.CostEstimate(
            flops=2 * rows * depth * width, bytes_accessed=depth * width * 8, transcendentals=0
        ),
        name="prepare",
    )(queries, key_weight)


def gather_rows(cfg, order_ref, prefix_ref, blocks, rows_ref, turned_ref):
    routes, line, cache_rows, tok_rows = cfg
    tiles = LATENT // 128
    me = lax.axis_index("ctx")
    core = lax.axis_index("head")
    place = lax.div(me, 2)
    side = lax.rem(me, 2)
    lanes = lax.broadcasted_iota(jnp.int32, (tok_rows, 128), 1)
    slots = lax.broadcasted_iota(jnp.int32, (cache_rows, 128), 0)
    flag_lane = lax.broadcasted_iota(jnp.int32, (cache_rows, 128), 1) == 0
    base = tiles * tok_rows + ROPE

    def take(slot, route, block):
        to = slice(slot * tok_rows, (slot + 1) * tok_rows)
        for tile in range(tiles):
            part = block[tile * tok_rows : (tile + 1) * tok_rows, :]
            rows_ref[to, tile * 128 : (tile + 1) * 128] = part
        source = origin(route, place, side, core, line)
        hidden = jnp.where(order_ref[source] > order_ref[me], 1.0, 0.0)
        flags = jnp.where(lanes == 0, hidden, 0.0)
        rotary = block[tiles * tok_rows : base, :]
        rows_ref[to, LATENT : LATENT + 128] = jnp.concatenate([rotary, rotary], axis=0).T
        rows_ref[to, LATENT + 128 :] = flags.astype(BF)
        at = len(routes) * tok_rows + slot * cache_rows
        to = slice(at, at + cache_rows)
        for tile in range(tiles):
            begin = base + tile * cache_rows
            rows_ref[to, tile * 128 : (tile + 1) * 128] = block[begin : begin + cache_rows, :]
        unused = jnp.logical_and(flag_lane, slots + source * cache_rows >= prefix_ref[0])
        rows_ref[to, LATENT : LATENT + 128] = block[base + tiles * cache_rows :, :]
        rows_ref[to, LATENT + 128 :] = jnp.where(unused, 1.0, 0.0).astype(BF)

    for slot, route in enumerate(routes):
        if len(blocks[slot]) == 1:
            take(slot, route, blocks[slot][0])
        else:
            for which in range(2):
                pl.when(core == which)(functools.partial(take, slot, route, blocks[slot][which]))

    def turn(here):
        turned_ref[:LATENT, here] = rows_ref[here, :LATENT].T

    total = rows_ref.shape[0]
    turned_ref[LATENT:, :] = jnp.ones((ONES, total), BF)
    return [functools.partial(turn, slice(at, at + 128)) for at in range(0, total, 128)]


def weave(*lanes):
    longest = max(len(lane) for lane in lanes)
    done = [0] * len(lanes)
    for turn in range(1, longest + 1):
        for index, lane in enumerate(lanes):
            while done[index] < len(lane) and done[index] * longest < turn * len(lane):
                lane[done[index]]()
                done[index] += 1


def attend_kernel(cfg, heads, steps, counts, order_ref, prefix_ref, latent_ref, wv_ref, *rest):
    routes = cfg[0]
    tok_rows = cfg[3]
    blocks = []
    for count in counts:
        blocks.append(rest[:count])
        rest = rest[count:]
    out_ref, rows_ref, turned_ref = rest[:3]
    scratch = rest[3:]
    score_refs, weight_refs, peak_refs = (scratch[at : at + 2] for at in (0, 2, 4))
    wvt_refs = scratch[6:8]
    keys = rows_ref.shape[0]
    width = heads * tok_rows
    step = pl.program_id(0)
    pieces = [slice(at, min(at + 384, keys)) for at in range(0, keys, 384)]

    def by_eights(value):
        return value.reshape(-1, 8, width)

    def scores(buffer):
        def piece(index):
            here = pieces[index]
            query = latent_ref[buffer * PACKED : (buffer + 1) * PACKED, :]
            result = jnp.dot(rows_ref[here, :], query, preferred_element_type=F32)
            if index == 0:
                key_ids = lax.broadcasted_iota(jnp.int32, (tok_rows, width), 0)
                query_ids = lax.broadcasted_iota(jnp.int32, (tok_rows, width), 1) % tok_rows
                causal = jnp.where(key_ids <= query_ids, 0.0, NEG)
                result = jnp.concatenate([result[:tok_rows] + causal, result[tok_rows:]], axis=0)
            score_refs[buffer][here, :] = result
            peak = jnp.max(by_eights(result), axis=0)
            if index:
                peak = jnp.maximum(peak, peak_refs[buffer][...])
            peak_refs[buffer][...] = peak

        return [functools.partial(piece, index) for index in range(len(pieces))]

    def weights(buffer):
        def piece(index):
            here = pieces[index]
            peak = jnp.max(peak_refs[buffer][...], axis=0, keepdims=True)
            weight_refs[buffer][here, :] = jnp.exp2(score_refs[buffer][here, :] - peak).astype(BF)

        return [functools.partial(piece, index) for index in range(len(pieces))]

    def outputs(buffer):
        held = []

        def mix():
            mixed = jnp.dot(turned_ref[...], weight_refs[buffer][...], preferred_element_type=F32)
            held.append(mixed[:LATENT].astype(BF))
            held.append(mixed[LATENT : LATENT + 1])

        def turn(part):
            for head in range(part * heads // 2, (part + 1) * heads // 2):
                place = buffer * heads + head
                to = slice(head * VDIM, (head + 1) * VDIM)
                wvt_refs[buffer][to, :] = wv_ref[:, place * VDIM : (place + 1) * VDIM].T

        def finish():
            mixed, total = held
            for head in range(heads):
                here = slice(head * tok_rows, (head + 1) * tok_rows)
                place = buffer * heads + head
                wvt = wvt_refs[buffer][head * VDIM : (head + 1) * VDIM, :]
                out = jnp.dot(wvt, mixed[:, here], preferred_element_type=F32) / total[:, here]
                out_ref[:, place * VDIM : (place + 1) * VDIM] = out.astype(BF).T

        return [functools.partial(turn, 0), mix, functools.partial(turn, 1), finish]

    @pl.when(step == 0)
    def _():
        turns = gather_rows(cfg, order_ref, prefix_ref, blocks, rows_ref, turned_ref)
        cut = len(turns) // 3
        weave(scores(0), turns[:cut])
        weave(scores(1), weights(0), turns[cut:])

    @pl.when(jnp.logical_and(step > 0, step < steps))
    def _():
        weave(scores(0), weights(1), outputs(0))
        weave(scores(1), weights(0), outputs(1))

    @pl.when(step == steps)
    def _():
        weave(weights(1), outputs(0))
        weave(outputs(1))


def attend(scalars, latent_queries, wv, blocks, line, cache_rows, heads):
    tok_rows = latent_queries.shape[1] // heads
    all_heads = wv.shape[1] // VDIM
    routes = tuple(route for route, _ in blocks)
    keys = len(routes) * (tok_rows + cache_rows)
    cfg = (routes, line, cache_rows, tok_rows)
    steps = all_heads // (2 * heads)
    width = heads * tok_rows
    return pl.pallas_call(
        functools.partial(attend_kernel, cfg, heads, steps, tuple(len(x) for _, x in blocks)),
        out_shape=jax.ShapeDtypeStruct((tok_rows, all_heads * VDIM), BF),
        grid=(steps + 1,),
        in_specs=[
            smem_spec(),
            smem_spec(),
            pl.BlockSpec((2 * PACKED, width), lambda i: (jnp.minimum(i, steps - 1), 0)),
            pl.BlockSpec((LATENT, 2 * heads * VDIM), lambda i: (0, jnp.maximum(i - 1, 0))),
        ]
        + [vmem_spec()] * sum(len(x) for _, x in blocks),
        out_specs=pl.BlockSpec((tok_rows, 2 * heads * VDIM), lambda i: (0, jnp.maximum(i - 1, 0))),
        scratch_shapes=[pltpu.VMEM((keys, PACKED), BF), pltpu.VMEM((LATENT + ONES, keys), BF)]
        + [pltpu.VMEM((keys, width), F32)] * 2
        + [pltpu.VMEM((keys, width), BF)] * 2
        + [pltpu.VMEM((8, width), F32)] * 2
        + [pltpu.VMEM((heads * VDIM, LATENT), BF)] * 2,
        compiler_params=pltpu.CompilerParams(vmem_limit_bytes=VMEM_BYTES),
        cost_estimate=pl.CostEstimate(
            flops=2 * keys * all_heads * tok_rows * (PACKED + LATENT),
            bytes_accessed=LATENT * all_heads * 512,
            transcendentals=keys * tok_rows * all_heads,
        ),
        name="attend",
    )(*scalars, latent_queries, wv, *[x for _, group in blocks for x in group])


def mover(line):
    def move(value, route):
        pairs = []
        for place in range(line):
            for side in range(2):
                for core in range(2):
                    to_place, to_side, to_core = route(place, side, core)
                    source = (place * 2 + side) * 2 + core
                    target = ((to_place % line) * 2 + to_side) * 2 + to_core
                    pairs.append((source, target))
        return lax.ppermute(value, AXES, pairs)

    return move


def per_device(
    queries,
    span_latents,
    cache_latents,
    latent_gain,
    key_weight,
    value_weight,
    prefix_length,
    block_order,
):
    line = lax.axis_size("ctx") // 2
    cache_rows = cache_latents.shape[0]
    move = mover(line)
    own = pack(span_latents, cache_latents, latent_gain)
    heads = 4 if line <= 8 else 2
    half = line // 2

    def swap(value):
        return move(value, lambda p, s, c: (p, s, 1 - c))

    across = move(own, lambda p, s, c: (p, 1 - s, c))
    along = [move(own, lambda p, s, c, k=k: (p + k, s ^ c, c)) for k in range(1, line) if k != half]
    far = move(own, lambda p, s, c: (p + half * (1 - c), s, c))
    latent_queries = prepare(queries, key_weight, heads)
    across, along, far, latent_queries = lax.optimization_barrier((across, along, far, latent_queries))
    crossed = move(far, lambda p, s, c: (p, s, 0) if c else (p, 1 - s, 1))
    swapped = [swap(a) for a in along]
    shared = swap(far)
    steps = [k for k in range(1, line) if k != half]
    blocks = [(("own", 0), (own,)), (("across", 0), (across,))]
    blocks += [(("along", k), (a,)) for k, a in zip(steps, along)]
    blocks += [(("swapped", k), (w,)) for k, w in zip(steps, swapped)]
    blocks += [(("along", half), (far, crossed)), (("swapped", half), (swap(crossed), shared))]
    return attend((block_order, prefix_length), latent_queries, value_weight, blocks, line, cache_rows, heads)


def solution(mesh):
    return jax.shard_map(
        per_device,
        mesh=mesh,
        in_specs=(
            P(("groups", "ctx"), "head"),
            P(("groups", "ctx"), None),
            P(("groups", "ctx"), None),
            P(),
            P(None, "head"),
            P(None, "head"),
            P("groups"),
            P("groups"),
        ),
        out_specs=P(("groups", "ctx"), "head"),
        check_vma=False,
    )
```

```python
import functools
import math

import jax
import jax.numpy as jnp
from jax import lax
from jax.experimental import pallas as pl
from jax.experimental.pallas import tpu as pltpu
from jax.sharding import PartitionSpec as P

LATENT = 512
ROPE = 64
NOPE = 128
VDIM = 128
PACKED = 768
ONES = 16
QK = 256
NEG = -1e30
VMEM_BYTES = 50 * 1024 * 1024
AXES = ("ctx", "head")
BF = jnp.bfloat16
F32 = jnp.float32


def vmem_spec():
    return pl.BlockSpec(memory_space=pltpu.VMEM)


def smem_spec():
    return pl.BlockSpec(memory_space=pltpu.SMEM)


def pack_kernel(span_ref, cache_ref, gain_ref, out_ref):
    tok_rows = span_ref.shape[1]
    cache_rows = cache_ref.shape[0]
    latent = span_ref[:LATENT, :].astype(F32)
    mean_square = jnp.mean(latent * latent, axis=0, keepdims=True)
    normed = ((latent * lax.rsqrt(mean_square + 1e-06)).T * gain_ref[...]).astype(BF)
    tiles = LATENT // 128
    for tile in range(tiles):
        out_ref[tile * tok_rows : (tile + 1) * tok_rows, :] = normed[:, tile * 128 : (tile + 1) * 128]
    at = tiles * tok_rows
    out_ref[at : at + ROPE, :] = span_ref[LATENT:, :]
    at += ROPE
    for tile in range(tiles):
        out_ref[at : at + cache_rows, :] = cache_ref[:, tile * 128 : (tile + 1) * 128]
        at += cache_rows
    out_ref[at:, :ROPE] = cache_ref[:, LATENT:]
    out_ref[at:, ROPE:] = cache_ref[:, LATENT:]


def pack(span_latents, cache_latents, gain):
    tok_rows = span_latents.shape[0]
    cache_rows = cache_latents.shape[0]
    rows = (LATENT // 128) * (tok_rows + cache_rows) + ROPE + cache_rows
    return pl.pallas_call(
        pack_kernel,
        out_shape=jax.ShapeDtypeStruct((rows, 128), BF),
        in_specs=[vmem_spec(), vmem_spec(), vmem_spec()],
        out_specs=vmem_spec(),
        name="pack_rows",
    )(span_latents.T, cache_latents, gain.reshape(1, LATENT))


def origin(route, place, side, core, line):
    kind, step = route
    if kind == "own":
        return place * 2 + side
    if kind == "across":
        return place * 2 + 1 - side
    came = lax.rem(place + line - step, line)
    lane_side = lax.rem(side + core, 2) if kind == "along" else lax.rem(side + 1 - core, 2)
    return came * 2 + lane_side


def prepare_kernel(heads, q_ref, wk_ref, wv_ref, latent_ref, wvt_ref):
    scale = math.log2(math.e) / math.sqrt(NOPE + ROPE)
    rows = q_ref.shape[0]
    ids = lax.broadcasted_iota(jnp.int32, (PACKED - LATENT - 2 * ROPE, rows), 0)
    flags = jnp.where(ids == 0, NEG, 0.0).astype(BF)
    nothing = jnp.zeros((NOPE, rows), BF)
    for pair in range(q_ref.shape[1] // (2 * (NOPE + ROPE))):
        turned = q_ref[:, pair * 384 : pair * 384 + 384].T
        left = jnp.concatenate([turned[:NOPE], nothing], axis=0)
        right = jnp.concatenate([nothing, turned[192 : 192 + NOPE]], axis=0)
        both = jnp.concatenate([left, right], axis=1)
        wk = wk_ref[:, pair * 2 * NOPE : (pair + 1) * 2 * NOPE]
        latent = (jnp.dot(wk, both, preferred_element_type=F32) * scale).astype(BF)
        group, head = divmod(2 * pair, heads)
        at = group * PACKED
        latent_ref[at : at + LATENT, head * rows : (head + 2) * rows] = latent
        for side in range(2):
            here = slice((head + side) * rows, (head + side + 1) * rows)
            begin = side * 192 + NOPE
            rotary = turned[begin : begin + ROPE].astype(F32) * scale
            rounded = rotary.astype(BF)
            latent_ref[at + LATENT : at + LATENT + ROPE, here] = rounded
            rest = (rotary - rounded.astype(F32)).astype(BF)
            latent_ref[at + LATENT + ROPE : at + LATENT + 2 * ROPE, here] = rest
            latent_ref[at + LATENT + 2 * ROPE : at + PACKED, here] = flags
        own = slice(pair * 2 * VDIM, (pair + 1) * 2 * VDIM)
        wvt_ref[own, :] = wv_ref[:, own].T


def prepare(queries, key_weight, value_weight, heads):
    rows = queries.shape[0]
    depth, width = key_weight.shape
    steps = width // (heads * NOPE)
    return pl.pallas_call(
        functools.partial(prepare_kernel, heads),
        out_shape=(
            jax.ShapeDtypeStruct((steps * PACKED, heads * rows), BF),
            jax.ShapeDtypeStruct((steps * heads * VDIM, depth), BF),
        ),
        grid=(steps // 2,),
        in_specs=[
            pl.BlockSpec((rows, 2 * heads * (NOPE + ROPE)), lambda i: (0, i)),
            pl.BlockSpec((depth, 2 * heads * NOPE), lambda i: (0, i)),
            pl.BlockSpec((depth, 2 * heads * VDIM), lambda i: (0, i)),
        ],
        out_specs=(
            pl.BlockSpec((2 * PACKED, heads * rows), lambda i: (i, 0)),
            pl.BlockSpec((2 * heads * VDIM, depth), lambda i: (i, 0)),
        ),
        compiler_params=pltpu.CompilerParams(vmem_limit_bytes=58 * 1024 * 1024),
        cost_estimate=pl.CostEstimate(
            flops=2 * rows * depth * width, bytes_accessed=depth * width * 8, transcendentals=0
        ),
        name="prepare",
    )(queries, key_weight, value_weight)


def gather_rows(cfg, order_ref, prefix_ref, blocks, rows_ref, turned_ref):
    routes, line, cache_rows, tok_rows = cfg
    tiles = LATENT // 128
    me = lax.axis_index("ctx")
    core = lax.axis_index("head")
    place = lax.div(me, 2)
    side = lax.rem(me, 2)
    lanes = lax.broadcasted_iota(jnp.int32, (tok_rows, 128), 1)
    slots = lax.broadcasted_iota(jnp.int32, (cache_rows, 128), 0)
    flag_lane = lax.broadcasted_iota(jnp.int32, (cache_rows, 128), 1) == 0
    base = tiles * tok_rows + ROPE
    for slot, route in enumerate(routes):
        block = blocks[slot]
        to = slice(slot * tok_rows, (slot + 1) * tok_rows)
        for tile in range(tiles):
            part = block[tile * tok_rows : (tile + 1) * tok_rows, :]
            rows_ref[to, tile * 128 : (tile + 1) * 128] = part
        source = origin(route, place, side, core, line)
        hidden = jnp.where(order_ref[source] > order_ref[me], 1.0, 0.0)
        flags = jnp.where(lanes == 0, hidden, 0.0)
        rotary = block[tiles * tok_rows : base, :]
        rows_ref[to, LATENT : LATENT + 128] = jnp.concatenate([rotary, rotary], axis=0).T
        rows_ref[to, LATENT + 128 :] = flags.astype(BF)
        at = len(routes) * tok_rows + slot * cache_rows
        to = slice(at, at + cache_rows)
        for tile in range(tiles):
            begin = base + tile * cache_rows
            rows_ref[to, tile * 128 : (tile + 1) * 128] = block[begin : begin + cache_rows, :]
        unused = jnp.logical_and(flag_lane, slots + source * cache_rows >= prefix_ref[0])
        rows_ref[to, LATENT : LATENT + 128] = block[base + tiles * cache_rows :, :]
        rows_ref[to, LATENT + 128 :] = jnp.where(unused, 1.0, 0.0).astype(BF)

    def turn(here):
        turned_ref[:LATENT, here] = rows_ref[here, :LATENT].T

    total = rows_ref.shape[0]
    turned_ref[LATENT:, :] = jnp.ones((ONES, total), BF)
    return [functools.partial(turn, slice(at, at + 128)) for at in range(0, total, 128)]


def weave(*lanes):
    longest = max(len(lane) for lane in lanes)
    done = [0] * len(lanes)
    for turn in range(1, longest + 1):
        for index, lane in enumerate(lanes):
            while done[index] < len(lane) and done[index] * longest < turn * len(lane):
                lane[done[index]]()
                done[index] += 1


def attend_kernel(cfg, heads, steps, order_ref, prefix_ref, latent_ref, wvt_ref, *rest):
    routes = cfg[0]
    tok_rows = cfg[3]
    blocks = rest[: len(routes)]
    out_ref, rows_ref, turned_ref = rest[len(routes) : len(routes) + 3]
    scratch = rest[len(routes) + 3 :]
    score_refs, weight_refs, peak_refs = (scratch[at : at + 2] for at in (0, 2, 4))
    keys = rows_ref.shape[0]
    width = heads * tok_rows
    step = pl.program_id(0)
    pieces = [slice(at, min(at + 576, keys)) for at in range(0, keys, 576)]

    def by_eights(value):
        return value.reshape(-1, 8, width)

    def scores(buffer):
        def piece(index):
            here = pieces[index]
            query = latent_ref[buffer * PACKED : (buffer + 1) * PACKED, :]
            result = jnp.dot(rows_ref[here, :], query, preferred_element_type=F32)
            if index == 0:
                key_ids = lax.broadcasted_iota(jnp.int32, (tok_rows, width), 0)
                query_ids = lax.broadcasted_iota(jnp.int32, (tok_rows, width), 1) % tok_rows
                causal = jnp.where(key_ids <= query_ids, 0.0, NEG)
                result = jnp.concatenate([result[:tok_rows] + causal, result[tok_rows:]], axis=0)
            score_refs[buffer][here, :] = result
            peak = jnp.max(by_eights(result), axis=0)
            if index:
                peak = jnp.maximum(peak, peak_refs[buffer][...])
            peak_refs[buffer][...] = peak

        return [functools.partial(piece, index) for index in range(len(pieces))]

    def weights(buffer):
        def piece(index):
            here = pieces[index]
            peak = jnp.max(peak_refs[buffer][...], axis=0, keepdims=True)
            weight_refs[buffer][here, :] = jnp.exp2(score_refs[buffer][here, :] - peak).astype(BF)

        return [functools.partial(piece, index) for index in range(len(pieces))]

    def outputs(buffer):
        held = []

        def mix():
            mixed = jnp.dot(turned_ref[...], weight_refs[buffer][...], preferred_element_type=F32)
            held.append(mixed[:LATENT].astype(BF))
            held.append(mixed[LATENT : LATENT + 1])

        def finish():
            mixed, total = held
            for head in range(heads):
                here = slice(head * tok_rows, (head + 1) * tok_rows)
                place = buffer * heads + head
                wvt = wvt_ref[place * VDIM : (place + 1) * VDIM, :]
                out = jnp.dot(wvt, mixed[:, here], preferred_element_type=F32) / total[:, here]
                out_ref[:, place * VDIM : (place + 1) * VDIM] = out.astype(BF).T

        return [mix, finish]

    @pl.when(step == 0)
    def _():
        turns = gather_rows(cfg, order_ref, prefix_ref, blocks, rows_ref, turned_ref)
        cut = len(turns) // 3
        weave(scores(0), turns[:cut])
        weave(scores(1), weights(0), turns[cut:])

    @pl.when(jnp.logical_and(step > 0, step < steps))
    def _():
        weave(scores(0), weights(1), outputs(0))
        weave(scores(1), weights(0), outputs(1))

    @pl.when(step == steps)
    def _():
        weave(weights(1), outputs(0))
        weave(outputs(1))


def attend(scalars, latent_queries, wvt, blocks, line, cache_rows, heads):
    tok_rows = latent_queries.shape[1] // heads
    all_heads = wvt.shape[0] // VDIM
    routes = tuple(route for route, _ in blocks)
    keys = len(routes) * (tok_rows + cache_rows)
    cfg = (routes, line, cache_rows, tok_rows)
    steps = all_heads // (2 * heads)
    width = heads * tok_rows
    return pl.pallas_call(
        functools.partial(attend_kernel, cfg, heads, steps),
        out_shape=jax.ShapeDtypeStruct((tok_rows, all_heads * VDIM), BF),
        grid=(steps + 1,),
        in_specs=[
            smem_spec(),
            smem_spec(),
            pl.BlockSpec((2 * PACKED, width), lambda i: (jnp.minimum(i, steps - 1), 0)),
            pl.BlockSpec((2 * heads * VDIM, LATENT), lambda i: (jnp.maximum(i - 1, 0), 0)),
        ]
        + [vmem_spec()] * len(blocks),
        out_specs=pl.BlockSpec((tok_rows, 2 * heads * VDIM), lambda i: (0, jnp.maximum(i - 1, 0))),
        scratch_shapes=[pltpu.VMEM((keys, PACKED), BF), pltpu.VMEM((LATENT + ONES, keys), BF)]
        + [pltpu.VMEM((keys, width), F32)] * 2
        + [pltpu.VMEM((keys, width), BF)] * 2
        + [pltpu.VMEM((8, width), F32)] * 2,
        compiler_params=pltpu.CompilerParams(vmem_limit_bytes=VMEM_BYTES),
        cost_estimate=pl.CostEstimate(
            flops=2 * keys * all_heads * tok_rows * (PACKED + LATENT),
            bytes_accessed=LATENT * all_heads * 512,
            transcendentals=keys * tok_rows * all_heads,
        ),
        name="attend",
    )(*scalars, latent_queries, wvt, *[x for _, x in blocks])


def mover(line):
    def move(value, route):
        pairs = []
        for place in range(line):
            for side in range(2):
                for core in range(2):
                    to_place, to_side, to_core = route(place, side, core)
                    source = (place * 2 + side) * 2 + core
                    target = ((to_place % line) * 2 + to_side) * 2 + to_core
                    pairs.append((source, target))
        return lax.ppermute(value, AXES, pairs)

    return move


def per_device(
    queries,
    span_latents,
    cache_latents,
    latent_gain,
    key_weight,
    value_weight,
    prefix_length,
    block_order,
):
    line = lax.axis_size("ctx") // 2
    cache_rows = cache_latents.shape[0]
    move = mover(line)
    own = pack(span_latents, cache_latents, latent_gain)
    heads = 4 if line <= 8 else 2
    across = move(own, lambda p, s, c: (p, 1 - s, c))
    along = [move(own, lambda p, s, c, k=k: (p + k, s ^ c, c)) for k in range(1, line)]
    latent_queries, wvt = prepare(queries, key_weight, value_weight, heads)
    along, latent_queries, wvt = lax.optimization_barrier((along, latent_queries, wvt))
    swapped = [move(a, lambda p, s, c: (p, s, 1 - c)) for a in along]
    blocks = [(("own", 0), own), (("across", 0), across)]
    blocks += [(("along", k + 1), a) for k, a in enumerate(along)]
    blocks += [(("swapped", k + 1), w) for k, w in enumerate(swapped)]
    return attend((block_order, prefix_length), latent_queries, wvt, blocks, line, cache_rows, heads)


def solution(mesh):
    return jax.shard_map(
        per_device,
        mesh=mesh,
        in_specs=(
            P(("groups", "ctx"), "head"),
            P(("groups", "ctx"), None),
            P(("groups", "ctx"), None),
            P(),
            P(None, "head"),
            P(None, "head"),
            P("groups"),
            P("groups"),
        ),
        out_specs=P(("groups", "ctx"), "head"),
        check_vma=False,
    )
```
